32 devices in a mesh: blk: 4 (over z), slab: 2 (over x), micro: 4 (over y, core).
Axes of the slice: x: 2, y: 2, z: 4, core: 2. Of those that a mesh axis runs over, the one named last changes fastest.
Arguments:
- displacement: float32 [32, 128, 256], P('blk', 'micro', 'slab'), may hold values from -6 to 6
- load_field: float32 [32, 128, 256], P('blk', 'micro', 'slab'), may hold values from -6 to 6
- foundation: float32 [32, 128, 256], P('blk', 'micro', 'slab'), may hold values from 0.2 to 2
- plastic_flags: int32 [32, 128, 256], P('blk', 'micro', 'slab'), may hold values 0 or 1
- point_slot: int32 [32, 128, 256], P('blk', 'micro', 'slab'), may hold values from 0 to 65535, as said below
- family_in: float32 [4, 3, 256], replicated, may hold values from -5 to 5
- family_mid: bfloat16 [4, 256, 256], replicated, may hold values from -0.375 to 0.375
- family_out: bfloat16 [4, 3, 256], replicated, may hold values from -0.375 to 0.375
- family_tan: float32 [4, 256], replicated, may hold values from 0.002 to 0.02
Outputs:
- updated_field: float32 [32, 128, 256], P('blk', 'micro', 'slab')
- solver_residual: float32 [32, 128, 256], P('blk', 'micro', 'slab')
The draws below stay inside these ranges and needn't reach their ends.
Inputs may be any that keep to these rules, and one draw needn't show every extreme that they name: `point_slot`: within each device's block of 8 x 32 x 128 nodes the values are distinct; value // 16384 is the point's fibre family and value % 16384 its position among that family's points of the block in node order (last dimension fastest); in every block one family holds exactly 16384 points.
All inputs are finite; a program needn't handle non-finite values. No bound on the sum of `plastic_flags` on one device may be relied on, other than what follows from the above.
Results may differ from the reference program's by a relative error of at most 0.0024.
Values sent between devices are 32-bit elements; how exact they have to be, the bound alone decides.
No kernel may reach another device: no remote copies, remote signals or barrier semaphores. Data moves between devices by JAX's collectives and lax.ppermute only.
A program may use at most 128 MiB of HBM per device.

```python
import math
import jax
import jax.numpy as jnp
from jax import lax

CX = 8
CY = 32
CZ = 128
MODES = 256
ITERS = 8
FAMILIES = 4
CAP = 16384
NX = 32
NY = 128
NZ = 256


def draw_point_slot(key, part):
    blocks_x = NX // CX
    blocks_y = NY // CY
    blocks_z = NZ // CZ
    block_count = blocks_x * blocks_y * blocks_z
    points_dev = CX * CY * CZ
    all_keys = jax.random.split(jax.random.fold_in(key, 17), block_count)

    def draw_block(block_key):
        key_heavy, key_order, key_other = jax.random.split(block_key, 3)
        heaviest = jax.random.randint(key_heavy, (), 0, FAMILIES)
        ordering = jax.random.permutation(key_order, points_dev)
        ranking = jnp.argsort(ordering, stable=True)
        others = (heaviest + 1 + jax.random.randint(key_other, (points_dev,), 0, FAMILIES - 1)) % FAMILIES
        family = jnp.where(ranking < CAP, heaviest, others).astype(jnp.int32)
        one_hot = (family[:, None] == jnp.arange(FAMILIES, dtype=jnp.int32)[None, :]).astype(jnp.int32)
        before = jnp.cumsum(one_hot, axis=0) - one_hot
        within = jnp.sum(before * one_hot, axis=1)
        return (family * CAP + within).astype(jnp.int32)
    slots = jax.vmap(draw_block)(all_keys)
    return slots.reshape(blocks_x, blocks_y, blocks_z, CX, CY, CZ).transpose(0, 3, 1, 4, 2, 5).reshape(NX, NY, NZ)


def plant(result, rng, least, high):
    dims = result.shape
    spot = [jax.random.randint(jax.random.fold_in(rng, axis), (), 0, dims[axis]) for axis in range(len(dims))]
    result = result.at[tuple(spot)].set(least)
    longest = dims.index(max(dims))
    spot[longest] = (spot[longest] + 1) % dims[longest]
    return result.at[tuple(spot)].set(high)


def shard_levels(stream_key, shape, cuts, smallest, top_value):
    factor_of = 1.0
    for dim, parts in cuts:
        steps = jax.random.uniform(jax.random.fold_in(jax.random.fold_in(stream_key, 6), dim), (parts,), jnp.float32, smallest / len(cuts), top_value / len(cuts))
        factor_of = factor_of * jnp.repeat(jnp.exp(steps), shape[dim] // parts).reshape((-1,) + (1,) * (len(shape) - 1 - dim))
    return factor_of


def scatter_about(rng, extent, width, bound, shards=(), kind=jnp.bfloat16):
    result = width * jax.random.normal(rng, extent, jnp.float32)
    if shards:
        result = result * shard_levels(rng, extent, shards, -0.22, 0.18)
    return jnp.clip(result, -bound, bound).astype(kind)


def setup_inputs(seed: int = 0) -> dict:
    key_list = jax.random.split(jax.random.key(seed), 10)
    return {
        "displacement": scatter_about(key_list[0], (NX, NY, NZ), 1.0, 6.0, ((0, 4), (1, 4), (2, 2)), jnp.float32),
        "load_field": scatter_about(key_list[1], (NX, NY, NZ), 1.0, 6.0, ((0, 4), (1, 4), (2, 2)), jnp.float32),
        "foundation": jnp.clip(jnp.exp(math.log(2.0) - 2.3025851 * jax.random.uniform(key_list[2], (NX, NY, NZ), jnp.float32) ** shard_levels(key_list[2], (NX, NY, NZ), ((0, 4), (1, 4), (2, 2)), -0.2, 0.2)), 0.2, 2.0),
        "plastic_flags": plant((jax.random.randint(key_list[3], (NX, NY, NZ), 0, 2) < 1).astype(jnp.int32), jax.random.fold_in(key_list[3], 1), 0, 1),
        "point_slot": draw_point_slot(jax.random.fold_in(key_list[9], 71), 0),
        "family_in": scatter_about(key_list[5], (FAMILIES, 3, MODES), 1.0, 5.0, (), jnp.float32),
        "family_mid": scatter_about(key_list[6], (FAMILIES, MODES, MODES), MODES ** -0.5, 0.375),
        "family_out": scatter_about(key_list[7], (FAMILIES, 3, MODES), MODES ** -0.5, 0.375),
        "family_tan": jnp.clip(jnp.exp(jax.random.uniform(key_list[8], (FAMILIES, MODES), jnp.float32, math.log(0.002), math.log(0.02))), 0.002, 0.02),
    }


def central_diff(values, dim_index):
    if dim_index == 0:
        return (jnp.roll(values, -1, 0) - jnp.roll(values, 1, 0)) * 0.5
    widths = [(0, 0), (0, 0), (0, 0)]
    widths[dim_index] = (1, 1)
    padded = jnp.pad(values, widths)
    length = values.shape[dim_index]
    upper_side = lax.slice_in_dim(padded, 2, length + 2, axis=dim_index)
    lower_side = lax.slice_in_dim(padded, 0, length, axis=dim_index)
    return (upper_side - lower_side) * 0.5


def fibre_model(block_rows, weight_in, weight_mid, weight_out, weight_tan):
    modal = weight_in[0][:, None] * block_rows[0][None, :] + weight_in[1][:, None] * block_rows[1][None, :] + weight_in[2][:, None] * block_rows[2][None, :]
    active = jnp.where(block_rows[3][None, :] > 0.5, jnp.tanh(modal), modal).astype(jnp.bfloat16)
    hidden = jnp.dot(weight_mid, active, preferred_element_type=jnp.float32)
    bounded = jnp.tanh(hidden).astype(jnp.bfloat16)
    stress = jnp.dot(weight_out, bounded, preferred_element_type=jnp.float32)
    widened = bounded.astype(jnp.float32)
    tangent = 0.5 + jnp.dot(weight_tan, widened * widened, precision=lax.Precision.HIGHEST)
    return jnp.concatenate([stress, tangent[None, :]], axis=0)


def reference(displacement, load_field, foundation, plastic_flags, point_slot, family_in, family_mid, family_out, family_tan):
    strains = [central_diff(displacement, dim_index) for dim_index in range(3)]
    payload = jnp.stack(strains + [plastic_flags.astype(jnp.float32)], axis=0)
    blocks_x = NX // CX
    blocks_y = NY // CY
    blocks_z = NZ // CZ
    block_count = blocks_x * blocks_y * blocks_z
    points_dev = CX * CY * CZ
    blocked_rows = payload.reshape(4, blocks_x, CX, blocks_y, CY, blocks_z, CZ).transpose(1, 3, 5, 0, 2, 4, 6).reshape(block_count, 4, points_dev)
    blocked_slots = point_slot.reshape(blocks_x, CX, blocks_y, CY, blocks_z, CZ).transpose(0, 2, 4, 1, 3, 5).reshape(block_count, points_dev)

    def evaluate_block(inputs):
        block_rows, block_slots = inputs
        padded = jnp.zeros((4, FAMILIES * CAP), jnp.float32).at[:, block_slots].set(block_rows)
        results = [fibre_model(padded[:, family_index * CAP:(family_index + 1) * CAP], family_in[family_index], family_mid[family_index], family_out[family_index], family_tan[family_index]) for family_index in range(FAMILIES)]
        merged = jnp.concatenate(results, axis=1)
        return merged[:, block_slots]

    evaluated = lax.map(evaluate_block, (blocked_rows, blocked_slots))
    answers = evaluated.reshape(blocks_x, blocks_y, blocks_z, 4, CX, CY, CZ).transpose(3, 0, 4, 1, 5, 2, 6).reshape(4, NX, NY, NZ)
    tangent = answers[3]
    rhs = load_field - foundation * displacement + (central_diff(answers[0], 0) + central_diff(answers[1], 1) + central_diff(answers[2], 2))

    def stiffness(values):
        total = central_diff(tangent * central_diff(values, 0), 0) + central_diff(tangent * central_diff(values, 1), 1) + central_diff(tangent * central_diff(values, 2), 2)
        return foundation * values - total

    solution = jnp.zeros_like(rhs)
    residual = rhs
    direction = rhs
    current = jnp.sum(residual * residual)
    for iteration in range(ITERS):
        image = stiffness(direction)
        alpha = current / jnp.sum(direction * image)
        solution = solution + alpha * direction
        residual = residual - alpha * image
        following = jnp.sum(residual * residual)
        direction = residual + (following / current) * direction
        current = following
    return displacement + solution, residual
```

```python
import jax
import jax.numpy as jnp
from jax import lax
from jax.experimental import pallas as pl
from jax.experimental.pallas import tpu as pltpu
from jax.sharding import PartitionSpec as P

ITERS = 8
AXES = ("blk", "slab", "micro")
BF = jnp.bfloat16
F32 = jnp.float32


def split(value):
    high = lax.reduce_precision(value, 8, 7)
    return high.astype(BF), (value - high).astype(BF)


def pack_families(family_in, family_mid, family_out, family_tan):
    families, _, modes = family_in.shape
    spread = jnp.transpose(family_in, (2, 1, 0))
    spread = jnp.concatenate([spread, spread], axis=2).reshape(modes, 6 * families)
    high, low = split(spread)
    weight_in = jnp.concatenate([high, low], axis=1)
    weight_mid = jnp.transpose(family_mid, (1, 0, 2)).reshape(modes, families * modes)
    none = jnp.zeros((families, 1, modes), BF)
    stress = jnp.concatenate([family_out, none], axis=1).reshape(4 * families, modes)
    none = jnp.zeros((families, 3, modes), BF)
    tan_high, tan_low = split(family_tan)
    tan_high = jnp.concatenate([none, tan_high[:, None]], axis=1).reshape(4 * families, modes)
    tan_low = jnp.concatenate([none, tan_low[:, None]], axis=1).reshape(4 * families, modes)
    weight_out = jnp.concatenate(
        [
            jnp.concatenate([stress, tan_high, tan_high], axis=1),
            jnp.concatenate([jnp.zeros_like(stress), tan_low, tan_low], axis=1),
        ],
        axis=0,
    )
    return weight_in, weight_mid, weight_out


def cells_kernel(families, planes, strain_ref, code_ref, in_ref, mid_ref, out_ref, answer_ref):
    modes = in_ref.shape[0]
    spots = [(a, x) for a in range(code_ref.shape[0]) for x in planes]
    width = len(spots) * 128
    place = lax.broadcasted_iota(jnp.int32, (2 * families, 128), 0)
    column, family_row, flag_row = [], [], []
    for a, x in spots:
        code = code_ref[a, pl.ds(x, 1), :]
        family = lax.shift_right_logical(code, 1)
        picked = lax.rem(place, families) == jnp.broadcast_to(family, place.shape)
        pieces = []
        for j in range(3):
            value = jnp.broadcast_to(strain_ref[j, a, pl.ds(x, 1), :], place.shape)
            high = value.astype(BF).astype(F32)
            piece = jnp.where(place < families, high, value - high)
            pieces.append(jnp.where(picked, piece, 0.0))
        column.append(jnp.concatenate(pieces, axis=0))
        family_row.append(family)
        flag_row.append(lax.bitwise_and(code, 1))
    spread = jnp.concatenate(column, axis=1).astype(BF)
    spread = jnp.concatenate([spread, spread], axis=0)
    family = jnp.concatenate(family_row, axis=1)
    flag = jnp.concatenate(flag_row, axis=1)
    modal = jnp.dot(in_ref[...], spread, preferred_element_type=F32)
    flagged = jnp.broadcast_to(flag, (modes, width)) > 0
    active = jnp.where(flagged, jnp.tanh(modal), modal).astype(BF)
    wide = jnp.broadcast_to(family, (modes, width)).astype(BF)
    nothing = jnp.zeros_like(active)
    stacked = jnp.concatenate(
        [jnp.where(wide == jnp.array(f, BF), active, nothing) for f in range(families)], axis=0
    )
    hidden = jnp.dot(mid_ref[...], stacked, preferred_element_type=F32)
    bounded = jnp.tanh(hidden).astype(BF)
    square = bounded.astype(F32) * bounded.astype(F32)
    square_high = square.astype(BF)
    square_low = (square - square_high.astype(F32)).astype(BF)
    all_three = jnp.concatenate([bounded, square_high, square_low], axis=0)
    result = jnp.dot(out_ref[...], all_three, preferred_element_type=F32)
    result = result[: 4 * families] + result[4 * families :]
    owner = lax.shift_right_logical(lax.broadcasted_iota(jnp.int32, (4 * families, width), 0), 2)
    result = jnp.where(owner == family, result, 0.0)
    total = result[:4]
    for f in range(1, families):
        total = total + result[4 * f : 4 * f + 4]
    for i, (a, x) in enumerate(spots):
        answer_ref[:, a, x, :] = total[:, i * 128 : (i + 1) * 128]


def cells(strain, code, packed, families, step, planes):
    weight_in, weight_mid, weight_out = packed
    count = code.shape[0]
    planes = tuple(planes)
    points = count * len(planes) * 128
    modes = weight_in.shape[0]

    def whole(array):
        return pl.BlockSpec(array.shape, lambda i: (0,) * array.ndim)

    def kernel(*refs):
        cells_kernel(families, planes, *refs)

    return pl.pallas_call(
        kernel,
        grid=(count // step,),
        in_specs=[
            pl.BlockSpec((3, step, 8, 128), lambda i: (0, i, 0, 0)),
            pl.BlockSpec((step, 8, 128), lambda i: (i, 0, 0)),
            whole(weight_in),
            whole(weight_mid),
            whole(weight_out),
        ],
        out_specs=pl.BlockSpec((4, step, 8, 128), lambda i: (0, i, 0, 0)),
        out_shape=jax.ShapeDtypeStruct((4, count, 8, 128), F32),
        compiler_params=pltpu.CompilerParams(vmem_limit_bytes=48 * 2**20),
        cost_estimate=pl.CostEstimate(
            flops=2 * points * modes * modes * (families + 1), bytes_accessed=points * 32, transcendentals=2 * points * modes
        ),
        name="cells",
    )(strain, code, weight_in, weight_mid, weight_out)


def global_sum(value):
    count = 1
    for axis in AXES:
        count = count * lax.axis_size(axis)
    spread = jnp.broadcast_to(value.reshape(1, 1), (count, 128))
    return jnp.sum(lax.all_to_all(spread, AXES, 0, 0, tiled=True)[:, 0])


def widened(cells_, axis, dim, width, closed):
    count = lax.axis_size(axis)
    ends = count if closed else count - 1
    head = lax.slice_in_dim(cells_, 0, width, axis=dim)
    tail = lax.slice_in_dim(cells_, cells_.shape[dim] - width, cells_.shape[dim], axis=dim)
    before = lax.ppermute(tail, axis, [(i, (i + 1) % count) for i in range(ends)])
    after = lax.ppermute(head, axis, [((i + 1) % count, i) for i in range(ends)])
    return jnp.concatenate([before, cells_, after], axis=dim)


HALOS = (("blk", True), ("micro", False), ("slab", False))


def widened_all(field, width):
    return [widened(field, axis, dim, width, closed) for dim, (axis, closed) in enumerate(HALOS)]


def difference(field, dim):
    length = field.shape[dim]
    return (lax.slice_in_dim(field, 2, length, axis=dim) - lax.slice_in_dim(field, 0, length - 2, axis=dim)) * 0.5


def plain_body(
    displacement, load_field, foundation, plastic_flags, point_slot, family_in, family_mid, family_out, family_tan
):
    size_x, size_y, size_z = displacement.shape
    points = size_x * size_y * size_z
    families = family_in.shape[0]
    capacity = points // 2
    packed = pack_families(family_in, family_mid, family_out, family_tan)
    strain = [difference(w, dim) for dim, w in enumerate(widened_all(displacement, 1))]
    code = 2 * (point_slot // capacity) + plastic_flags
    tiles = points // 1024
    answers = cells(jnp.stack(strain).reshape(3, tiles, 8, 128), code.reshape(tiles, 8, 128), packed, families, 2, range(8))
    answers = answers.reshape(4, size_x, size_y, size_z)
    tangents = widened_all(0.5 + answers[3], 1)
    divergence = sum(
        difference(widened(answers[dim], axis, dim, 1, closed), dim) for dim, (axis, closed) in enumerate(HALOS)
    )
    rhs = load_field - foundation * displacement + divergence
    solution_ = jnp.zeros_like(rhs)
    residual = rhs
    direction = rhs
    current = global_sum(jnp.sum(residual * residual))
    for _ in range(ITERS):
        total = sum(
            difference(tangents[dim] * difference(w, dim), dim) for dim, w in enumerate(widened_all(direction, 2))
        )
        image = foundation * direction - total
        alpha = current / global_sum(jnp.sum(direction * image))
        solution_ = solution_ + alpha * direction
        residual = residual - alpha * image
        following = global_sum(jnp.sum(residual * residual))
        direction = residual + following / current * direction
        current = following
    return displacement + solution_, residual


VMEM = pl.BlockSpec(memory_space=pltpu.VMEM)
SMEM = pl.BlockSpec(memory_space=pltpu.SMEM)
GROUP = ("blk", "micro")


def call(kernel, out_shapes, scratch, name, *args, smem=0):
    return pl.pallas_call(
        kernel,
        out_shape=[jax.ShapeDtypeStruct(shape, dtype) for shape, dtype in out_shapes],
        in_specs=[SMEM] * smem + [VMEM] * (len(args) - smem),
        out_specs=[VMEM] * len(out_shapes),
        scratch_shapes=scratch,
        compiler_params=pltpu.CompilerParams(vmem_limit_bytes=40 * 2**20),
        name=name,
    )(*args)


def regroup(tiles):
    group = lax.broadcasted_iota(jnp.int32, (8, 128), 1) // 32
    result = []
    for a in range(4):
        tile = tiles[0]
        for m in range(4):
            shift = (m - a) * 32 % 128
            moved = pltpu.roll(tiles[m], shift, 1) if shift else tiles[m]
            tile = moved if m == 0 else jnp.where(group == m, moved, tile)
        result.append(tile)
    return result


def spread_kernel(place_ref, u_ref, load_ref, found_ref, code_ref, send_ref, turned):
    count = send_ref.shape[0]
    rest = load_ref[...] - found_ref[...] * u_ref[...]
    fields = (u_ref[...], code_ref[...].astype(F32), found_ref[...], rest)
    for number, field in enumerate(fields):
        for half in range(2):
            turned[number, half, 8:136, :] = jnp.transpose(field[4 * half : 4 * half + 4].reshape(128, 128))
    for half in range(2):
        turned[0, half, 0:8, :] = jnp.zeros((8, 128), F32)
        turned[0, half, 136:144, :] = jnp.zeros((8, 128), F32)
    row = lax.broadcasted_iota(jnp.int32, (8, 128), 0)
    for target in range(count):
        start = pl.multiple_of(8 * place_ref[target], 8)
        for number in range(4):
            for half in range(2):
                send_ref[target, 2 * number + half] = turned[number, half, pl.ds(start + 8, 8), :]
        edges = jnp.zeros((8, 128), F32)
        for half in range(2):
            low = turned[0, half, pl.ds(start, 8), :]
            high = turned[0, half, pl.ds(start + 16, 8), :]
            edges = jnp.where(row == half, jnp.broadcast_to(low[7:8], (8, 128)), edges)
            edges = jnp.where(row == 2 + half, jnp.broadcast_to(high[0:1], (8, 128)), edges)
        send_ref[target, 8] = edges


def beside(tile, low, high):
    row = lax.broadcasted_iota(jnp.int32, (8, 128), 0)
    after = jnp.where(row == 7, jnp.broadcast_to(high, (8, 128)), pltpu.roll(tile, 7, 0))
    before = jnp.where(row == 0, jnp.broadcast_to(low, (8, 128)), pltpu.roll(tile, 1, 0))
    return after, before


def radial(tile):
    lane = lax.broadcasted_iota(jnp.int32, tile.shape, tile.ndim - 1)
    after = jnp.where(lane == 127, 0.0, pltpu.roll(tile, 127, tile.ndim - 1))
    before = jnp.where(lane == 0, 0.0, pltpu.roll(tile, 1, tile.ndim - 1))
    return (after - before) * 0.5


def collect_kernel(around, recv_ref, strain_ref, code_ref, found_ref, rest_ref, u):
    along = recv_ref.shape[0] // 4
    edges = []
    for b in range(along):
        for half in range(2):
            for number in range(4):
                tiles = regroup([recv_ref[4 * b + m, 2 * number + half] for m in range(4)])
                for a in range(4):
                    at = 8 * b + 4 * half + a
                    if number == 0:
                        u[at] = tiles[a]
                    elif number == 1:
                        code_ref[at] = tiles[a].astype(jnp.int32)
                    elif number == 2:
                        found_ref[at] = tiles[a]
                    else:
                        rest_ref[at] = tiles[a]
        edges.append(regroup([recv_ref[4 * b + m, 8] for m in range(4)]))
    for at in range(around):
        tile = u[at]
        strain_ref[0, at] = (u[(at + 1) % around] - u[(at - 1) % around]) * 0.5
        strain_ref[1, at] = radial(tile)
        edge, half = edges[at // 8][at % 4], at % 8 // 4
        after, before = beside(tile, edge[half : half + 1], edge[2 + half : 3 + half])
        strain_ref[2, at] = (after - before) * 0.5


def rhs_kernel(around, outer_ref, inner_ref, rest_ref, low_ref, high_ref, own_ref):
    row = lax.broadcasted_iota(jnp.int32, (8, 128), 0)
    rim = (row == 0) | (row == 7)

    def answer(number, at):
        return jnp.where(rim, outer_ref[number, at], inner_ref[number, at])

    cycle = [answer(0, at) for at in range(around)]
    for at in range(around):
        low = low_ref[around + at // 8, pl.ds(at % 8, 1), :]
        high = high_ref[around + at // 8, pl.ds(at % 8, 1), :]
        after, before = beside(answer(2, at), low, high)
        divergence = (cycle[(at + 1) % around] - cycle[(at - 1) % around]) * 0.5
        divergence = divergence + radial(answer(1, at)) + (after - before) * 0.5
        own_ref[0, at] = rest_ref[at] + divergence
        own_ref[1, at] = 0.5 + answer(3, at)


HALF = ITERS // 2


def basis_kernel(
    around, seeds, ends_ref, scale_ref, tan_ref, tan_low_ref, tan_high_ref, found_ref, found_low_ref, found_high_ref,
    seed_ref, seed_low_ref, seed_high_ref, own_ref, gram_ref, tan, main, off_a, off_r, back_r, off_x, back_x, vectors
):
    centre, inverse = scale_ref[0], scale_ref[1]
    lane = lax.broadcasted_iota(jnp.int32, (24, 128), 1)
    plane = lax.broadcasted_iota(jnp.int32, (24, 128), 0)
    cut = ((plane == 7) & (ends_ref[0] == 1)) | ((plane == 14) & (ends_ref[1] == 1))
    quarter = 0.25 * inverse

    def three(low, own, high):
        return jnp.concatenate([low, own, high], axis=0)

    for at in range(around):
        tan[at] = three(tan_low_ref[at], tan_ref[at], tan_high_ref[at]) * quarter
    for at in range(around):
        here = tan[at]
        up_a, down_a = tan[(at + 1) % around], tan[(at - 1) % around]
        up_r = jnp.where(lane == 127, 0.0, pltpu.roll(here, 127, 1))
        down_r = jnp.where(lane == 0, 0.0, pltpu.roll(here, 1, 1))
        up_x = pltpu.roll(here, 23, 0)
        down_x = pltpu.roll(here, 1, 0)
        found = three(found_low_ref[at], found_ref[at], found_high_ref[at])
        main[at] = (found - centre) * inverse + ((up_a + down_a) + (up_r + down_r) + (up_x + down_x))
        beyond = jnp.where(lane >= 126, 0.0, up_r)
        off_r[at] = beyond
        back_r[at] = pltpu.roll(beyond, 2, 1)
        beyond = jnp.where(cut, 0.0, up_x)
        off_x[at] = beyond
        back_x[at] = pltpu.roll(beyond, 2, 0)

    def apply(index, at):
        value = vectors[index, at]
        result = main[at] * value
        result = result - tan[(at + 1) % around] * vectors[index, (at + 2) % around]
        result = result - tan[(at - 1) % around] * vectors[index, (at - 2) % around]
        result = result - off_r[at] * pltpu.roll(value, 126, 1) - back_r[at] * pltpu.roll(value, 2, 1)
        return result - off_x[at] * pltpu.roll(value, 22, 0) - back_x[at] * pltpu.roll(value, 2, 0)

    size = HALF + 1
    for seed in range(seeds):
        base = seed * size
        for at in range(around):
            vectors[base, at] = three(seed_low_ref[seed, at], seed_ref[seed, at], seed_high_ref[seed, at])
        for degree in range(1, size):
            for at in range(around):
                value = apply(base + degree - 1, at)
                if degree > 1:
                    value = value + value - vectors[base + degree - 2, at]
                vectors[base + degree, at] = value
    total = seeds * size
    for index in range(total):
        for at in range(around):
            own_ref[index, at] = vectors[index, at, 8:16, :]
    column = lax.broadcasted_iota(jnp.int32, (1, 128), 1)
    gram = jnp.zeros((1, 128), F32)
    number = 0
    for i in range(total):
        sums = [jnp.zeros((8, 128), F32)] * (total - i)
        for at in range(around):
            left = own_ref[i, at]
            for j in range(i, total):
                sums[j - i] = sums[j - i] + left * own_ref[j, at]
        for value in sums:
            entry = jnp.sum(jnp.sum(value, axis=0, keepdims=True), axis=1, keepdims=True)
            gram = jnp.where(column == number, jnp.broadcast_to(entry, (1, 128)), gram)
            number += 1
    gram_ref[...] = gram


def unpack_gram(all_ref, total):
    row = jnp.sum(all_ref[...], axis=0, keepdims=True)
    gram, number = {}, 0
    for i in range(total):
        for j in range(i, total):
            gram[i, j] = gram[j, i] = jnp.broadcast_to(row[:, number : number + 1], (1, 128))
            number += 1
    return gram


def dot(gram, left, right):
    total = len(left)
    result = None
    for i in range(total):
        if left[i] is None:
            continue
        inner = None
        for j in range(total):
            if right[j] is not None:
                term = gram[i, j] * right[j]
                inner = term if inner is None else inner + term
        if inner is not None:
            result = left[i] * inner if result is None else result + left[i] * inner
    return result


def axpy(scale, left, right):
    result = []
    for a, b in zip(left, right, strict=True):
        a = None if a is None else (a if scale is None else scale * a)
        result.append(b if a is None else (a if b is None else b + a))
    return result


def times_operator(vector, centre, half_width, size):
    result = []
    half = 0.5 * half_width
    for base in range(0, len(vector), size):
        part = vector[base : base + size]
        for j in range(size):
            terms = []
            if part[j] is not None:
                terms.append(centre * part[j])
            if j > 0 and part[j - 1] is not None:
                terms.append((half_width if j == 1 else half) * part[j - 1])
            if j + 1 < size and part[j + 1] is not None:
                terms.append(half * part[j + 1])
            result.append(sum(terms[1:], terms[0]) if terms else None)
    return result


def iterate(gram, total, residual, direction, current, centre, half_width, worst):
    size = HALF + 1
    change = [None] * total
    norms = [jnp.sqrt(gram[i, i]) for i in range(total)]
    before = current
    for step in range(HALF):
        image = times_operator(direction, centre, half_width, size)
        alpha = current / dot(gram, direction, image)
        change = axpy(alpha, direction, change)
        residual = axpy(-alpha, image, residual)
        following = dot(gram, residual, residual)
        bound = None
        for c, n in zip(residual, norms, strict=True):
            if c is not None:
                bound = jnp.abs(c) * n if bound is None else bound + jnp.abs(c) * n
        worst = jnp.maximum(worst, bound * bound / following)
        worst = jnp.where(following > 0.0, worst, jnp.inf)
        before = current
        if step < HALF - 1:
            direction = axpy(following / current, direction, residual)
        current = following
    return change, residual, direction, before, current, worst


def combine(coefficients, own_ref, at):
    result = None
    for index, c in enumerate(coefficients):
        if c is not None:
            term = jnp.broadcast_to(c, (8, 128)) * own_ref[index, at]
            result = term if result is None else result + term
    return result


def middle_kernel(around, scale_ref, all_ref, own_ref, seeds_ref, change_ref, state_ref):
    total = HALF + 1
    gram = unpack_gram(all_ref, total)
    one = [jnp.ones((1, 128), F32)] + [None] * HALF
    nothing = jnp.zeros((1, 128), F32)
    change, residual, direction, before, _, worst = iterate(
        gram, total, one, one, gram[0, 0], scale_ref[0], scale_ref[2], nothing
    )
    for at in range(around):
        seeds_ref[0, at] = combine(residual, own_ref, at)
        seeds_ref[1, at] = combine(direction, own_ref, at)
        change_ref[at] = combine(change, own_ref, at)
    state_ref[...] = jnp.concatenate([before, worst] + [nothing] * 6, axis=0)


def last_kernel(around, scale_ref, all_ref, own_ref, change_ref, state_ref, send_ref, worst_ref):
    size = HALF + 1
    total = 2 * size
    gram = unpack_gram(all_ref, total)
    ones = jnp.ones((1, 128), F32)
    residual = [ones] + [None] * (total - 1)
    beta = gram[0, 0] / state_ref[0:1, :]
    direction = list(residual)
    direction[size] = beta
    change, residual, _, _, _, worst = iterate(
        gram, total, residual, direction, gram[0, 0], scale_ref[0], scale_ref[2], state_ref[1:2, :]
    )
    worst_ref[...] = jnp.broadcast_to(worst, (8, 128))
    for b in range(around // 8):
        for half in range(2):
            for number in range(2):
                tiles = []
                for a in range(4):
                    at = 8 * b + 4 * half + a
                    if number == 0:
                        tiles.append(change_ref[at] + combine(change, own_ref, at))
                    else:
                        tiles.append(combine(residual, own_ref, at))
                tiles = regroup(tiles)
                for m in range(4):
                    send_ref[4 * b + m, 2 * number + half] = tiles[m]


def deliver_kernel(place_ref, u_ref, recv_ref, updated_ref, residual_ref, turned):
    for source in range(recv_ref.shape[0]):
        start = pl.multiple_of(8 * place_ref[source], 8)
        for index in range(4):
            turned[index, pl.ds(start, 8), :] = recv_ref[source, index]
    for half in range(2):
        part = slice(4 * half, 4 * half + 4)
        updated_ref[part] = u_ref[part] + jnp.transpose(turned[half]).reshape(4, 32, 128)
        residual_ref[part] = jnp.transpose(turned[2 + half]).reshape(4, 32, 128)


def sliced_body(
    displacement, load_field, foundation, plastic_flags, point_slot, family_in, family_mid, family_out, family_tan
):
    size_x, size_y, size_z = displacement.shape
    families = family_in.shape[0]
    along, across = lax.axis_size("blk"), lax.axis_size("micro")
    peers = along * across
    around = size_x * along
    everyone = peers * lax.axis_size("slab")
    slab = lax.axis_index("slab")
    path = [b * across + (m if b % 2 == 0 else across - 1 - m) for b in range(along) for m in range(across)]
    forth = jnp.array(path, jnp.int32)
    place = jnp.where(slab == 0, forth, peers - 1 - forth)
    mine = jnp.take(place, lax.axis_index("blk") * across + lax.axis_index("micro")) + peers * slab
    ends = jnp.stack([(mine == 0), (mine == everyone - 1)]).astype(jnp.int32)
    spots = [0] * everyone
    for b in range(along):
        for s in range(2):
            for m in range(across):
                position = path[b * across + m]
                spots[position if s == 0 else 2 * peers - 1 - position] = (b * 2 + s) * across + m
    rising = [(spots[i], spots[i + 1]) for i in range(everyone - 1)]
    falling = [(b, a) for a, b in rising]

    def neighbours(to_next, to_previous):
        return lax.ppermute(to_next, AXES, rising), lax.ppermute(to_previous, AXES, falling)

    packed = pack_families(family_in, family_mid, family_out, family_tan)
    typical = 0.5 + 0.33 * jnp.mean(jnp.sum(family_tan, axis=1))
    centre = 1.1 + 1.5 * typical
    half_width = centre - 0.2
    scale = jnp.stack([centre, 1.0 / half_width, half_width])

    rim = jnp.where(slab == 0, displacement[:, :, size_z - 1], displacement[:, :, 0]).reshape(2, 128)
    rim = lax.ppermute(rim, "slab", [(0, 1), (1, 0)])
    code = 2 * (point_slot // (size_x * size_y * size_z // 2)) + plastic_flags
    (send,) = call(
        spread_kernel, [((peers, 9, 8, 128), F32)], [pltpu.VMEM((4, 2, 144, 128), F32)], "spread",
        place, displacement, load_field, foundation, code, smem=1,
    )
    middle = path.index(peers - 1)
    send = lax.dynamic_update_slice(send, rim[None, None], (middle, 8, jnp.where(slab == 0, 2, 0), 0))
    recv = lax.all_to_all(send, GROUP, 0, 0, tiled=True)
    field = (around, 8, 128)
    strain, code, found, rest = call(
        lambda *refs: collect_kernel(around, *refs),
        [((3,) + field, F32), (field, jnp.int32), (field, F32), (field, F32)],
        [pltpu.VMEM(field, F32)], "collect", recv,
    )
    outer = cells(strain, code, packed, families, 8, (0, 7))
    rows = (around // 8, 8, 128)
    low, high = neighbours(
        jnp.concatenate([found, outer[2, :, 7].reshape(rows)]), jnp.concatenate([found, outer[2, :, 0].reshape(rows)])
    )
    inner = cells(strain, code, packed, families, 4, range(1, 7))
    (own,) = call(
        lambda *refs: rhs_kernel(around, *refs), [((2,) + field, F32)], [], "rhs", outer, inner, rest, low, high
    )
    own_low, own_high = neighbours(own, own)

    def basis(seeds, tangents, vectors):
        tall = pltpu.VMEM((around, 24, 128), F32)
        total = seeds * (HALF + 1)
        products, gram = call(
            lambda *refs: basis_kernel(around, seeds, *refs),
            [((total,) + field, F32), ((1, 128), F32)],
            [tall] * 7 + [pltpu.VMEM((total, around, 24, 128), F32)],
            "basis", ends, scale, *tangents, found, low, high, *vectors, smem=2,
        )
        return products, lax.all_to_all(jnp.broadcast_to(gram, (everyone, 128)), AXES, 0, 0, tiled=True)

    tangents = (own[1], own_low[1], own_high[1])
    first, sums = basis(1, tangents, (own[:1], own_low[:1], own_high[:1]))
    seeds, change, state = call(
        lambda *refs: middle_kernel(around, *refs),
        [((2,) + field, F32), (field, F32), ((8, 128), F32)], [], "middle", scale, sums, first, smem=1,
    )
    second, sums = basis(2, tangents, (seeds, *neighbours(seeds, seeds)))
    send, worst = call(
        lambda *refs: last_kernel(around, *refs),
        [((peers, 4, 8, 128), F32), ((8, 128), F32)], [], "last", scale, sums, second, change, state, smem=1,
    )
    recv = lax.all_to_all(send, GROUP, 0, 0, tiled=True)
    shape = displacement.shape
    updated, residual = call(
        deliver_kernel, [(shape, F32), (shape, F32)], [pltpu.VMEM((4, 128, 128), F32)], "deliver",
        place, displacement, recv, smem=1,
    )
    return updated, residual, worst[0, 0]


MOST_LOST = 3000.0


def body(*inputs):
    size_x, size_y, size_z = inputs[0].shape
    along, across = lax.axis_size("blk"), lax.axis_size("micro")
    fits = (
        (size_x, size_y, size_z) == (8, 32, 128)
        and across == 4
        and size_z == 8 * along * across
        and lax.axis_size("slab") == 2
    )
    if not fits:
        return plain_body(*inputs)
    updated, residual, worst = sliced_body(*inputs)
    return lax.cond(worst < MOST_LOST, lambda: (updated, residual), lambda: plain_body(*inputs))


def solution(mesh):
    field = P("blk", "micro", "slab")
    return jax.shard_map(
        body,
        mesh=mesh,
        in_specs=(field,) * 5 + (P(),) * 4,
        out_specs=(field, field),
        check_vma=False,
    )
```

```python
import jax
import jax.numpy as jnp
from jax import lax
from jax.experimental import pallas as pl
from jax.experimental.pallas import tpu as pltpu
from jax.sharding import PartitionSpec as P

ITERS = 8
AXES = ("blk", "slab", "micro")
BF = jnp.bfloat16
F32 = jnp.float32


def split(value):
    high = lax.reduce_precision(value, 8, 7)
    return high.astype(BF), (value - high).astype(BF)


def pack_families(family_in, family_mid, family_out, family_tan):
    families, _, modes = family_in.shape
    spread = jnp.transpose(family_in, (2, 1, 0))
    spread = jnp.concatenate([spread, spread], axis=2).reshape(modes, 6 * families)
    high, low = split(spread)
    weight_in = jnp.concatenate([high, low], axis=1)
    weight_mid = jnp.transpose(family_mid, (1, 0, 2)).reshape(modes, families * modes)
    none = jnp.zeros((families, 1, modes), BF)
    stress = jnp.concatenate([family_out, none], axis=1).reshape(4 * families, modes)
    none = jnp.zeros((families, 3, modes), BF)
    tan_high, tan_low = split(family_tan)
    tan_high = jnp.concatenate([none, tan_high[:, None]], axis=1).reshape(4 * families, modes)
    tan_low = jnp.concatenate([none, tan_low[:, None]], axis=1).reshape(4 * families, modes)
    weight_out = jnp.concatenate(
        [
            jnp.concatenate([stress, tan_high, tan_high], axis=1),
            jnp.concatenate([jnp.zeros_like(stress), tan_low, tan_low], axis=1),
        ],
        axis=0,
    )
    return weight_in, weight_mid, weight_out


def cells_kernel(families, planes, strain_ref, code_ref, in_ref, mid_ref, out_ref, *refs):
    *edges, answer_ref = refs
    modes = in_ref.shape[0]
    spots = [(a, x) for a in range(code_ref.shape[0]) for x in planes]
    width = len(spots) * 128
    place = lax.broadcasted_iota(jnp.int32, (2 * families, 128), 0)
    column, family_row, flag_row = [], [], []
    for a, x in spots:
        code = code_ref[a, pl.ds(x, 1), :]
        family = lax.shift_right_logical(code, 1)
        picked = lax.rem(place, families) == jnp.broadcast_to(family, place.shape)
        pieces = []
        for j in range(3):
            value = strain_ref[j, a, pl.ds(x, 1), :]
            if edges and j == 2:
                part = edges[0 if x == 0 else 1][0, pl.ds(a, 1), :] * 0.5
                value = value - part if x == 0 else value + part
            value = jnp.broadcast_to(value, place.shape)
            high = value.astype(BF).astype(F32)
            piece = jnp.where(place < families, high, value - high)
            pieces.append(jnp.where(picked, piece, 0.0))
        column.append(jnp.concatenate(pieces, axis=0))
        family_row.append(family)
        flag_row.append(lax.bitwise_and(code, 1))
    spread = jnp.concatenate(column, axis=1).astype(BF)
    spread = jnp.concatenate([spread, spread], axis=0)
    family = jnp.concatenate(family_row, axis=1)
    flag = jnp.concatenate(flag_row, axis=1)
    modal = jnp.dot(in_ref[...], spread, preferred_element_type=F32)
    flagged = jnp.broadcast_to(flag, (modes, width)) > 0
    active = jnp.where(flagged, jnp.tanh(modal), modal).astype(BF)
    wide = jnp.broadcast_to(family, (modes, width)).astype(BF)
    nothing = jnp.zeros_like(active)
    stacked = jnp.concatenate(
        [jnp.where(wide == jnp.array(f, BF), active, nothing) for f in range(families)], axis=0
    )
    hidden = jnp.dot(mid_ref[...], stacked, preferred_element_type=F32)
    bounded = jnp.tanh(hidden).astype(BF)
    square = bounded.astype(F32) * bounded.astype(F32)
    square_high = square.astype(BF)
    square_low = (square - square_high.astype(F32)).astype(BF)
    all_three = jnp.concatenate([bounded, square_high, square_low], axis=0)
    result = jnp.dot(out_ref[...], all_three, preferred_element_type=F32)
    result = result[: 4 * families] + result[4 * families :]
    owner = lax.shift_right_logical(lax.broadcasted_iota(jnp.int32, (4 * families, width), 0), 2)
    result = jnp.where(owner == family, result, 0.0)
    total = result[:4]
    for f in range(1, families):
        total = total + result[4 * f : 4 * f + 4]
    for i, (a, x) in enumerate(spots):
        answer_ref[:, a, x, :] = total[:, i * 128 : (i + 1) * 128]


def cells(strain, code, packed, families, step, planes, *edges):
    weight_in, weight_mid, weight_out = packed
    count = code.shape[0]
    planes = tuple(planes)
    points = count * len(planes) * 128
    modes = weight_in.shape[0]

    def whole(array):
        return pl.BlockSpec(array.shape, lambda i: (0,) * array.ndim)

    def kernel(*refs):
        cells_kernel(families, planes, *refs)

    return pl.pallas_call(
        kernel,
        grid=(count // step,),
        in_specs=[
            pl.BlockSpec((3, step, 8, 128), lambda i: (0, i, 0, 0)),
            pl.BlockSpec((step, 8, 128), lambda i: (i, 0, 0)),
            whole(weight_in),
            whole(weight_mid),
            whole(weight_out),
        ]
        + [pl.BlockSpec((1, 8, 128), lambda i: (count + i, 0, 0)) for _ in edges],
        out_specs=pl.BlockSpec((4, step, 8, 128), lambda i: (0, i, 0, 0)),
        out_shape=jax.ShapeDtypeStruct((4, count, 8, 128), F32),
        compiler_params=pltpu.CompilerParams(vmem_limit_bytes=48 * 2**20),
        cost_estimate=pl.CostEstimate(
            flops=2 * points * modes * modes * (families + 1), bytes_accessed=points * 32, transcendentals=2 * points * modes
        ),
        name="cells",
    )(strain, code, weight_in, weight_mid, weight_out, *edges)


def global_sum(value):
    count = 1
    for axis in AXES:
        count = count * lax.axis_size(axis)
    spread = jnp.broadcast_to(value.reshape(1, 1), (count, 128))
    return jnp.sum(lax.all_to_all(spread, AXES, 0, 0, tiled=True)[:, 0])


def widened(cells_, axis, dim, width, closed):
    count = lax.axis_size(axis)
    ends = count if closed else count - 1
    head = lax.slice_in_dim(cells_, 0, width, axis=dim)
    tail = lax.slice_in_dim(cells_, cells_.shape[dim] - width, cells_.shape[dim], axis=dim)
    before = lax.ppermute(tail, axis, [(i, (i + 1) % count) for i in range(ends)])
    after = lax.ppermute(head, axis, [((i + 1) % count, i) for i in range(ends)])
    return jnp.concatenate([before, cells_, after], axis=dim)


HALOS = (("blk", True), ("micro", False), ("slab", False))


def widened_all(field, width):
    return [widened(field, axis, dim, width, closed) for dim, (axis, closed) in enumerate(HALOS)]


def difference(field, dim):
    length = field.shape[dim]
    return (lax.slice_in_dim(field, 2, length, axis=dim) - lax.slice_in_dim(field, 0, length - 2, axis=dim)) * 0.5


def plain_body(
    displacement, load_field, foundation, plastic_flags, point_slot, family_in, family_mid, family_out, family_tan
):
    size_x, size_y, size_z = displacement.shape
    points = size_x * size_y * size_z
    families = family_in.shape[0]
    capacity = points // 2
    packed = pack_families(family_in, family_mid, family_out, family_tan)
    strain = [difference(w, dim) for dim, w in enumerate(widened_all(displacement, 1))]
    code = 2 * (point_slot // capacity) + plastic_flags
    tiles = points // 1024
    answers = cells(jnp.stack(strain).reshape(3, tiles, 8, 128), code.reshape(tiles, 8, 128), packed, families, 2, range(8))
    answers = answers.reshape(4, size_x, size_y, size_z)
    tangents = widened_all(0.5 + answers[3], 1)
    divergence = sum(
        difference(widened(answers[dim], axis, dim, 1, closed), dim) for dim, (axis, closed) in enumerate(HALOS)
    )
    rhs = load_field - foundation * displacement + divergence
    solution_ = jnp.zeros_like(rhs)
    residual = rhs
    direction = rhs
    current = global_sum(jnp.sum(residual * residual))
    for _ in range(ITERS):
        total = sum(
            difference(tangents[dim] * difference(w, dim), dim) for dim, w in enumerate(widened_all(direction, 2))
        )
        image = foundation * direction - total
        alpha = current / global_sum(jnp.sum(direction * image))
        solution_ = solution_ + alpha * direction
        residual = residual - alpha * image
        following = global_sum(jnp.sum(residual * residual))
        direction = residual + following / current * direction
        current = following
    return displacement + solution_, residual


VMEM = pl.BlockSpec(memory_space=pltpu.VMEM)
SMEM = pl.BlockSpec(memory_space=pltpu.SMEM)
GROUP = ("blk", "micro")


def call(kernel, out_shapes, scratch, name, *args, smem=0):
    return pl.pallas_call(
        kernel,
        out_shape=[jax.ShapeDtypeStruct(shape, dtype) for shape, dtype in out_shapes],
        in_specs=[SMEM] * smem + [VMEM] * (len(args) - smem),
        out_specs=[VMEM] * len(out_shapes),
        scratch_shapes=scratch,
        compiler_params=pltpu.CompilerParams(vmem_limit_bytes=40 * 2**20),
        name=name,
    )(*args)


def regroup(tiles):
    group = lax.broadcasted_iota(jnp.int32, (8, 128), 1) // 32
    result = []
    for a in range(4):
        tile = tiles[0]
        for m in range(4):
            shift = (m - a) * 32 % 128
            moved = pltpu.roll(tiles[m], shift, 1) if shift else tiles[m]
            tile = moved if m == 0 else jnp.where(group == m, moved, tile)
        result.append(tile)
    return result


def place(slab, position, peers):
    return position + slab * (peers - 1 - 2 * position)


def spread_kernel(path, capacity, u_ref, load_ref, found_ref, slot_ref, flag_ref, send_ref, turned):
    peers = len(path)
    slab = lax.axis_index("slab")
    code = jnp.zeros(slot_ref.shape, jnp.int32)
    for family in range(1, 4):
        code = code + jnp.where(slot_ref[...] >= family * capacity, 2, 0)
    rest = load_ref[...] - found_ref[...] * u_ref[...]
    fields = (u_ref[...], (code + flag_ref[...]).astype(F32), found_ref[...], rest)
    for number, field in enumerate(fields):
        for half in range(2):
            turned[number, half] = jnp.transpose(field[4 * half : 4 * half + 4].reshape(128, 128))
    for target in range(peers):
        start = pl.multiple_of(8 * place(slab, path[target], peers), 8)
        for number in range(4):
            for half in range(2):
                send_ref[target, 2 * number + half] = turned[number, half, pl.ds(start, 8), :]


def beside(tile, low, high):
    row = lax.broadcasted_iota(jnp.int32, (8, 128), 0)
    after = jnp.where(row == 7, jnp.broadcast_to(high, (8, 128)), pltpu.roll(tile, 7, 0))
    before = jnp.where(row == 0, jnp.broadcast_to(low, (8, 128)), pltpu.roll(tile, 1, 0))
    return after, before


def radial(tile):
    lane = lax.broadcasted_iota(jnp.int32, tile.shape, tile.ndim - 1)
    after = jnp.where(lane == 127, 0.0, pltpu.roll(tile, 127, tile.ndim - 1))
    before = jnp.where(lane == 0, 0.0, pltpu.roll(tile, 1, tile.ndim - 1))
    return (after - before) * 0.5


def collect_kernel(around, recv_ref, strain_ref, code_ref, found_ref, rest_ref, next_ref, previous_ref, u):
    for b in range(around // 8):
        for half in range(2):
            for number in range(4):
                tiles = regroup([recv_ref[4 * b + m, 2 * number + half] for m in range(4)])
                for a in range(4):
                    at = 8 * b + 4 * half + a
                    if number == 0:
                        u[at] = tiles[a]
                    elif number == 1:
                        code_ref[at] = tiles[a].astype(jnp.int32)
                    elif number == 2:
                        found_ref[at] = tiles[a]
                        next_ref[at] = tiles[a]
                        previous_ref[at] = tiles[a]
                    else:
                        rest_ref[at] = tiles[a]
    nothing = jnp.zeros((1, 128), F32)
    for at in range(around):
        tile = u[at]
        strain_ref[0, at] = (u[(at + 1) % around] - u[(at - 1) % around]) * 0.5
        strain_ref[1, at] = radial(tile)
        after, before = beside(tile, nothing, nothing)
        strain_ref[2, at] = (after - before) * 0.5
        next_ref[around + at // 8, pl.ds(at % 8, 1), :] = tile[7:8]
        previous_ref[around + at // 8, pl.ds(at % 8, 1), :] = tile[0:1]


def rhs_kernel(around, first_ref, outer_ref, second_ref, rest_ref, low_ref, high_ref, own_ref):
    row = lax.broadcasted_iota(jnp.int32, (8, 128), 0)
    rim = (row == 0) | (row == 7)

    def answer(number, at):
        inner = jnp.where(row < 4, first_ref[number, at], second_ref[number, at])
        return jnp.where(rim, outer_ref[number, at], inner)

    cycle = [answer(0, at) for at in range(around)]
    for at in range(around):
        low = low_ref[at // 8, pl.ds(at % 8, 1), :]
        high = high_ref[at // 8, pl.ds(at % 8, 1), :]
        after, before = beside(answer(2, at), low, high)
        divergence = (cycle[(at + 1) % around] - cycle[(at - 1) % around]) * 0.5
        divergence = divergence + radial(answer(1, at)) + (after - before) * 0.5
        own_ref[0, at] = rest_ref[at] + divergence
        own_ref[1, at] = 0.5 + answer(3, at)


HALF = ITERS // 2


def basis_kernel(
    around, last, ends_ref, scale_ref, tan_ref, tan_low_ref, tan_high_ref, found_ref, found_low_ref, found_high_ref,
    seed_ref, seed_low_ref, seed_high_ref, *refs
):
    if last:
        earlier_ref, own_ref, gram_ref, *scratch = refs
    else:
        own_ref, *scratch = refs
    tan, main, off_r, back_r, off_x, back_x, vectors = scratch
    centre, inverse = scale_ref[0], scale_ref[1]
    lane = lax.broadcasted_iota(jnp.int32, (24, 128), 1)
    plane = lax.broadcasted_iota(jnp.int32, (24, 128), 0)
    cut = ((plane == 7) & (ends_ref[0] == 1)) | ((plane == 14) & (ends_ref[1] == 1))
    quarter = 0.25 * inverse

    def three(low, own, high):
        return jnp.concatenate([low, own, high], axis=0)

    for at in range(around):
        tan[at] = three(tan_low_ref[at], tan_ref[at], tan_high_ref[at]) * quarter
    for at in range(around):
        here = tan[at]
        up_a, down_a = tan[(at + 1) % around], tan[(at - 1) % around]
        up_r = jnp.where(lane == 127, 0.0, pltpu.roll(here, 127, 1))
        down_r = jnp.where(lane == 0, 0.0, pltpu.roll(here, 1, 1))
        up_x = pltpu.roll(here, 23, 0)
        down_x = pltpu.roll(here, 1, 0)
        found = three(found_low_ref[at], found_ref[at], found_high_ref[at])
        main[at] = (found - centre) * inverse + ((up_a + down_a) + (up_r + down_r) + (up_x + down_x))
        beyond = jnp.where(lane >= 126, 0.0, up_r)
        off_r[at] = beyond
        back_r[at] = pltpu.roll(beyond, 2, 1)
        beyond = jnp.where(cut, 0.0, up_x)
        off_x[at] = beyond
        back_x[at] = pltpu.roll(beyond, 2, 0)

    def apply(index, at):
        value = vectors[index, at]
        result = main[at] * value
        result = result - tan[(at + 1) % around] * vectors[index, (at + 2) % around]
        result = result - tan[(at - 1) % around] * vectors[index, (at - 2) % around]
        result = result - off_r[at] * pltpu.roll(value, 126, 1) - back_r[at] * pltpu.roll(value, 2, 1)
        return result - off_x[at] * pltpu.roll(value, 22, 0) - back_x[at] * pltpu.roll(value, 2, 0)

    for at in range(around):
        vectors[0, at] = three(seed_low_ref[at], seed_ref[at], seed_high_ref[at])
    for degree in range(1, HALF + 1):
        for at in range(around):
            value = apply(degree - 1, at)
            if degree > 1:
                value = value + value - vectors[degree - 2, at]
            vectors[degree, at] = value
    skipped = 1 if last else 0
    for index in range(skipped, HALF + 1):
        for at in range(around):
            own_ref[index - skipped, at] = vectors[index, at, 8:16, :]
    if not last:
        return
    total = 2 * HALF + 1
    column = lax.broadcasted_iota(jnp.int32, (1, 128), 1)
    gram = jnp.zeros((1, 128), F32)
    number = 0

    def own(index, at):
        return earlier_ref[index, at] if index <= HALF else own_ref[index - HALF - 1, at]

    for i in range(total):
        sums = [jnp.zeros((8, 128), F32)] * (total - i)
        for at in range(around):
            left = own(i, at)
            for j in range(i, total):
                sums[j - i] = sums[j - i] + left * own(j, at)
        for value in sums:
            entry = jnp.sum(jnp.sum(value, axis=0, keepdims=True), axis=1, keepdims=True)
            gram = jnp.where(column == number, jnp.broadcast_to(entry, (1, 128)), gram)
            number += 1
    gram_ref[...] = gram


def unpack_gram(all_ref, total):
    row = jnp.sum(all_ref[...], axis=0, keepdims=True)
    gram, number = {}, 0
    for i in range(total):
        for j in range(i, total):
            gram[i, j] = gram[j, i] = jnp.broadcast_to(row[:, number : number + 1], (1, 128))
            number += 1
    return gram


def dot(gram, left, right):
    total = len(left)
    result = None
    for i in range(total):
        if left[i] is None:
            continue
        inner = None
        for j in range(total):
            if right[j] is not None:
                term = gram[i, j] * right[j]
                inner = term if inner is None else inner + term
        if inner is not None:
            result = left[i] * inner if result is None else result + left[i] * inner
    return result


def axpy(scale, left, right):
    result = []
    for a, b in zip(left, right, strict=True):
        a = None if a is None else (a if scale is None else scale * a)
        result.append(b if a is None else (a if b is None else b + a))
    return result


def times_operator(vector, centre, half_width):
    total = len(vector)
    result = [None] * total
    half = 0.5 * half_width

    def add(index, term):
        result[index] = term if result[index] is None else result[index] + term

    for j, c in enumerate(vector):
        if c is None:
            continue
        add(j, centre * c)
        if j in (0, HALF):
            add(j + 1, half_width * c)
        else:
            add(j + 1, half * c)
            add(j - 1, half * c)
    return result


def iterate(gram, total, centre, half_width):
    residual = [jnp.ones((1, 128), F32)] + [None] * (total - 1)
    direction = residual
    change = [None] * total
    norms = [jnp.sqrt(gram[i, i]) for i in range(total)]
    current = gram[0, 0]
    worst = jnp.zeros((1, 128), F32)
    for step in range(ITERS):
        image = times_operator(direction, centre, half_width)
        alpha = current / dot(gram, direction, image)
        change = axpy(alpha, direction, change)
        residual = axpy(-alpha, image, residual)
        following = dot(gram, residual, residual)
        bound = None
        for c, n in zip(residual, norms, strict=True):
            if c is not None:
                bound = jnp.abs(c) * n if bound is None else bound + jnp.abs(c) * n
        worst = jnp.maximum(worst, bound * bound / following)
        worst = jnp.where(following > 0.0, worst, jnp.inf)
        if step < ITERS - 1:
            direction = axpy(following / current, direction, residual)
        current = following
    return change, residual, worst


def combine(coefficients, early_ref, late_ref, at):
    result = None
    for index, c in enumerate(coefficients):
        if c is not None:
            vector = early_ref[index, at] if index <= HALF else late_ref[index - HALF - 1, at]
            result = c * vector if result is None else result + c * vector
    return result


def last_kernel(around, scale_ref, all_ref, early_ref, late_ref, send_ref, worst_ref):
    total = 2 * HALF + 1
    change, residual, worst = iterate(unpack_gram(all_ref, total), total, scale_ref[0], scale_ref[2])
    worst_ref[...] = jnp.broadcast_to(worst, (8, 128))
    pairs = [[None if c is None else jnp.broadcast_to(c, (8, 128)) for c in part] for part in (change, residual)]
    for b in range(around // 8):
        for half in range(2):
            for number in range(2):
                tiles = [combine(pairs[number], early_ref, late_ref, 8 * b + 4 * half + a) for a in range(4)]
                tiles = regroup(tiles)
                for m in range(4):
                    send_ref[4 * b + m, 2 * number + half] = tiles[m]


def deliver_kernel(path, u_ref, recv_ref, updated_ref, residual_ref, turned):
    slab = lax.axis_index("slab")
    for source in range(recv_ref.shape[0]):
        start = pl.multiple_of(8 * place(slab, path[source], len(path)), 8)
        for index in range(4):
            turned[index, pl.ds(start, 8), :] = recv_ref[source, index]
    for half in range(2):
        part = slice(4 * half, 4 * half + 4)
        updated_ref[part] = u_ref[part] + jnp.transpose(turned[half]).reshape(4, 32, 128)
        residual_ref[part] = jnp.transpose(turned[2 + half]).reshape(4, 32, 128)


def sliced_body(
    displacement, load_field, foundation, plastic_flags, point_slot, family_in, family_mid, family_out, family_tan
):
    size_x, size_y, size_z = displacement.shape
    families = family_in.shape[0]
    along, across = lax.axis_size("blk"), lax.axis_size("micro")
    peers = along * across
    around = size_x * along
    everyone = peers * lax.axis_size("slab")
    slab = lax.axis_index("slab")
    path = [b * across + (m if b % 2 == 0 else across - 1 - m) for b in range(along) for m in range(across)]
    forth = jnp.array(path, jnp.int32)[lax.axis_index("blk") * across + lax.axis_index("micro")]
    mine = place(slab, forth, peers) + peers * slab
    ends = jnp.stack([(mine == 0), (mine == everyone - 1)]).astype(jnp.int32)
    spots = [0] * everyone
    for b in range(along):
        for s in range(2):
            for m in range(across):
                spots[place(s, path[b * across + m], peers) + peers * s] = (b * 2 + s) * across + m
    rising = [(spots[i], spots[i + 1]) for i in range(everyone - 1)]
    falling = [(b, a) for a, b in rising]

    def neighbours(to_next, to_previous):
        return lax.ppermute(to_next, AXES, rising), lax.ppermute(to_previous, AXES, falling)

    packed = pack_families(family_in, family_mid, family_out, family_tan)
    typical = 0.5 + 0.33 * jnp.mean(jnp.sum(family_tan, axis=1))
    centre = 1.1 + 1.4 * typical
    half_width = centre - 0.4
    scale = jnp.stack([centre, 1.0 / half_width, half_width])

    capacity = size_x * size_y * size_z // 2
    (send,) = call(
        lambda *refs: spread_kernel(path, capacity, *refs),
        [((peers, 8, 8, 128), F32)], [pltpu.VMEM((4, 2, 128, 128), F32)], "spread",
        displacement, load_field, foundation, point_slot, plastic_flags,
    )
    recv = lax.all_to_all(send, GROUP, 0, 0, tiled=True)
    field = (around, 8, 128)
    edge = (around // 8, 8, 128)
    message = (around + around // 8, 8, 128)
    strain, code, found, rest, to_next, to_previous = call(
        lambda *refs: collect_kernel(around, *refs),
        [((3,) + field, F32), (field, jnp.int32), (field, F32), (field, F32), (message, F32), (message, F32)],
        [pltpu.VMEM(field, F32)], "collect", recv,
    )
    low, high = neighbours(to_next, to_previous)
    first = cells(strain, code, packed, families, 8, (1, 2, 3))
    outer = cells(strain, code, packed, families, 8, (0, 7), low, high)
    edge_low, edge_high = neighbours(outer[2, :, 7].reshape(edge), outer[2, :, 0].reshape(edge))
    second = cells(strain, code, packed, families, 8, (4, 5, 6))
    (own,) = call(
        lambda *refs: rhs_kernel(around, *refs), [((2,) + field, F32)], [], "rhs",
        first, outer, second, rest, edge_low, edge_high,
    )
    own_low, own_high = neighbours(own, own)

    def basis(last, outputs, *vectors):
        return call(
            lambda *refs: basis_kernel(around, last, *refs), outputs,
            [pltpu.VMEM((around, 24, 128), F32)] * 6 + [pltpu.VMEM((HALF + 1, around, 24, 128), F32)],
            "basis", ends, scale, own[1], own_low[1], own_high[1], found, low, high, *vectors, smem=2,
        )

    (early,) = basis(False, [((HALF + 1,) + field, F32)], own[0], own_low[0], own_high[0])
    late, gram = basis(
        True, [((HALF,) + field, F32), ((1, 128), F32)], early[HALF], *neighbours(early[HALF], early[HALF]), early
    )
    sums = lax.all_to_all(jnp.broadcast_to(gram, (everyone, 128)), AXES, 0, 0, tiled=True)
    send, worst = call(
        lambda *refs: last_kernel(around, *refs),
        [((peers, 4, 8, 128), F32), ((8, 128), F32)], [], "last", scale, sums, early, late, smem=1,
    )
    recv = lax.all_to_all(send, GROUP, 0, 0, tiled=True)
    shape = displacement.shape
    updated, residual = call(
        lambda *refs: deliver_kernel(path, *refs),
        [(shape, F32), (shape, F32)], [pltpu.VMEM((4, 128, 128), F32)], "deliver", displacement, recv,
    )
    return updated, residual, worst[0, 0]


MOST_LOST = 1.0e5


def body(*inputs):
    size_x, size_y, size_z = inputs[0].shape
    along, across = lax.axis_size("blk"), lax.axis_size("micro")
    fits = (
        (size_x, size_y, size_z) == (8, 32, 128)
        and across == 4
        and size_z == 8 * along * across
        and lax.axis_size("slab") == 2
        and inputs[5].shape[0] == 4
    )
    if not fits:
        return plain_body(*inputs)
    updated, residual, worst = sliced_body(*inputs)
    return lax.cond(worst < MOST_LOST, lambda: (updated, residual), lambda: plain_body(*inputs))


def solution(mesh):
    field = P("blk", "micro", "slab")
    return jax.shard_map(
        body,
        mesh=mesh,
        in_specs=(field,) * 5 + (P(),) * 4,
        out_specs=(field, field),
        check_vma=False,
    )
```

```python
import jax
import jax.numpy as jnp
from jax import lax
from jax.experimental import pallas as pl
from jax.experimental.pallas import tpu as pltpu
from jax.sharding import PartitionSpec as P

ITERS = 8
AXES = ("blk", "slab", "micro")
BF = jnp.bfloat16
F32 = jnp.float32


def split(value):
    high = lax.reduce_precision(value, 8, 7)
    return high.astype(BF), (value - high).astype(BF)


def pack_families(family_in, family_mid, family_out, family_tan):
    families, _, modes = family_in.shape
    spread = jnp.transpose(family_in, (2, 1, 0))
    spread = jnp.concatenate([spread, spread], axis=2).reshape(modes, 6 * families)
    high, low = split(spread)
    weight_in = jnp.concatenate([high, low], axis=1)
    weight_mid = jnp.transpose(family_mid, (1, 0, 2)).reshape(modes, families * modes)
    none = jnp.zeros((families, 1, modes), BF)
    stress = jnp.concatenate([family_out, none], axis=1).reshape(4 * families, modes)
    none = jnp.zeros((families, 3, modes), BF)
    tan_high, tan_low = split(family_tan)
    tan_high = jnp.concatenate([none, tan_high[:, None]], axis=1).reshape(4 * families, modes)
    tan_low = jnp.concatenate([none, tan_low[:, None]], axis=1).reshape(4 * families, modes)
    weight_out = jnp.concatenate(
        [
            jnp.concatenate([stress, tan_high], axis=1),
            jnp.concatenate([jnp.zeros_like(stress), tan_low], axis=1),
        ],
        axis=0,
    )
    return weight_in, weight_mid, weight_out


def cells_kernel(families, planes, strain_ref, code_ref, in_ref, mid_ref, out_ref, *refs):
    *edges, answer_ref = refs
    modes = in_ref.shape[0]
    spots = [(a, x) for a in range(code_ref.shape[0]) for x in planes]
    width = len(spots) * 128
    place = lax.broadcasted_iota(jnp.int32, (2 * families, 128), 0)
    column, family_row, flag_row = [], [], []
    for a, x in spots:
        code = code_ref[a, pl.ds(x, 1), :]
        family = lax.shift_right_logical(code, 1)
        picked = lax.rem(place, families) == jnp.broadcast_to(family, place.shape)
        pieces = []
        for j in range(3):
            value = strain_ref[j, a, pl.ds(x, 1), :]
            if edges and j == 2:
                even, chip_ref, far_ref = edges
                chip, far = chip_ref[0, pl.ds(a, 1), :], far_ref[0, pl.ds(a, 1), :]
                beyond = jnp.where(even[...] == (1 if x == 7 else 0), chip, far) * 0.5
                value = value - beyond if x == 0 else value + beyond
            value = jnp.broadcast_to(value, place.shape)
            high = value.astype(BF).astype(F32)
            piece = jnp.where(place < families, high, value - high)
            pieces.append(jnp.where(picked, piece, 0.0))
        column.append(jnp.concatenate(pieces, axis=0))
        family_row.append(family)
        flag_row.append(lax.bitwise_and(code, 1))
    spread = jnp.concatenate(column, axis=1).astype(BF)
    spread = jnp.concatenate([spread, spread], axis=0)
    family = jnp.concatenate(family_row, axis=1)
    flag = jnp.concatenate(flag_row, axis=1)
    modal = jnp.dot(in_ref[...], spread, preferred_element_type=F32)
    flagged = jnp.broadcast_to(flag, (modes, width)) > 0
    active = jnp.where(flagged, jnp.tanh(modal), modal).astype(BF)
    wide = jnp.broadcast_to(family, (modes, width)).astype(BF)
    nothing = jnp.zeros_like(active)
    stacked = jnp.concatenate(
        [jnp.where(wide == jnp.array(f, BF), active, nothing) for f in range(families)], axis=0
    )
    hidden = jnp.dot(mid_ref[...], stacked, preferred_element_type=F32)
    bounded = jnp.tanh(hidden).astype(BF)
    both = jnp.concatenate([bounded, bounded * bounded], axis=0)
    result = jnp.dot(out_ref[...], both, preferred_element_type=F32)
    result = result[: 4 * families] + result[4 * families :]
    owner = lax.shift_right_logical(lax.broadcasted_iota(jnp.int32, (4 * families, width), 0), 2)
    result = jnp.where(owner == family, result, 0.0)
    total = result[:4]
    for f in range(1, families):
        total = total + result[4 * f : 4 * f + 4]
    for i, (a, x) in enumerate(spots):
        answer_ref[:, a, x, :] = total[:, i * 128 : (i + 1) * 128]


def cells(strain, code, packed, families, step, planes, *edges):
    weight_in, weight_mid, weight_out = packed
    count = code.shape[0]
    planes = tuple(planes)
    points = count * len(planes) * 128
    modes = weight_in.shape[0]

    def whole(array):
        return pl.BlockSpec(array.shape, lambda i: (0,) * array.ndim)

    def kernel(*refs):
        cells_kernel(families, planes, *refs)

    return pl.pallas_call(
        kernel,
        grid=(count // step,),
        in_specs=[
            pl.BlockSpec((3, step, 8, 128), lambda i: (0, i, 0, 0)),
            pl.BlockSpec((step, 8, 128), lambda i: (i, 0, 0)),
            whole(weight_in),
            whole(weight_mid),
            whole(weight_out),
        ]
        + [pl.BlockSpec((1, 128), lambda i: (0, 0)) for _ in edges[:1]]
        + [pl.BlockSpec((1, 8, 128), lambda i: (count + i, 0, 0)) for _ in edges[1:]],
        out_specs=pl.BlockSpec((4, step, 8, 128), lambda i: (0, i, 0, 0)),
        out_shape=jax.ShapeDtypeStruct((4, count, 8, 128), F32),
        compiler_params=pltpu.CompilerParams(vmem_limit_bytes=48 * 2**20),
        cost_estimate=pl.CostEstimate(
            flops=2 * points * modes * modes * (families + 1), bytes_accessed=points * 32, transcendentals=2 * points * modes
        ),
        name="cells",
    )(strain, code, weight_in, weight_mid, weight_out, *edges)


def global_sum(value):
    count = 1
    for axis in AXES:
        count = count * lax.axis_size(axis)
    spread = jnp.broadcast_to(value.reshape(1, 1), (count, 128))
    return jnp.sum(lax.all_to_all(spread, AXES, 0, 0, tiled=True)[:, 0])


def widened(cells_, axis, dim, width, closed):
    count = lax.axis_size(axis)
    ends = count if closed else count - 1
    head = lax.slice_in_dim(cells_, 0, width, axis=dim)
    tail = lax.slice_in_dim(cells_, cells_.shape[dim] - width, cells_.shape[dim], axis=dim)
    before = lax.ppermute(tail, axis, [(i, (i + 1) % count) for i in range(ends)])
    after = lax.ppermute(head, axis, [((i + 1) % count, i) for i in range(ends)])
    return jnp.concatenate([before, cells_, after], axis=dim)


HALOS = (("blk", True), ("micro", False), ("slab", False))


def widened_all(field, width):
    return [widened(field, axis, dim, width, closed) for dim, (axis, closed) in enumerate(HALOS)]


def difference(field, dim):
    length = field.shape[dim]
    return (lax.slice_in_dim(field, 2, length, axis=dim) - lax.slice_in_dim(field, 0, length - 2, axis=dim)) * 0.5


def plain_body(
    displacement, load_field, foundation, plastic_flags, point_slot, family_in, family_mid, family_out, family_tan
):
    size_x, size_y, size_z = displacement.shape
    points = size_x * size_y * size_z
    families = family_in.shape[0]
    capacity = points // 2
    packed = pack_families(family_in, family_mid, family_out, family_tan)
    strain = [difference(w, dim) for dim, w in enumerate(widened_all(displacement, 1))]
    code = 2 * (point_slot // capacity) + plastic_flags
    tiles = points // 1024
    answers = cells(jnp.stack(strain).reshape(3, tiles, 8, 128), code.reshape(tiles, 8, 128), packed, families, 2, range(8))
    answers = answers.reshape(4, size_x, size_y, size_z)
    tangents = widened_all(0.5 + answers[3], 1)
    divergence = sum(
        difference(widened(answers[dim], axis, dim, 1, closed), dim) for dim, (axis, closed) in enumerate(HALOS)
    )
    rhs = load_field - foundation * displacement + divergence
    solution_ = jnp.zeros_like(rhs)
    residual = rhs
    direction = rhs
    current = global_sum(jnp.sum(residual * residual))
    for _ in range(ITERS):
        total = sum(
            difference(tangents[dim] * difference(w, dim), dim) for dim, w in enumerate(widened_all(direction, 2))
        )
        image = foundation * direction - total
        alpha = current / global_sum(jnp.sum(direction * image))
        solution_ = solution_ + alpha * direction
        residual = residual - alpha * image
        following = global_sum(jnp.sum(residual * residual))
        direction = residual + following / current * direction
        current = following
    return displacement + solution_, residual


VMEM = pl.BlockSpec(memory_space=pltpu.VMEM)
GROUP = ("blk", "micro")


def call(kernel, out_shapes, scratch, name, *args):
    return pl.pallas_call(
        kernel,
        out_shape=[jax.ShapeDtypeStruct(shape, dtype) for shape, dtype in out_shapes],
        in_specs=[VMEM] * len(args),
        out_specs=[VMEM] * len(out_shapes),
        scratch_shapes=scratch,
        compiler_params=pltpu.CompilerParams(vmem_limit_bytes=40 * 2**20),
        name=name,
    )(*args)


def regroup(tiles):
    group = lax.broadcasted_iota(jnp.int32, (8, 128), 1) // 32
    result = []
    for a in range(4):
        tile = tiles[0]
        for m in range(4):
            shift = (m - a) * 32 % 128
            moved = pltpu.roll(tiles[m], shift, 1) if shift else tiles[m]
            tile = moved if m == 0 else jnp.where(group == m, moved, tile)
        result.append(tile)
    return result


def place(slab, position, peers):
    return position + slab * (peers - 1 - 2 * position)


def whereabouts(peers):
    across = lax.axis_size("micro")
    b, m, slab = lax.axis_index("blk"), lax.axis_index("micro"), lax.axis_index("slab")
    position = place(slab, b * across + jnp.where(b % 2 == 0, m, across - 1 - m), peers)
    return (slab == 0) & (position == 0), (slab == 1) & (position == peers - 1), position % 2 == 0


def spread_kernel(path, capacity, u_ref, load_ref, found_ref, slot_ref, flag_ref, send_ref, turned):
    peers = len(path)
    slab = lax.axis_index("slab")
    code = jnp.zeros(slot_ref.shape, jnp.int32)
    for family in range(1, 4):
        code = code + jnp.where(slot_ref[...] >= family * capacity, 2, 0)
    rest = load_ref[...] - found_ref[...] * u_ref[...]
    fields = (u_ref[...], (code + flag_ref[...]).astype(F32), found_ref[...], rest)
    for number, field in enumerate(fields):
        for half in range(2):
            turned[number, half] = jnp.transpose(field[4 * half : 4 * half + 4].reshape(128, 128))
    for target in range(peers):
        start = pl.multiple_of(8 * place(slab, path[target], peers), 8)
        for number in range(4):
            for half in range(2):
                send_ref[target, 2 * number + half] = turned[number, half, pl.ds(start, 8), :]


def beside(tile, low, high):
    row = lax.broadcasted_iota(jnp.int32, (8, 128), 0)
    after = jnp.where(row == 7, jnp.broadcast_to(high, (8, 128)), pltpu.roll(tile, 7, 0))
    before = jnp.where(row == 0, jnp.broadcast_to(low, (8, 128)), pltpu.roll(tile, 1, 0))
    return after, before


def radial(tile):
    lane = lax.broadcasted_iota(jnp.int32, tile.shape, tile.ndim - 1)
    after = jnp.where(lane == 127, 0.0, pltpu.roll(tile, 127, tile.ndim - 1))
    before = jnp.where(lane == 0, 0.0, pltpu.roll(tile, 1, tile.ndim - 1))
    return (after - before) * 0.5


def collect_kernel(around, recv_ref, strain_ref, code_ref, found_ref, rest_ref, chip_ref, far_ref, u):
    _, _, even = whereabouts(recv_ref.shape[0])
    for b in range(around // 8):
        for half in range(2):
            for number in range(4):
                tiles = regroup([recv_ref[4 * b + m, 2 * number + half] for m in range(4)])
                for a in range(4):
                    at = 8 * b + 4 * half + a
                    if number == 0:
                        u[at] = tiles[a]
                    elif number == 1:
                        code_ref[at] = tiles[a].astype(jnp.int32)
                    elif number == 2:
                        found_ref[at] = tiles[a]
                        chip_ref[at] = tiles[a]
                        far_ref[at] = tiles[a]
                    else:
                        rest_ref[at] = tiles[a]
    nothing = jnp.zeros((1, 128), F32)
    for at in range(around):
        tile = u[at]
        strain_ref[0, at] = (u[(at + 1) % around] - u[(at - 1) % around]) * 0.5
        strain_ref[1, at] = radial(tile)
        after, before = beside(tile, nothing, nothing)
        strain_ref[2, at] = (after - before) * 0.5
        chip_ref[around + at // 8, pl.ds(at % 8, 1), :] = tile[7:8]
        far_ref[around + at // 8, pl.ds(at % 8, 1), :] = tile[0:1]
    for index in range(around, around + around // 8):
        bottom, top = far_ref[index], chip_ref[index]
        chip_ref[index] = jnp.where(even, top, bottom)
        far_ref[index] = jnp.where(even, bottom, top)


def rhs_kernel(around, peers, first_ref, outer_ref, second_ref, rest_ref, chip_ref, far_ref, own_ref, low_ref, high_ref):
    _, _, even = whereabouts(peers)
    for index in range(around // 8):
        low_ref[index] = jnp.where(even, far_ref[index], chip_ref[index])
        high_ref[index] = jnp.where(even, chip_ref[index], far_ref[index])
    row = lax.broadcasted_iota(jnp.int32, (8, 128), 0)
    rim = (row == 0) | (row == 7)

    def answer(number, at):
        inner = jnp.where(row < 4, first_ref[number, at], second_ref[number, at])
        return jnp.where(rim, outer_ref[number, at], inner)

    cycle = [answer(0, at) for at in range(around)]
    for at in range(around):
        low = low_ref[at // 8, pl.ds(at % 8, 1), :]
        high = high_ref[at // 8, pl.ds(at % 8, 1), :]
        after, before = beside(answer(2, at), low, high)
        divergence = (cycle[(at + 1) % around] - cycle[(at - 1) % around]) * 0.5
        divergence = divergence + radial(answer(1, at)) + (after - before) * 0.5
        own_ref[0, at] = rest_ref[at] + divergence
        own_ref[1, at] = 0.5 + answer(3, at)


HALF = ITERS // 2
MOST_LOST = 1.0e5


def basis_kernel(
    around, peers, last, scale_ref, tan_ref, tan_chip_ref, tan_far_ref, found_ref, found_chip_ref, found_far_ref,
    seed_ref, seed_chip_ref, seed_far_ref, *refs
):
    if last:
        earlier_ref, own_ref, gram_ref, *scratch = refs
    else:
        own_ref, *scratch = refs
    tan, main, off_r, back_r, off_x, back_x, vectors = scratch
    centre, inverse = scale_ref[0:1, :], scale_ref[1:2, :]
    is_first, is_last, even = whereabouts(peers)
    lane = lax.broadcasted_iota(jnp.int32, (24, 128), 1)
    plane = lax.broadcasted_iota(jnp.int32, (24, 128), 0)
    cut = ((plane == 7) & is_first) | ((plane == 14) & is_last)
    quarter = 0.25 * inverse

    def three(own, chip, far):
        return jnp.concatenate([jnp.where(even, far, chip), own, jnp.where(even, chip, far)], axis=0)

    for at in range(around):
        tan[at] = three(tan_ref[at], tan_chip_ref[at], tan_far_ref[at]) * quarter
    for at in range(around):
        here = tan[at]
        up_a, down_a = tan[(at + 1) % around], tan[(at - 1) % around]
        up_r = jnp.where(lane == 127, 0.0, pltpu.roll(here, 127, 1))
        down_r = jnp.where(lane == 0, 0.0, pltpu.roll(here, 1, 1))
        up_x = pltpu.roll(here, 23, 0)
        down_x = pltpu.roll(here, 1, 0)
        found = three(found_ref[at], found_chip_ref[at], found_far_ref[at])
        main[at] = (found - centre) * inverse + ((up_a + down_a) + (up_r + down_r) + (up_x + down_x))
        beyond = jnp.where(lane >= 126, 0.0, up_r)
        off_r[at] = beyond
        back_r[at] = pltpu.roll(beyond, 2, 1)
        beyond = jnp.where(cut, 0.0, up_x)
        off_x[at] = beyond
        back_x[at] = pltpu.roll(beyond, 2, 0)

    def apply(index, at):
        value = vectors[index, at]
        result = main[at] * value
        result = result - tan[(at + 1) % around] * vectors[index, (at + 2) % around]
        result = result - tan[(at - 1) % around] * vectors[index, (at - 2) % around]
        result = result - off_r[at] * pltpu.roll(value, 126, 1) - back_r[at] * pltpu.roll(value, 2, 1)
        return result - off_x[at] * pltpu.roll(value, 22, 0) - back_x[at] * pltpu.roll(value, 2, 0)

    for at in range(around):
        vectors[0, at] = three(seed_ref[at], seed_chip_ref[at], seed_far_ref[at])
    for degree in range(1, HALF + 1):
        for at in range(around):
            value = apply(degree - 1, at)
            if degree > 1:
                value = value + value - vectors[degree - 2, at]
            vectors[degree, at] = value
    skipped = 1 if last else 0
    for index in range(skipped, HALF + 1):
        for at in range(around):
            own_ref[index - skipped, at] = vectors[index, at, 8:16, :]
    if not last:
        return
    total = 2 * HALF + 1
    column = lax.broadcasted_iota(jnp.int32, (1, 128), 1)
    gram = jnp.zeros((1, 128), F32)
    number = 0

    def own(index, at):
        return earlier_ref[index, at] if index <= HALF else own_ref[index - HALF - 1, at]

    for i in range(total):
        sums = [jnp.zeros((8, 128), F32)] * (total - i)
        for at in range(around):
            left = own(i, at)
            for j in range(i, total):
                sums[j - i] = sums[j - i] + left * own(j, at)
        for value in sums:
            entry = jnp.sum(jnp.sum(value, axis=0, keepdims=True), axis=1, keepdims=True)
            gram = jnp.where(column == number, jnp.broadcast_to(entry, (1, 128)), gram)
            number += 1
    gram_ref[...] = jnp.broadcast_to(gram, gram_ref.shape)


def unpack_gram(all_ref, total):
    row = jnp.sum(all_ref[...], axis=0, keepdims=True)
    gram, number = {}, 0
    for i in range(total):
        for j in range(i, total):
            gram[i, j] = gram[j, i] = jnp.broadcast_to(row[:, number : number + 1], (1, 128))
            number += 1
    return gram


def dot(gram, left, right):
    total = len(left)
    result = None
    for i in range(total):
        if left[i] is None:
            continue
        inner = None
        for j in range(total):
            if right[j] is not None:
                term = gram[i, j] * right[j]
                inner = term if inner is None else inner + term
        if inner is not None:
            result = left[i] * inner if result is None else result + left[i] * inner
    return result


def axpy(scale, left, right):
    result = []
    for a, b in zip(left, right, strict=True):
        a = None if a is None else (a if scale is None else scale * a)
        result.append(b if a is None else (a if b is None else b + a))
    return result


def times_operator(vector, centre, half_width):
    total = len(vector)
    result = [None] * total
    half = 0.5 * half_width

    def add(index, term):
        result[index] = term if result[index] is None else result[index] + term

    for j, c in enumerate(vector):
        if c is None:
            continue
        add(j, centre * c)
        if j in (0, HALF):
            add(j + 1, half_width * c)
        else:
            add(j + 1, half * c)
            add(j - 1, half * c)
    return result


def iterate(gram, total, centre, half_width):
    residual = [jnp.ones((1, 128), F32)] + [None] * (total - 1)
    direction = residual
    change = [None] * total
    norms = [jnp.sqrt(gram[i, i]) for i in range(total)]
    current = gram[0, 0]
    worst = jnp.zeros((1, 128), F32)
    for step in range(ITERS):
        image = times_operator(direction, centre, half_width)
        alpha = current / dot(gram, direction, image)
        change = axpy(alpha, direction, change)
        residual = axpy(-alpha, image, residual)
        following = dot(gram, residual, residual)
        bound = None
        for c, n in zip(residual, norms, strict=True):
            if c is not None:
                bound = jnp.abs(c) * n if bound is None else bound + jnp.abs(c) * n
        worst = jnp.maximum(worst, bound * bound / following)
        worst = jnp.where(following > 0.0, worst, jnp.inf)
        if step < ITERS - 1:
            direction = axpy(following / current, direction, residual)
        current = following
    return change, residual, worst


def combine(coefficients, early_ref, late_ref, at):
    result = None
    for index, c in enumerate(coefficients):
        if c is not None:
            vector = early_ref[index, at] if index <= HALF else late_ref[index - HALF - 1, at]
            result = c * vector if result is None else result + c * vector
    return result


def last_kernel(around, scale_ref, all_ref, early_ref, late_ref, send_ref, worst_ref):
    total = 2 * HALF + 1
    change, residual, worst = iterate(unpack_gram(all_ref, total), total, scale_ref[0:1, :], scale_ref[2:3, :])
    worst_ref[...] = jnp.broadcast_to(worst, (8, 128))
    pairs = [[None if c is None else jnp.broadcast_to(c, (8, 128)) for c in part] for part in (change, residual)]
    for b in range(around // 8):
        for half in range(2):
            for number in range(2):
                tiles = [combine(pairs[number], early_ref, late_ref, 8 * b + 4 * half + a) for a in range(4)]
                tiles = regroup(tiles)
                for m in range(4):
                    send_ref[4 * b + m, 2 * number + half] = tiles[m]


def deliver_kernel(path, u_ref, recv_ref, worst_ref, instead_updated_ref, instead_residual_ref, *refs):
    updated_ref, residual_ref, turned = refs
    slab = lax.axis_index("slab")
    for source in range(recv_ref.shape[0]):
        start = pl.multiple_of(8 * place(slab, path[source], len(path)), 8)
        for index in range(4):
            turned[index, pl.ds(start, 8), :] = recv_ref[source, index]
    good = jnp.broadcast_to(worst_ref[0:1, :] < MOST_LOST, (32, 128))
    for half in range(2):
        change = jnp.transpose(turned[half]).reshape(4, 32, 128)
        residual = jnp.transpose(turned[2 + half]).reshape(4, 32, 128)
        for i in range(4):
            at = 4 * half + i
            updated_ref[at] = jnp.where(good, u_ref[at] + change[i], instead_updated_ref[at])
            residual_ref[at] = jnp.where(good, residual[i], instead_residual_ref[at])


def sliced_body(
    displacement, load_field, foundation, plastic_flags, point_slot, family_in, family_mid, family_out, family_tan
):
    size_x, size_y, size_z = displacement.shape
    families = family_in.shape[0]
    along, across = lax.axis_size("blk"), lax.axis_size("micro")
    peers = along * across
    around = size_x * along
    everyone = peers * lax.axis_size("slab")
    path = [b * across + (m if b % 2 == 0 else across - 1 - m) for b in range(along) for m in range(across)]
    _, _, even = whereabouts(peers)
    spots = [0] * everyone
    for b in range(along):
        for s in range(2):
            for m in range(across):
                spots[place(s, path[b * across + m], peers) + peers * s] = (b * 2 + s) * across + m

    def swap(first, value):
        pairs = [(spots[i], spots[i + 1]) for i in range(first, everyone - 1, 2)]
        return lax.ppermute(value, AXES, pairs + [(b, a) for a, b in pairs])

    def neighbours(to_chip, to_far):
        return swap(0, to_chip), swap(1, to_far)

    packed = pack_families(family_in, family_mid, family_out, family_tan)
    typical = 0.5 + 0.33 * jnp.mean(jnp.sum(family_tan, axis=1))
    centre = 1.1 + 1.4 * typical
    half_width = centre - 0.4
    scale = jnp.broadcast_to(jnp.stack([centre, 1.0 / half_width, half_width] + [centre] * 5)[:, None], (8, 128))

    capacity = size_x * size_y * size_z // 2
    (send,) = call(
        lambda *refs: spread_kernel(path, capacity, *refs),
        [((peers, 8, 8, 128), F32)], [pltpu.VMEM((4, 2, 128, 128), F32)], "spread",
        displacement, load_field, foundation, point_slot, plastic_flags,
    )
    recv = lax.all_to_all(send, GROUP, 0, 0, tiled=True)
    field = (around, 8, 128)
    edge = (around // 8, 8, 128)
    message = (around + around // 8, 8, 128)
    strain, code, found, rest, to_chip, to_far = call(
        lambda *refs: collect_kernel(around, *refs),
        [((3,) + field, F32), (field, jnp.int32), (field, F32), (field, F32), (message, F32), (message, F32)],
        [pltpu.VMEM(field, F32)], "collect", recv,
    )
    chip, far = neighbours(to_chip, to_far)
    first = cells(strain, code, packed, families, 8, (1, 2, 3))
    outer = cells(strain, code, packed, families, 8, (0, 7), jnp.broadcast_to(even.astype(jnp.int32), (1, 128)), chip, far)
    top, bottom = outer[2, :, 7].reshape(edge), outer[2, :, 0].reshape(edge)
    edge_chip, edge_far = neighbours(jnp.where(even, top, bottom), jnp.where(even, bottom, top))
    second = cells(strain, code, packed, families, 8, (4, 5, 6))
    (own,) = call(
        lambda *refs: rhs_kernel(around, peers, *refs), [((2,) + field, F32)], [pltpu.VMEM(edge, F32)] * 2, "rhs",
        first, outer, second, rest, edge_chip, edge_far,
    )
    own_chip, own_far = neighbours(own, own)

    def basis(last, outputs, *vectors):
        return call(
            lambda *refs: basis_kernel(around, peers, last, *refs), outputs,
            [pltpu.VMEM((around, 24, 128), F32)] * 6 + [pltpu.VMEM((HALF + 1, around, 24, 128), F32)],
            "basis", scale, own[1], own_chip[1], own_far[1], found, chip, far, *vectors,
        )

    (early,) = basis(False, [((HALF + 1,) + field, F32)], own[0], own_chip[0], own_far[0])
    late, gram = basis(
        True, [((HALF,) + field, F32), ((everyone, 128), F32)], early[HALF], *neighbours(early[HALF], early[HALF]), early
    )
    sums = lax.all_to_all(gram, AXES, 0, 0, tiled=True)
    send, worst = call(
        lambda *refs: last_kernel(around, *refs),
        [((peers, 4, 8, 128), F32), ((8, 128), F32)], [], "last", scale, sums, early, late,
    )
    recv = lax.all_to_all(send, GROUP, 0, 0, tiled=True)
    inputs = (
        displacement, load_field, foundation, plastic_flags, point_slot, family_in, family_mid, family_out, family_tan
    )
    good, recv = lax.optimization_barrier((worst[0, 0] < MOST_LOST, recv))
    instead = lax.cond(good, lambda: (jnp.zeros_like(displacement),) * 2, lambda: plain_body(*inputs))
    shape = displacement.shape
    return call(
        lambda *refs: deliver_kernel(path, *refs), [(shape, F32), (shape, F32)], [pltpu.VMEM((4, 128, 128), F32)],
        "deliver", displacement, recv, worst, *instead,
    )


def body(*inputs):
    size_x, size_y, size_z = inputs[0].shape
    along, across = lax.axis_size("blk"), lax.axis_size("micro")
    fits = (
        (size_x, size_y, size_z) == (8, 32, 128)
        and across == 4
        and size_z == 8 * along * across
        and lax.axis_size("slab") == 2
        and inputs[5].shape[0] == 4
    )
    if not fits:
        return plain_body(*inputs)
    return tuple(sliced_body(*inputs))


def solution(mesh):
    field = P("blk", "micro", "slab")
    return jax.shard_map(
        body,
        mesh=mesh,
        in_specs=(field,) * 5 + (P(),) * 4,
        out_specs=(field, field),
        check_vma=False,
    )
```

```python
import jax
import jax.numpy as jnp
from jax import lax
from jax.experimental import pallas as pl
from jax.experimental.pallas import tpu as pltpu
from jax.sharding import PartitionSpec as P

ITERS = 8
AXES = ("blk", "slab", "micro")
BF = jnp.bfloat16
F32 = jnp.float32


def split(value):
    high = lax.reduce_precision(value, 8, 7)
    return high.astype(BF), (value - high).astype(BF)


def pack_families(family_in, family_mid, family_out, family_tan):
    families, _, modes = family_in.shape
    spread = jnp.transpose(family_in, (2, 1, 0))
    spread = jnp.concatenate([spread, spread], axis=2).reshape(modes, 6 * families)
    high, low = split(spread)
    weight_in = jnp.concatenate([high, low], axis=1)
    weight_mid = jnp.transpose(family_mid, (1, 0, 2)).reshape(modes, families * modes)
    none = jnp.zeros((families, 1, modes), BF)
    stress = jnp.concatenate([family_out, none], axis=1).reshape(4 * families, modes)
    none = jnp.zeros((families, 3, modes), BF)
    tan_high, tan_low = split(family_tan)
    tan_high = jnp.concatenate([none, tan_high[:, None]], axis=1).reshape(4 * families, modes)
    tan_low = jnp.concatenate([none, tan_low[:, None]], axis=1).reshape(4 * families, modes)
    weight_out = jnp.concatenate(
        [
            jnp.concatenate([stress, tan_high], axis=1),
            jnp.concatenate([jnp.zeros_like(stress), tan_low], axis=1),
        ],
        axis=0,
    )
    return weight_in, weight_mid, weight_out


def cells_kernel(families, planes, strain_ref, code_ref, in_ref, mid_ref, out_ref, *refs):
    *edges, answer_ref = refs
    modes = in_ref.shape[0]
    spots = [(a, x) for a in range(code_ref.shape[0]) for x in planes]
    width = len(spots) * 128
    place = lax.broadcasted_iota(jnp.int32, (2 * families, 128), 0)
    column, family_row, flag_row = [], [], []
    for a, x in spots:
        code = code_ref[a, pl.ds(x, 1), :]
        family = lax.shift_right_logical(code, 1)
        picked = lax.rem(place, families) == jnp.broadcast_to(family, place.shape)
        pieces = []
        for j in range(3):
            value = strain_ref[j, a, pl.ds(x, 1), :]
            if edges and j == 2:
                even, chip_ref, far_ref = edges
                chip, far = chip_ref[0, pl.ds(a, 1), :], far_ref[0, pl.ds(a, 1), :]
                beyond = jnp.where(even[...] == (1 if x == 7 else 0), chip, far) * 0.5
                value = value - beyond if x == 0 else value + beyond
            value = jnp.broadcast_to(value, place.shape)
            high = value.astype(BF).astype(F32)
            piece = jnp.where(place < families, high, value - high)
            pieces.append(jnp.where(picked, piece, 0.0))
        column.append(jnp.concatenate(pieces, axis=0))
        family_row.append(family)
        flag_row.append(lax.bitwise_and(code, 1))
    spread = jnp.concatenate(column, axis=1).astype(BF)
    spread = jnp.concatenate([spread, spread], axis=0)
    family = jnp.concatenate(family_row, axis=1)
    flag = jnp.concatenate(flag_row, axis=1)
    modal = jnp.dot(in_ref[...], spread, preferred_element_type=F32)
    flagged = jnp.broadcast_to(flag, (modes, width)) > 0
    active = jnp.where(flagged, jnp.tanh(modal), modal).astype(BF)
    wide = jnp.broadcast_to(family, (modes, width)).astype(BF)
    nothing = jnp.zeros_like(active)
    stacked = jnp.concatenate(
        [jnp.where(wide == jnp.array(f, BF), active, nothing) for f in range(families)], axis=0
    )
    hidden = jnp.dot(mid_ref[...], stacked, preferred_element_type=F32)
    bounded = jnp.tanh(hidden).astype(BF)
    both = jnp.concatenate([bounded, bounded * bounded], axis=0)
    result = jnp.dot(out_ref[...], both, preferred_element_type=F32)
    result = result[: 4 * families] + result[4 * families :]
    owner = lax.shift_right_logical(lax.broadcasted_iota(jnp.int32, (4 * families, width), 0), 2)
    result = jnp.where(owner == family, result, 0.0)
    total = result[:4]
    for f in range(1, families):
        total = total + result[4 * f : 4 * f + 4]
    for i, (a, x) in enumerate(spots):
        answer_ref[:, a, x, :] = total[:, i * 128 : (i + 1) * 128]


def cells(strain, code, packed, families, step, planes, *edges):
    weight_in, weight_mid, weight_out = packed
    count = code.shape[0]
    planes = tuple(planes)
    points = count * len(planes) * 128
    modes = weight_in.shape[0]

    def whole(array):
        return pl.BlockSpec(array.shape, lambda i: (0,) * array.ndim)

    def kernel(*refs):
        cells_kernel(families, planes, *refs)

    return pl.pallas_call(
        kernel,
        grid=(count // step,),
        in_specs=[
            pl.BlockSpec((3, step, 8, 128), lambda i: (0, i, 0, 0)),
            pl.BlockSpec((step, 8, 128), lambda i: (i, 0, 0)),
            whole(weight_in),
            whole(weight_mid),
            whole(weight_out),
        ]
        + [pl.BlockSpec((1, 128), lambda i: (0, 0)) for _ in edges[:1]]
        + [pl.BlockSpec((1, 8, 128), lambda i: (count + i, 0, 0)) for _ in edges[1:]],
        out_specs=pl.BlockSpec((4, step, 8, 128), lambda i: (0, i, 0, 0)),
        out_shape=jax.ShapeDtypeStruct((4, count, 8, 128), F32),
        compiler_params=pltpu.CompilerParams(vmem_limit_bytes=48 * 2**20),
        cost_estimate=pl.CostEstimate(
            flops=2 * points * modes * modes * (families + 1), bytes_accessed=points * 32, transcendentals=2 * points * modes
        ),
        name="cells",
    )(strain, code, weight_in, weight_mid, weight_out, *edges)


def global_sum(value):
    count = 1
    for axis in AXES:
        count = count * lax.axis_size(axis)
    spread = jnp.broadcast_to(value.reshape(1, 1), (count, 128))
    return jnp.sum(lax.all_to_all(spread, AXES, 0, 0, tiled=True)[:, 0])


def widened(cells_, axis, dim, width, closed):
    count = lax.axis_size(axis)
    ends = count if closed else count - 1
    head = lax.slice_in_dim(cells_, 0, width, axis=dim)
    tail = lax.slice_in_dim(cells_, cells_.shape[dim] - width, cells_.shape[dim], axis=dim)
    before = lax.ppermute(tail, axis, [(i, (i + 1) % count) for i in range(ends)])
    after = lax.ppermute(head, axis, [((i + 1) % count, i) for i in range(ends)])
    return jnp.concatenate([before, cells_, after], axis=dim)


HALOS = (("blk", True), ("micro", False), ("slab", False))


def widened_all(field, width):
    return [widened(field, axis, dim, width, closed) for dim, (axis, closed) in enumerate(HALOS)]


def difference(field, dim):
    length = field.shape[dim]
    return (lax.slice_in_dim(field, 2, length, axis=dim) - lax.slice_in_dim(field, 0, length - 2, axis=dim)) * 0.5


def plain_body(
    displacement, load_field, foundation, plastic_flags, point_slot, family_in, family_mid, family_out, family_tan
):
    size_x, size_y, size_z = displacement.shape
    points = size_x * size_y * size_z
    families = family_in.shape[0]
    capacity = points // 2
    packed = pack_families(family_in, family_mid, family_out, family_tan)
    strain = [difference(w, dim) for dim, w in enumerate(widened_all(displacement, 1))]
    code = 2 * (point_slot // capacity) + plastic_flags
    tiles = points // 1024
    answers = cells(jnp.stack(strain).reshape(3, tiles, 8, 128), code.reshape(tiles, 8, 128), packed, families, 2, range(8))
    answers = answers.reshape(4, size_x, size_y, size_z)
    tangents = widened_all(0.5 + answers[3], 1)
    divergence = sum(
        difference(widened(answers[dim], axis, dim, 1, closed), dim) for dim, (axis, closed) in enumerate(HALOS)
    )
    rhs = load_field - foundation * displacement + divergence
    solution_ = jnp.zeros_like(rhs)
    residual = rhs
    direction = rhs
    current = global_sum(jnp.sum(residual * residual))
    for _ in range(ITERS):
        total = sum(
            difference(tangents[dim] * difference(w, dim), dim) for dim, w in enumerate(widened_all(direction, 2))
        )
        image = foundation * direction - total
        alpha = current / global_sum(jnp.sum(direction * image))
        solution_ = solution_ + alpha * direction
        residual = residual - alpha * image
        following = global_sum(jnp.sum(residual * residual))
        direction = residual + following / current * direction
        current = following
    return displacement + solution_, residual


VMEM = pl.BlockSpec(memory_space=pltpu.VMEM)
GROUP = ("blk", "micro")


def call(kernel, out_shapes, scratch, name, *args, grid=(), ins=None, outs=None):
    return pl.pallas_call(
        kernel,
        out_shape=[jax.ShapeDtypeStruct(shape, dtype) for shape, dtype in out_shapes],
        grid=grid,
        in_specs=ins or [VMEM] * len(args),
        out_specs=outs or [VMEM] * len(out_shapes),
        scratch_shapes=scratch,
        compiler_params=pltpu.CompilerParams(vmem_limit_bytes=40 * 2**20),
        name=name,
    )(*args)


def regroup(tiles):
    group = lax.broadcasted_iota(jnp.int32, (8, 128), 1) // 32
    result = []
    for a in range(4):
        tile = tiles[0]
        for m in range(4):
            shift = (m - a) * 32 % 128
            moved = pltpu.roll(tiles[m], shift, 1) if shift else tiles[m]
            tile = moved if m == 0 else jnp.where(group == m, moved, tile)
        result.append(tile)
    return result


def place(slab, position, peers):
    return position + slab * (peers - 1 - 2 * position)


def whereabouts(peers):
    across = lax.axis_size("micro")
    b, m, slab = lax.axis_index("blk"), lax.axis_index("micro"), lax.axis_index("slab")
    position = place(slab, b * across + jnp.where(b % 2 == 0, m, across - 1 - m), peers)
    return (slab == 0) & (position == 0), (slab == 1) & (position == peers - 1), position % 2 == 0


def spread_kernel(path, capacity, u_ref, load_ref, found_ref, slot_ref, flag_ref, send_ref, turned):
    peers = len(path)
    slab = lax.axis_index("slab")
    code = flag_ref[...]
    for family in range(1, 4):
        code = code + jnp.where(slot_ref[...] >= family * capacity, 2, 0)
    rest = load_ref[...] - found_ref[...] * u_ref[...]
    for number, value in enumerate((u_ref[...], code.astype(F32), found_ref[...], rest)):
        turned[number] = jnp.transpose(value.reshape(128, 128))
    for target in range(peers):
        start = pl.multiple_of(8 * place(slab, path[target], peers), 8)
        for number in range(4):
            send_ref[target, 0, number] = turned[number, pl.ds(start, 8), :]


def beside(tile, low, high):
    row = lax.broadcasted_iota(jnp.int32, (8, 128), 0)
    after = jnp.where(row == 7, jnp.broadcast_to(high, (8, 128)), pltpu.roll(tile, 7, 0))
    before = jnp.where(row == 0, jnp.broadcast_to(low, (8, 128)), pltpu.roll(tile, 1, 0))
    return after, before


def radial(tile):
    lane = lax.broadcasted_iota(jnp.int32, tile.shape, tile.ndim - 1)
    after = jnp.where(lane == 127, 0.0, pltpu.roll(tile, 127, tile.ndim - 1))
    before = jnp.where(lane == 0, 0.0, pltpu.roll(tile, 1, tile.ndim - 1))
    return (after - before) * 0.5


def collect_kernel(around, tan_ref, recv_ref, strain_ref, code_ref, found_ref, rest_ref, chip_ref, far_ref, scale_ref, u):
    _, _, even = whereabouts(recv_ref.shape[0])
    typical = jnp.sum(jnp.sum(tan_ref[...], axis=1, keepdims=True), axis=0, keepdims=True) / tan_ref.shape[0]
    centre = jnp.broadcast_to(1.1 + 1.4 * (0.5 + 0.33 * typical), (8, 128))
    row = lax.broadcasted_iota(jnp.int32, (8, 128), 0)
    scale_ref[...] = jnp.where(row == 0, centre, jnp.where(row == 1, 1.0 / (centre - 0.4), centre - 0.4))
    for b in range(around // 8):
        for half in range(2):
            for number in range(4):
                tiles = regroup([recv_ref[4 * b + m, half, number] for m in range(4)])
                for a in range(4):
                    at = 8 * b + 4 * half + a
                    if number == 0:
                        u[at] = tiles[a]
                    elif number == 1:
                        code_ref[at] = tiles[a].astype(jnp.int32)
                    elif number == 2:
                        found_ref[at] = tiles[a]
                        chip_ref[at] = tiles[a]
                        far_ref[at] = tiles[a]
                    else:
                        rest_ref[at] = tiles[a]
    nothing = jnp.zeros((1, 128), F32)
    for at in range(around):
        tile = u[at]
        strain_ref[0, at] = (u[(at + 1) % around] - u[(at - 1) % around]) * 0.5
        strain_ref[1, at] = radial(tile)
        after, before = beside(tile, nothing, nothing)
        strain_ref[2, at] = (after - before) * 0.5
        chip_ref[around + at // 8, pl.ds(at % 8, 1), :] = tile[7:8]
        far_ref[around + at // 8, pl.ds(at % 8, 1), :] = tile[0:1]
    for index in range(around, around + around // 8):
        bottom, top = far_ref[index], chip_ref[index]
        chip_ref[index] = jnp.where(even, top, bottom)
        far_ref[index] = jnp.where(even, bottom, top)


def rhs_kernel(around, peers, first_ref, outer_ref, second_ref, rest_ref, chip_ref, far_ref, own_ref, low_ref, high_ref):
    _, _, even = whereabouts(peers)
    for index in range(around // 8):
        low_ref[index] = jnp.where(even, far_ref[index], chip_ref[index])
        high_ref[index] = jnp.where(even, chip_ref[index], far_ref[index])
    row = lax.broadcasted_iota(jnp.int32, (8, 128), 0)
    rim = (row == 0) | (row == 7)

    def answer(number, at):
        inner = jnp.where(row < 4, first_ref[number, at], second_ref[number, at])
        return jnp.where(rim, outer_ref[number, at], inner)

    cycle = [answer(0, at) for at in range(around)]
    for at in range(around):
        low = low_ref[at // 8, pl.ds(at % 8, 1), :]
        high = high_ref[at // 8, pl.ds(at % 8, 1), :]
        after, before = beside(answer(2, at), low, high)
        divergence = (cycle[(at + 1) % around] - cycle[(at - 1) % around]) * 0.5
        divergence = divergence + radial(answer(1, at)) + (after - before) * 0.5
        own_ref[0, at] = rest_ref[at] + divergence
        own_ref[1, at] = 0.5 + answer(3, at)


HALF = ITERS // 2
MOST_LOST = 1.0e5


def basis_kernel(
    around, peers, last, scale_ref, tan_ref, tan_chip_ref, tan_far_ref, found_ref, found_chip_ref, found_far_ref,
    seed_ref, seed_chip_ref, seed_far_ref, *refs
):
    if last:
        earlier_ref, previous_ref, own_ref, sums_ref, *scratch = refs
    else:
        own_ref, sums_ref, *scratch = refs
    tan, main, off_r, back_r, off_x, back_x, vectors = scratch
    centre, inverse = scale_ref[0:1, :], scale_ref[1:2, :]
    is_first, is_last, even = whereabouts(peers)
    lane = lax.broadcasted_iota(jnp.int32, (24, 128), 1)
    plane = lax.broadcasted_iota(jnp.int32, (24, 128), 0)
    cut = ((plane == 7) & is_first) | ((plane == 14) & is_last)
    quarter = 0.25 * inverse

    def three(own, chip, far):
        return jnp.concatenate([jnp.where(even, far, chip), own, jnp.where(even, chip, far)], axis=0)

    for at in range(around):
        tan[at] = three(tan_ref[at], tan_chip_ref[at], tan_far_ref[at]) * quarter
    for at in range(around):
        here = tan[at]
        up_a, down_a = tan[(at + 1) % around], tan[(at - 1) % around]
        up_r = jnp.where(lane == 127, 0.0, pltpu.roll(here, 127, 1))
        down_r = jnp.where(lane == 0, 0.0, pltpu.roll(here, 1, 1))
        up_x = pltpu.roll(here, 23, 0)
        down_x = pltpu.roll(here, 1, 0)
        found = three(found_ref[at], found_chip_ref[at], found_far_ref[at])
        main[at] = (found - centre) * inverse + ((up_a + down_a) + (up_r + down_r) + (up_x + down_x))
        beyond = jnp.where(lane >= 126, 0.0, up_r)
        off_r[at] = beyond
        back_r[at] = pltpu.roll(beyond, 2, 1)
        beyond = jnp.where(cut, 0.0, up_x)
        off_x[at] = beyond
        back_x[at] = pltpu.roll(beyond, 2, 0)

    def apply(index, at):
        value = vectors[index, at]
        result = main[at] * value
        result = result - tan[(at + 1) % around] * vectors[index, (at + 2) % around]
        result = result - tan[(at - 1) % around] * vectors[index, (at - 2) % around]
        result = result - off_r[at] * pltpu.roll(value, 126, 1) - back_r[at] * pltpu.roll(value, 2, 1)
        return result - off_x[at] * pltpu.roll(value, 22, 0) - back_x[at] * pltpu.roll(value, 2, 0)

    for at in range(around):
        vectors[0, at] = three(seed_ref[at], seed_chip_ref[at], seed_far_ref[at])
    for degree in range(1, HALF + 1):
        for at in range(around):
            value = apply(degree - 1, at)
            if degree > 1:
                value = value + value - vectors[degree - 2, at]
            vectors[degree, at] = value
    pairs = []
    if last:
        for degree in range(1, HALF + 1):
            for at in range(around):
                value = vectors[degree, at, 8:16, :]
                own_ref[degree - 1, at] = value + value - earlier_ref[HALF - degree, at]
            before = earlier_ref.at[HALF] if degree == 1 else own_ref.at[degree - 2]
            pairs += [(before, own_ref.at[degree - 1]), (own_ref.at[degree - 1], own_ref.at[degree - 1])]
    else:
        for degree in range(HALF + 1):
            for at in range(around):
                own_ref[degree, at] = vectors[degree, at, 8:16, :]
            if degree:
                pairs.append((own_ref.at[degree - 1], own_ref.at[degree]))
            pairs.append((own_ref.at[degree], own_ref.at[degree]))
    column = lax.broadcasted_iota(jnp.int32, (1, 128), 1)
    sums = previous_ref[0:1, :] if last else jnp.zeros((1, 128), F32)
    for number, (left, right) in enumerate(pairs):
        parts = [left[at] * right[at] for at in range(around)]
        while len(parts) > 1:
            parts = [a + b for a, b in zip(parts[::2], parts[1::2], strict=True)]
        entry = jnp.sum(jnp.sum(parts[0], axis=0, keepdims=True), axis=1, keepdims=True)
        place_of = number + (2 * HALF + 1 if last else 0)
        sums = jnp.where(column == place_of, jnp.broadcast_to(entry, (1, 128)), sums)
    sums_ref[...] = jnp.broadcast_to(sums, sums_ref.shape)


def unpack_gram(all_ref, total):
    row = jnp.sum(all_ref[...], axis=0, keepdims=True)
    moments = []
    for number in range(2 * total - 1):
        entry = jnp.broadcast_to(row[:, number : number + 1], (1, 128))
        moments.append(entry if number < 2 else entry + entry - moments[number % 2])
    gram = {}
    for i in range(total):
        for j in range(i, total):
            gram[i, j] = gram[j, i] = 0.5 * (moments[i + j] + moments[j - i])
    return gram


def dot(gram, left, right):
    total = len(left)
    result = None
    for i in range(total):
        if left[i] is None:
            continue
        inner = None
        for j in range(total):
            if right[j] is not None:
                term = gram[i, j] * right[j]
                inner = term if inner is None else inner + term
        if inner is not None:
            result = left[i] * inner if result is None else result + left[i] * inner
    return result


def axpy(scale, left, right):
    result = []
    for a, b in zip(left, right, strict=True):
        a = None if a is None else (a if scale is None else scale * a)
        result.append(b if a is None else (a if b is None else b + a))
    return result


def times_operator(vector, centre, half_width):
    total = len(vector)
    result = [None] * total
    half = 0.5 * half_width

    def add(index, term):
        result[index] = term if result[index] is None else result[index] + term

    for j, c in enumerate(vector):
        if c is None:
            continue
        add(j, centre * c)
        add(j + 1, (half if j else half_width) * c)
        if j:
            add(j - 1, half * c)
    return result


def iterate(gram, total, centre, half_width):
    residual = [jnp.ones((1, 128), F32)] + [None] * (total - 1)
    direction = residual
    change = [None] * total
    norms = [jnp.sqrt(gram[i, i]) for i in range(total)]
    current = gram[0, 0]
    worst = jnp.zeros((1, 128), F32)
    for step in range(ITERS):
        image = times_operator(direction, centre, half_width)
        alpha = current / dot(gram, direction, image)
        change = axpy(alpha, direction, change)
        residual = axpy(-alpha, image, residual)
        following = dot(gram, residual, residual)
        bound = None
        for c, n in zip(residual, norms, strict=True):
            if c is not None:
                bound = jnp.abs(c) * n if bound is None else bound + jnp.abs(c) * n
        worst = jnp.maximum(worst, bound * bound / following)
        worst = jnp.where(following > 0.0, worst, jnp.inf)
        if step < ITERS - 1:
            direction = axpy(following / current, direction, residual)
        current = following
    return change, residual, worst


def combine(coefficients, early_ref, late_ref, at):
    result = None
    for index, c in enumerate(coefficients):
        if c is not None:
            vector = early_ref[index, at] if index <= HALF else late_ref[index - HALF - 1, at]
            result = c * vector if result is None else result + c * vector
    return result


def last_kernel(around, scale_ref, all_ref, early_ref, late_ref, send_ref, worst_ref):
    total = 2 * HALF + 1
    change, residual, worst = iterate(unpack_gram(all_ref, total), total, scale_ref[0:1, :], scale_ref[2:3, :])
    worst_ref[...] = jnp.broadcast_to(worst, (8, 128))
    pairs = [[None if c is None else jnp.broadcast_to(c, (8, 128)) for c in part] for part in (change, residual)]
    for b in range(around // 8):
        for half in range(2):
            for number in range(2):
                tiles = [combine(pairs[number], early_ref, late_ref, 8 * b + 4 * half + a) for a in range(4)]
                tiles = regroup(tiles)
                for m in range(4):
                    send_ref[4 * b + m, half, number] = tiles[m]


def deliver_kernel(path, u_ref, recv_ref, worst_ref, instead_updated_ref, instead_residual_ref, *refs):
    updated_ref, residual_ref, turned = refs
    slab = lax.axis_index("slab")
    for source in range(recv_ref.shape[0]):
        start = pl.multiple_of(8 * place(slab, path[source], len(path)), 8)
        for index in range(2):
            turned[index, pl.ds(start, 8), :] = recv_ref[source, 0, index]
    good = jnp.broadcast_to(worst_ref[0:1, :] < MOST_LOST, (32, 128))
    change = jnp.transpose(turned[0]).reshape(4, 32, 128)
    residual = jnp.transpose(turned[1]).reshape(4, 32, 128)
    for i in range(4):
        updated_ref[i] = jnp.where(good, u_ref[i] + change[i], instead_updated_ref[i])
        residual_ref[i] = jnp.where(good, residual[i], instead_residual_ref[i])


def sliced_body(
    displacement, load_field, foundation, plastic_flags, point_slot, family_in, family_mid, family_out, family_tan
):
    size_x, size_y, size_z = displacement.shape
    families = family_in.shape[0]
    along, across = lax.axis_size("blk"), lax.axis_size("micro")
    peers = along * across
    around = size_x * along
    everyone = peers * lax.axis_size("slab")
    path = [b * across + (m if b % 2 == 0 else across - 1 - m) for b in range(along) for m in range(across)]
    _, _, even = whereabouts(peers)
    spots = [0] * everyone
    for b in range(along):
        for s in range(2):
            for m in range(across):
                spots[place(s, path[b * across + m], peers) + peers * s] = (b * 2 + s) * across + m

    def swap(first, value):
        pairs = [(spots[i], spots[i + 1]) for i in range(first, everyone - 1, 2)]
        return lax.ppermute(value, AXES, pairs + [(b, a) for a, b in pairs])

    def neighbours(to_chip, to_far):
        far = swap(1, to_far)
        return swap(0, to_chip), far

    packed = pack_families(family_in, family_mid, family_out, family_tan)
    capacity = size_x * size_y * size_z // 2
    halves = pl.BlockSpec((4, 32, 128), lambda i: (i, 0, 0))
    (send,) = call(
        lambda *refs: spread_kernel(path, capacity, *refs),
        [((peers, 2, 4, 8, 128), F32)], [pltpu.VMEM((4, 128, 128), F32)], "spread",
        displacement, load_field, foundation, point_slot, plastic_flags,
        grid=(2,), ins=[halves] * 5, outs=[pl.BlockSpec((peers, 1, 4, 8, 128), lambda i: (0, i, 0, 0, 0))],
    )
    recv = lax.all_to_all(send, GROUP, 0, 0, tiled=True)
    field = (around, 8, 128)
    edge = (around // 8, 8, 128)
    message = (around + around // 8, 8, 128)
    strain, code, found, rest, to_chip, to_far, scale = call(
        lambda *refs: collect_kernel(around, *refs),
        [((3,) + field, F32), (field, jnp.int32), (field, F32), (field, F32), (message, F32), (message, F32), ((8, 128), F32)],
        [pltpu.VMEM(field, F32)], "collect", family_tan, recv,
    )
    chip, far = neighbours(to_chip, to_far)
    first = cells(strain, code, packed, families, 8, (1, 2, 3))
    outer = cells(strain, code, packed, families, 8, (0, 7), jnp.broadcast_to(even.astype(jnp.int32), (1, 128)), chip, far)
    top, bottom = outer[2, :, 7].reshape(edge), outer[2, :, 0].reshape(edge)
    edge_chip, edge_far = neighbours(jnp.where(even, top, bottom), jnp.where(even, bottom, top))
    second = cells(strain, code, packed, families, 8, (4, 5, 6))
    (own,) = call(
        lambda *refs: rhs_kernel(around, peers, *refs), [((2,) + field, F32)], [pltpu.VMEM(edge, F32)] * 2, "rhs",
        first, outer, second, rest, edge_chip, edge_far,
    )
    own_chip, own_far = neighbours(own, own)

    def basis(last, outputs, *vectors):
        return call(
            lambda *refs: basis_kernel(around, peers, last, *refs), outputs,
            [pltpu.VMEM((around, 24, 128), F32)] * 6 + [pltpu.VMEM((HALF + 1, around, 24, 128), F32)],
            "basis", scale, own[1], own_chip[1], own_far[1], found, chip, far, *vectors,
        )

    early, sums = basis(False, [((HALF + 1,) + field, F32), ((8, 128), F32)], own[0], own_chip[0], own_far[0])
    late, sums = basis(
        True, [((HALF,) + field, F32), ((everyone, 128), F32)], early[HALF], *neighbours(early[HALF], early[HALF]), early, sums
    )
    sums = lax.all_to_all(sums, AXES, 0, 0, tiled=True)
    send, worst = call(
        lambda *refs: last_kernel(around, *refs),
        [((peers, 2, 2, 8, 128), F32), ((8, 128), F32)], [], "last", scale, sums, early, late,
    )
    recv = lax.all_to_all(send, GROUP, 0, 0, tiled=True)
    inputs = (
        displacement, load_field, foundation, plastic_flags, point_slot, family_in, family_mid, family_out, family_tan
    )
    good, recv = lax.optimization_barrier((worst[0, 0] < MOST_LOST, recv))
    instead = lax.cond(good, lambda: (jnp.zeros_like(displacement),) * 2, lambda: plain_body(*inputs))
    shape = displacement.shape
    return call(
        lambda *refs: deliver_kernel(path, *refs), [(shape, F32), (shape, F32)], [pltpu.VMEM((2, 128, 128), F32)],
        "deliver", displacement, recv, worst, *instead, grid=(2,), outs=[halves] * 2,
        ins=[
            halves,
            pl.BlockSpec((peers, 1, 2, 8, 128), lambda i: (0, i, 0, 0, 0)),
            pl.BlockSpec((8, 128), lambda i: (0, 0)),
            halves,
            halves,
        ],
    )


def body(*inputs):
    size_x, size_y, size_z = inputs[0].shape
    along, across = lax.axis_size("blk"), lax.axis_size("micro")
    fits = (
        (size_x, size_y, size_z) == (8, 32, 128)
        and across == 4
        and size_z == 8 * along * across
        and lax.axis_size("slab") == 2
        and inputs[5].shape[0] == 4
    )
    if not fits:
        return plain_body(*inputs)
    return tuple(sliced_body(*inputs))


def solution(mesh):
    field = P("blk", "micro", "slab")
    return jax.shard_map(
        body,
        mesh=mesh,
        in_specs=(field,) * 5 + (P(),) * 4,
        out_specs=(field, field),
        check_vma=False,
    )
```

```python
import jax
import jax.numpy as jnp
from jax import lax
from jax.experimental import pallas as pl
from jax.experimental.pallas import tpu as pltpu
from jax.sharding import PartitionSpec as P

ITERS = 8
AXES = ("blk", "slab", "micro")
BF = jnp.bfloat16
F32 = jnp.float32


def split(value):
    high = lax.reduce_precision(value, 8, 7)
    return high.astype(BF), (value - high).astype(BF)


def pack_families(family_in, family_mid, family_out, family_tan):
    families, _, modes = family_in.shape
    spread = jnp.transpose(family_in, (2, 1, 0))
    spread = jnp.concatenate([spread, spread], axis=2).reshape(modes, 6 * families)
    high, low = split(spread)
    weight_in = jnp.concatenate([high, low], axis=1)
    none = jnp.zeros((families, 1, modes), BF)
    stress = jnp.concatenate([family_out, none], axis=1).reshape(4 * families, modes)
    none = jnp.zeros((families, 3, modes), BF)
    tan_high, tan_low = split(family_tan)
    tan_high = jnp.concatenate([none, tan_high[:, None]], axis=1).reshape(4 * families, modes)
    tan_low = jnp.concatenate([none, tan_low[:, None]], axis=1).reshape(4 * families, modes)
    weight_out = jnp.concatenate(
        [
            jnp.concatenate([stress, tan_high], axis=1),
            jnp.concatenate([jnp.zeros_like(stress), tan_low], axis=1),
        ],
        axis=0,
    )
    return weight_in, family_mid, weight_out


def cells_kernel(families, planes, strain_ref, code_ref, in_ref, mid_ref, out_ref, *refs, info_ref=None):
    *edges, answer_ref = refs
    modes = in_ref.shape[0]
    step = code_ref.shape[0]
    spots = [(a + i, x) for a in range(0, step, 2) for x in planes for i in range(2)]
    width = len(spots) * 128

    def evaluate(pairs):
        place = lax.broadcasted_iota(jnp.int32, (2 * families, 128), 0)
        column, family_row, flag_row = [], [], []
        for a, x in spots:
            code = code_ref[a, pl.ds(x, 1), :]
            family = lax.shift_right_logical(code, 1)
            picked = lax.rem(place, families) == jnp.broadcast_to(family, place.shape)
            pieces = []
            for j in range(3):
                value = strain_ref[j, a, pl.ds(x, 1), :]
                if edges and j == 2:
                    even, chip_ref, far_ref = edges
                    chip, far = chip_ref[0, pl.ds(a, 1), :], far_ref[0, pl.ds(a, 1), :]
                    beyond = jnp.where(even[...] == (1 if x == 7 else 0), chip, far) * 0.5
                    value = value - beyond if x == 0 else value + beyond
                value = jnp.broadcast_to(value, place.shape)
                high = value.astype(BF).astype(F32)
                piece = jnp.where(place < families, high, value - high)
                pieces.append(jnp.where(picked, piece, 0.0))
            column.append(jnp.concatenate(pieces, axis=0))
            family_row.append(family)
            flag_row.append(lax.bitwise_and(code, 1))
        spread = jnp.concatenate(column, axis=1).astype(BF)
        spread = jnp.concatenate([spread, spread], axis=0)
        family = jnp.concatenate(family_row, axis=1)
        flag = jnp.concatenate(flag_row, axis=1)
        modal = jnp.dot(in_ref[...], spread, preferred_element_type=F32)
        flagged = jnp.broadcast_to(flag, (modes, width)) > 0
        active = jnp.where(flagged, jnp.tanh(modal), modal).astype(BF)
        if pairs is None:
            wide = jnp.broadcast_to(family, (modes, width)).astype(BF)
            nothing = jnp.zeros_like(active)
            stacked = jnp.concatenate(
                [jnp.where(wide == jnp.array(f, BF), active, nothing) for f in range(families)], axis=0
            )
            mixing = jnp.concatenate([mid_ref[f] for f in range(families)], axis=1)
            hidden = jnp.dot(mixing, stacked, preferred_element_type=F32)
        else:
            nothing = jnp.zeros((modes, 256), BF)
            parts = []
            for number, (one, other) in enumerate(pairs):
                part = slice(256 * number, 256 * number + 256)
                ours = jnp.where(family[:, part] == one, 1.0, 0.0)
                ours = jnp.broadcast_to(ours, (modes, 256)).astype(BF) > jnp.array(0.5, BF)
                mine = active[:, part]
                stacked = jnp.concatenate([jnp.where(ours, mine, nothing), jnp.where(ours, nothing, mine)], axis=0)
                mixing = jnp.concatenate([mid_ref[one], mid_ref[other]], axis=1)
                parts.append(jnp.dot(mixing, stacked, preferred_element_type=F32))
            hidden = jnp.concatenate(parts, axis=1)
        bounded = jnp.tanh(hidden).astype(BF)
        both = jnp.concatenate([bounded, bounded * bounded], axis=0)
        result = jnp.dot(out_ref[...], both, preferred_element_type=F32)
        result = result[: 4 * families] + result[4 * families :]
        owner = lax.shift_right_logical(lax.broadcasted_iota(jnp.int32, (4 * families, width), 0), 2)
        result = jnp.where(owner == family, result, 0.0)
        total = result[:4]
        for f in range(1, families):
            total = total + result[4 * f : 4 * f + 4]
        for i, (a, x) in enumerate(spots):
            answer_ref[:, a, x, :] = total[:, i * 128 : (i + 1) * 128]

    if info_ref is None:
        evaluate(None)
        return
    first = pl.program_id(0) * (step // 2)
    pairs, more = [], 0
    for a in range(step // 2):
        for x in planes:
            pairs.append((info_ref[x, first + a], info_ref[x, 16 + first + a]))
            more = more + info_ref[x, 32 + first + a]

    @pl.when(more == 0)
    def _():
        evaluate(pairs)

    @pl.when(more != 0)
    def _():
        evaluate(None)


def cells(strain, code, packed, families, step, planes, *edges, info=None):
    weight_in, weight_mid, weight_out = packed
    count = code.shape[0]
    planes = tuple(planes)
    points = count * len(planes) * 128
    modes = weight_in.shape[0]

    def whole(array):
        return pl.BlockSpec(array.shape, lambda i, *_: (0,) * array.ndim)

    def kernel(*refs):
        if info is None:
            cells_kernel(families, planes, *refs)
        else:
            cells_kernel(families, planes, *refs[1:], info_ref=refs[0])

    scalars = () if info is None else (info,)
    return pl.pallas_call(
        kernel,
        grid_spec=pltpu.PrefetchScalarGridSpec(
            num_scalar_prefetch=len(scalars),
            grid=(count // step,),
            in_specs=[
                pl.BlockSpec((3, step, 8, 128), lambda i, *_: (0, i, 0, 0)),
                pl.BlockSpec((step, 8, 128), lambda i, *_: (i, 0, 0)),
                whole(weight_in),
                whole(weight_mid),
                whole(weight_out),
            ]
            + [pl.BlockSpec((1, 128), lambda i, *_: (0, 0)) for _ in edges[:1]]
            + [pl.BlockSpec((1, 8, 128), lambda i, *_: (count + i, 0, 0)) for _ in edges[1:]],
            out_specs=pl.BlockSpec((4, step, 8, 128), lambda i, *_: (0, i, 0, 0)),
        ),
        out_shape=jax.ShapeDtypeStruct((4, count, 8, 128), F32),
        compiler_params=pltpu.CompilerParams(vmem_limit_bytes=48 * 2**20),
        cost_estimate=pl.CostEstimate(
            flops=2 * points * modes * modes * (families + 1), bytes_accessed=points * 32, transcendentals=2 * points * modes
        ),
        name="cells",
    )(*scalars, strain, code, weight_in, weight_mid, weight_out, *edges)


def global_sum(value):
    count = 1
    for axis in AXES:
        count = count * lax.axis_size(axis)
    spread = jnp.broadcast_to(value.reshape(1, 1), (count, 128))
    return jnp.sum(lax.all_to_all(spread, AXES, 0, 0, tiled=True)[:, 0])


def widened(cells_, axis, dim, width, closed):
    count = lax.axis_size(axis)
    ends = count if closed else count - 1
    head = lax.slice_in_dim(cells_, 0, width, axis=dim)
    tail = lax.slice_in_dim(cells_, cells_.shape[dim] - width, cells_.shape[dim], axis=dim)
    before = lax.ppermute(tail, axis, [(i, (i + 1) % count) for i in range(ends)])
    after = lax.ppermute(head, axis, [((i + 1) % count, i) for i in range(ends)])
    return jnp.concatenate([before, cells_, after], axis=dim)


HALOS = (("blk", True), ("micro", False), ("slab", False))


def widened_all(field, width):
    return [widened(field, axis, dim, width, closed) for dim, (axis, closed) in enumerate(HALOS)]


def difference(field, dim):
    length = field.shape[dim]
    return (lax.slice_in_dim(field, 2, length, axis=dim) - lax.slice_in_dim(field, 0, length - 2, axis=dim)) * 0.5


def plain_body(
    displacement, load_field, foundation, plastic_flags, point_slot, family_in, family_mid, family_out, family_tan
):
    size_x, size_y, size_z = displacement.shape
    points = size_x * size_y * size_z
    families = family_in.shape[0]
    capacity = points // 2
    packed = pack_families(family_in, family_mid, family_out, family_tan)
    strain = [difference(w, dim) for dim, w in enumerate(widened_all(displacement, 1))]
    code = 2 * (point_slot // capacity) + plastic_flags
    tiles = points // 1024
    answers = cells(jnp.stack(strain).reshape(3, tiles, 8, 128), code.reshape(tiles, 8, 128), packed, families, 2, range(8))
    answers = answers.reshape(4, size_x, size_y, size_z)
    tangents = widened_all(0.5 + answers[3], 1)
    divergence = sum(
        difference(widened(answers[dim], axis, dim, 1, closed), dim) for dim, (axis, closed) in enumerate(HALOS)
    )
    rhs = load_field - foundation * displacement + divergence
    solution_ = jnp.zeros_like(rhs)
    residual = rhs
    direction = rhs
    current = global_sum(jnp.sum(residual * residual))
    for _ in range(ITERS):
        total = sum(
            difference(tangents[dim] * difference(w, dim), dim) for dim, w in enumerate(widened_all(direction, 2))
        )
        image = foundation * direction - total
        alpha = current / global_sum(jnp.sum(direction * image))
        solution_ = solution_ + alpha * direction
        residual = residual - alpha * image
        following = global_sum(jnp.sum(residual * residual))
        direction = residual + following / current * direction
        current = following
    return displacement + solution_, residual


VMEM = pl.BlockSpec(memory_space=pltpu.VMEM)
GROUP = ("blk", "micro")


def call(kernel, out_shapes, scratch, name, *args, grid=(), ins=None, outs=None):
    return pl.pallas_call(
        kernel,
        out_shape=[jax.ShapeDtypeStruct(shape, dtype) for shape, dtype in out_shapes],
        grid=grid,
        in_specs=ins or [VMEM] * len(args),
        out_specs=outs or [VMEM] * len(out_shapes),
        scratch_shapes=scratch,
        compiler_params=pltpu.CompilerParams(vmem_limit_bytes=40 * 2**20),
        name=name,
    )(*args)


def regroup(tiles):
    group = lax.broadcasted_iota(jnp.int32, (8, 128), 1) // 32
    result = []
    for a in range(4):
        tile = tiles[0]
        for m in range(4):
            shift = (m - a) * 32 % 128
            moved = pltpu.roll(tiles[m], shift, 1) if shift else tiles[m]
            tile = moved if m == 0 else jnp.where(group == m, moved, tile)
        result.append(tile)
    return result


def place(slab, position, peers):
    return position + slab * (peers - 1 - 2 * position)


def whereabouts(peers):
    across = lax.axis_size("micro")
    b, m, slab = lax.axis_index("blk"), lax.axis_index("micro"), lax.axis_index("slab")
    position = place(slab, b * across + jnp.where(b % 2 == 0, m, across - 1 - m), peers)
    return (slab == 0) & (position == 0), (slab == 1) & (position == peers - 1), position % 2 == 0


def spread_kernel(path, capacity, u_ref, load_ref, found_ref, slot_ref, flag_ref, send_ref, turned):
    peers = len(path)
    slab = lax.axis_index("slab")
    code = flag_ref[...]
    for family in range(1, 4):
        code = code + jnp.where(slot_ref[...] >= family * capacity, 2, 0)
    rest = load_ref[...] - found_ref[...] * u_ref[...]
    for number, value in enumerate((u_ref[...], code.astype(F32), found_ref[...], rest)):
        turned[number] = jnp.transpose(value.reshape(128, 128))
    for target in range(peers):
        start = pl.multiple_of(8 * place(slab, path[target], peers), 8)
        for number in range(4):
            send_ref[target, 0, number] = turned[number, pl.ds(start, 8), :]


def beside(tile, low, high):
    row = lax.broadcasted_iota(jnp.int32, (8, 128), 0)
    after = jnp.where(row == 7, jnp.broadcast_to(high, (8, 128)), pltpu.roll(tile, 7, 0))
    before = jnp.where(row == 0, jnp.broadcast_to(low, (8, 128)), pltpu.roll(tile, 1, 0))
    return after, before


def radial(tile):
    lane = lax.broadcasted_iota(jnp.int32, tile.shape, tile.ndim - 1)
    after = jnp.where(lane == 127, 0.0, pltpu.roll(tile, 127, tile.ndim - 1))
    before = jnp.where(lane == 0, 0.0, pltpu.roll(tile, 1, tile.ndim - 1))
    return (after - before) * 0.5


def collect_kernel(around, tan_ref, recv_ref, strain_ref, code_ref, found_ref, rest_ref, chip_ref, far_ref, scale_ref, u):
    _, _, even = whereabouts(recv_ref.shape[0])
    typical = jnp.sum(jnp.sum(tan_ref[...], axis=1, keepdims=True), axis=0, keepdims=True) / tan_ref.shape[0]
    centre = jnp.broadcast_to(1.1 + 1.4 * (0.5 + 0.33 * typical), (8, 128))
    row = lax.broadcasted_iota(jnp.int32, (8, 128), 0)
    scale_ref[...] = jnp.where(row == 0, centre, jnp.where(row == 1, 1.0 / (centre - 0.4), centre - 0.4))
    for b in range(around // 8):
        for half in range(2):
            for number in range(4):
                tiles = regroup([recv_ref[4 * b + m, half, number] for m in range(4)])
                for a in range(4):
                    at = 8 * b + 4 * half + a
                    if number == 0:
                        u[at] = tiles[a]
                    elif number == 1:
                        code_ref[at] = tiles[a].astype(jnp.int32)
                    elif number == 2:
                        found_ref[at] = tiles[a]
                        chip_ref[at] = tiles[a]
                        far_ref[at] = tiles[a]
                    else:
                        rest_ref[at] = tiles[a]
    nothing = jnp.zeros((1, 128), F32)
    for at in range(around):
        tile = u[at]
        strain_ref[0, at] = (u[(at + 1) % around] - u[(at - 1) % around]) * 0.5
        strain_ref[1, at] = radial(tile)
        after, before = beside(tile, nothing, nothing)
        strain_ref[2, at] = (after - before) * 0.5
        chip_ref[around + at // 8, pl.ds(at % 8, 1), :] = tile[7:8]
        far_ref[around + at // 8, pl.ds(at % 8, 1), :] = tile[0:1]
    for index in range(around, around + around // 8):
        bottom, top = far_ref[index], chip_ref[index]
        chip_ref[index] = jnp.where(even, top, bottom)
        far_ref[index] = jnp.where(even, bottom, top)


def network(count):
    pairs = []
    p = 1
    while p < count:
        k = p
        while k >= 1:
            for j in range(k % p, count - k, 2 * k):
                for i in range(j, min(j + k, count - k)):
                    if i // (2 * p) == (i + k) // (2 * p):
                        pairs.append((i, i + k))
            k //= 2
        p *= 2
    return pairs


def sort_tiles(keys, *carried):
    keys, carried = list(keys), [list(c) for c in carried]
    for i, j in network(len(keys)):
        wrong = keys[i] > keys[j]
        keys[i], keys[j] = jnp.minimum(keys[i], keys[j]), jnp.maximum(keys[i], keys[j])
        for c in carried:
            c[i], c[j] = jnp.where(wrong, c[j], c[i]), jnp.where(wrong, c[i], c[j])
    return keys, carried


def take(tile, index):
    return jnp.take_along_axis(tile, index, axis=1, mode="promise_in_bounds")


def arrange_kernel(around, strain_ref, code_ref, sorted_ref, sorted_code_ref, rank_ref, origin_ref, info_ref):
    lane = lax.broadcasted_iota(jnp.int32, (8, 128), 1)
    right = lax.shift_right_logical
    keys, strains = [], [[], [], []]
    for at in range(around):
        code = code_ref[at]
        shift = right(code, 1) * 8
        counts = lax.shift_left(jnp.ones((8, 128), jnp.int32), shift)
        for step in (1, 2, 4, 8, 16, 32, 64):
            counts = counts + jnp.where(lane >= step, pltpu.roll(counts, step, 1), 0)
        total = jnp.broadcast_to(counts[:, 127:128], (8, 128))
        first = total & 255
        second = first + (right(total, 8) & 255)
        third = second + (right(total, 16) & 255)

        def start(family):
            return jnp.where(
                family < 2, jnp.where(family < 1, 0, first), jnp.where(family < 3, second, third)
            )

        turn = (at % 8 * 16 + at // 8 * 4) % 128
        rank_ref[at] = (start(right(code, 1)) + (right(counts, shift) & 255) + (turn - 1)) & 127
        spot = (lane + (128 - turn)) & 127
        family = (
            jnp.where(spot >= first, 1, 0) + jnp.where(spot >= second, 1, 0) + jnp.where(spot >= third, 1, 0)
        )
        wanted = spot - start(family)
        shift = family * 8
        source = jnp.zeros((8, 128), jnp.int32)
        for step in (64, 32, 16, 8, 4, 2, 1):
            seen = right(take(counts, source + (step - 1)), shift) & 255
            source = jnp.where(seen <= wanted, source + step, source)
        moved = take(code, source)
        keys.append(lax.shift_left(right(moved, 1), jnp.full((8, 128), 6, jnp.int32)) + (2 * at) + (moved & 1))
        for j in range(3):
            strains[j].append(take(strain_ref[j, at], source))
    keys, strains = sort_tiles(keys, *strains)
    info = jnp.zeros((8, 128), jnp.int32)
    for at in range(around):
        family = right(keys[at], 6)
        sorted_code_ref[at] = 2 * family + (keys[at] & 1)
        origin_ref[at] = right(keys[at], 1) & 31
        for j in range(3):
            sorted_ref[j, at] = strains[j][at]
        if at % 2:
            before = right(keys[at - 1], 6)
            low = jnp.min(jnp.minimum(before, family), axis=1, keepdims=True)
            high = jnp.max(jnp.maximum(before, family), axis=1, keepdims=True)
            low, high = jnp.broadcast_to(low, (8, 128)), jnp.broadcast_to(high, (8, 128))
            odd = jnp.where((family != low) & (family != high), 1, 0) + jnp.where((before != low) & (before != high), 1, 0)
            odd = jnp.broadcast_to(jnp.max(odd, axis=1, keepdims=True), (8, 128))
            for number, value in enumerate((low, high, odd)):
                info = jnp.where(lane == 16 * number + at // 2, value, info)
    info_ref[...] = info


def rhs_kernel(around, peers, first_ref, outer_ref, second_ref, rank_ref, origin_ref, rest_ref, chip_ref, far_ref, own_ref, low_ref, high_ref, answers):
    _, _, even = whereabouts(peers)
    for index in range(around // 8):
        low_ref[index] = jnp.where(even, far_ref[index], chip_ref[index])
        high_ref[index] = jnp.where(even, chip_ref[index], far_ref[index])
    row = lax.broadcasted_iota(jnp.int32, (8, 128), 0)
    rim = (row == 0) | (row == 7)

    moved = [[jnp.where(row < 4, first_ref[j, at], second_ref[j, at]) for at in range(around)] for j in range(4)]
    _, moved = sort_tiles([origin_ref[at] for at in range(around)], *moved)
    for at in range(around):
        for j in range(4):
            answers[j, at] = jnp.where(rim, outer_ref[j, at], take(moved[j][at], rank_ref[at]))

    def answer(number, at):
        return answers[number, at]

    cycle = [answer(0, at) for at in range(around)]
    for at in range(around):
        low = low_ref[at // 8, pl.ds(at % 8, 1), :]
        high = high_ref[at // 8, pl.ds(at % 8, 1), :]
        after, before = beside(answer(2, at), low, high)
        divergence = (cycle[(at + 1) % around] - cycle[(at - 1) % around]) * 0.5
        divergence = divergence + radial(answer(1, at)) + (after - before) * 0.5
        own_ref[0, at] = rest_ref[at] + divergence
        own_ref[1, at] = 0.5 + answer(3, at)


HALF = ITERS // 2
MOST_LOST = 1.0e5


def basis_kernel(
    around, peers, last, scale_ref, tan_ref, tan_chip_ref, tan_far_ref, found_ref, found_chip_ref, found_far_ref,
    seed_ref, seed_chip_ref, seed_far_ref, *refs
):
    if last:
        earlier_ref, previous_ref, own_ref, sums_ref, *scratch = refs
    else:
        own_ref, sums_ref, *scratch = refs
    tan, main, off_r, back_r, off_x, back_x, vectors = scratch
    centre, inverse = scale_ref[0:1, :], scale_ref[1:2, :]
    is_first, is_last, even = whereabouts(peers)
    lane = lax.broadcasted_iota(jnp.int32, (24, 128), 1)
    plane = lax.broadcasted_iota(jnp.int32, (24, 128), 0)
    cut = ((plane == 7) & is_first) | ((plane == 14) & is_last)
    quarter = 0.25 * inverse

    def three(own, chip, far):
        return jnp.concatenate([jnp.where(even, far, chip), own, jnp.where(even, chip, far)], axis=0)

    for at in range(around):
        tan[at] = three(tan_ref[at], tan_chip_ref[at], tan_far_ref[at]) * quarter
    for at in range(around):
        here = tan[at]
        up_a, down_a = tan[(at + 1) % around], tan[(at - 1) % around]
        up_r = jnp.where(lane == 127, 0.0, pltpu.roll(here, 127, 1))
        down_r = jnp.where(lane == 0, 0.0, pltpu.roll(here, 1, 1))
        up_x = pltpu.roll(here, 23, 0)
        down_x = pltpu.roll(here, 1, 0)
        found = three(found_ref[at], found_chip_ref[at], found_far_ref[at])
        main[at] = (found - centre) * inverse + ((up_a + down_a) + (up_r + down_r) + (up_x + down_x))
        beyond = jnp.where(lane >= 126, 0.0, up_r)
        off_r[at] = beyond
        back_r[at] = pltpu.roll(beyond, 2, 1)
        beyond = jnp.where(cut, 0.0, up_x)
        off_x[at] = beyond
        back_x[at] = pltpu.roll(beyond, 2, 0)

    def apply(index, at):
        value = vectors[index, at]
        result = main[at] * value
        result = result - tan[(at + 1) % around] * vectors[index, (at + 2) % around]
        result = result - tan[(at - 1) % around] * vectors[index, (at - 2) % around]
        result = result - off_r[at] * pltpu.roll(value, 126, 1) - back_r[at] * pltpu.roll(value, 2, 1)
        return result - off_x[at] * pltpu.roll(value, 22, 0) - back_x[at] * pltpu.roll(value, 2, 0)

    for at in range(around):
        vectors[0, at] = three(seed_ref[at], seed_chip_ref[at], seed_far_ref[at])
    for degree in range(1, HALF + 1):
        for at in range(around):
            value = apply(degree - 1, at)
            if degree > 1:
                value = value + value - vectors[degree - 2, at]
            vectors[degree, at] = value
    pairs = []
    if last:
        for degree in range(1, HALF + 1):
            for at in range(around):
                value = vectors[degree, at, 8:16, :]
                own_ref[degree - 1, at] = value + value - earlier_ref[HALF - degree, at]
            before = earlier_ref.at[HALF] if degree == 1 else own_ref.at[degree - 2]
            pairs += [(before, own_ref.at[degree - 1]), (own_ref.at[degree - 1], own_ref.at[degree - 1])]
    else:
        for degree in range(HALF + 1):
            for at in range(around):
                own_ref[degree, at] = vectors[degree, at, 8:16, :]
            if degree:
                pairs.append((own_ref.at[degree - 1], own_ref.at[degree]))
            pairs.append((own_ref.at[degree], own_ref.at[degree]))
    column = lax.broadcasted_iota(jnp.int32, (1, 128), 1)
    sums = previous_ref[0:1, :] if last else jnp.zeros((1, 128), F32)
    for number, (left, right) in enumerate(pairs):
        parts = [left[at] * right[at] for at in range(around)]
        while len(parts) > 1:
            parts = [a + b for a, b in zip(parts[::2], parts[1::2], strict=True)]
        entry = jnp.sum(jnp.sum(parts[0], axis=0, keepdims=True), axis=1, keepdims=True)
        place_of = number + (2 * HALF + 1 if last else 0)
        sums = jnp.where(column == place_of, jnp.broadcast_to(entry, (1, 128)), sums)
    sums_ref[...] = jnp.broadcast_to(sums, sums_ref.shape)


def unpack_gram(all_ref, total):
    row = jnp.sum(all_ref[...], axis=0, keepdims=True)
    moments = []
    for number in range(2 * total - 1):
        entry = jnp.broadcast_to(row[:, number : number + 1], (1, 128))
        moments.append(entry if number < 2 else entry + entry - moments[number % 2])
    gram = {}
    for i in range(total):
        for j in range(i, total):
            gram[i, j] = gram[j, i] = 0.5 * (moments[i + j] + moments[j - i])
    return gram


def dot(gram, left, right):
    total = len(left)
    result = None
    for i in range(total):
        if left[i] is None:
            continue
        inner = None
        for j in range(total):
            if right[j] is not None:
                term = gram[i, j] * right[j]
                inner = term if inner is None else inner + term
        if inner is not None:
            result = left[i] * inner if result is None else result + left[i] * inner
    return result


def axpy(scale, left, right):
    result = []
    for a, b in zip(left, right, strict=True):
        a = None if a is None else (a if scale is None else scale * a)
        result.append(b if a is None else (a if b is None else b + a))
    return result


def times_operator(vector, centre, half_width):
    total = len(vector)
    result = [None] * total
    half = 0.5 * half_width

    def add(index, term):
        result[index] = term if result[index] is None else result[index] + term

    for j, c in enumerate(vector):
        if c is None:
            continue
        add(j, centre * c)
        add(j + 1, (half if j else half_width) * c)
        if j:
            add(j - 1, half * c)
    return result


def iterate(gram, total, centre, half_width):
    residual = [jnp.ones((1, 128), F32)] + [None] * (total - 1)
    direction = residual
    change = [None] * total
    norms = [jnp.sqrt(gram[i, i]) for i in range(total)]
    current = gram[0, 0]
    worst = jnp.zeros((1, 128), F32)
    for step in range(ITERS):
        image = times_operator(direction, centre, half_width)
        alpha = current / dot(gram, direction, image)
        change = axpy(alpha, direction, change)
        residual = axpy(-alpha, image, residual)
        following = dot(gram, residual, residual)
        bound = None
        for c, n in zip(residual, norms, strict=True):
            if c is not None:
                bound = jnp.abs(c) * n if bound is None else bound + jnp.abs(c) * n
        worst = jnp.maximum(worst, bound * bound / following)
        worst = jnp.where(following > 0.0, worst, jnp.inf)
        if step < ITERS - 1:
            direction = axpy(following / current, direction, residual)
        current = following
    return change, residual, worst


def combine(coefficients, early_ref, late_ref, at):
    result = None
    for index, c in enumerate(coefficients):
        if c is not None:
            vector = early_ref[index, at] if index <= HALF else late_ref[index - HALF - 1, at]
            result = c * vector if result is None else result + c * vector
    return result


def last_kernel(around, scale_ref, all_ref, early_ref, late_ref, send_ref, worst_ref):
    total = 2 * HALF + 1
    change, residual, worst = iterate(unpack_gram(all_ref, total), total, scale_ref[0:1, :], scale_ref[2:3, :])
    worst_ref[...] = jnp.broadcast_to(worst, (8, 128))
    pairs = [[None if c is None else jnp.broadcast_to(c, (8, 128)) for c in part] for part in (change, residual)]
    for b in range(around // 8):
        for half in range(2):
            for number in range(2):
                tiles = [combine(pairs[number], early_ref, late_ref, 8 * b + 4 * half + a) for a in range(4)]
                tiles = regroup(tiles)
                for m in range(4):
                    send_ref[4 * b + m, half, number] = tiles[m]


def deliver_kernel(path, u_ref, recv_ref, worst_ref, instead_updated_ref, instead_residual_ref, *refs):
    updated_ref, residual_ref, turned = refs
    slab = lax.axis_index("slab")
    for source in range(recv_ref.shape[0]):
        start = pl.multiple_of(8 * place(slab, path[source], len(path)), 8)
        for index in range(2):
            turned[index, pl.ds(start, 8), :] = recv_ref[source, 0, index]
    good = jnp.broadcast_to(worst_ref[0:1, :] < MOST_LOST, (32, 128))
    change = jnp.transpose(turned[0]).reshape(4, 32, 128)
    residual = jnp.transpose(turned[1]).reshape(4, 32, 128)
    for i in range(4):
        updated_ref[i] = jnp.where(good, u_ref[i] + change[i], instead_updated_ref[i])
        residual_ref[i] = jnp.where(good, residual[i], instead_residual_ref[i])


def sliced_body(
    displacement, load_field, foundation, plastic_flags, point_slot, family_in, family_mid, family_out, family_tan
):
    size_x, size_y, size_z = displacement.shape
    families = family_in.shape[0]
    along, across = lax.axis_size("blk"), lax.axis_size("micro")
    peers = along * across
    around = size_x * along
    everyone = peers * lax.axis_size("slab")
    path = [b * across + (m if b % 2 == 0 else across - 1 - m) for b in range(along) for m in range(across)]
    _, _, even = whereabouts(peers)
    spots = [0] * everyone
    for b in range(along):
        for s in range(2):
            for m in range(across):
                spots[place(s, path[b * across + m], peers) + peers * s] = (b * 2 + s) * across + m

    def swap(first, value):
        pairs = [(spots[i], spots[i + 1]) for i in range(first, everyone - 1, 2)]
        return lax.ppermute(value, AXES, pairs + [(b, a) for a, b in pairs])

    def neighbours(to_chip, to_far):
        far = swap(1, to_far)
        return swap(0, to_chip), far

    packed = pack_families(family_in, family_mid, family_out, family_tan)
    capacity = size_x * size_y * size_z // 2
    halves = pl.BlockSpec((4, 32, 128), lambda i: (i, 0, 0))
    (send,) = call(
        lambda *refs: spread_kernel(path, capacity, *refs),
        [((peers, 2, 4, 8, 128), F32)], [pltpu.VMEM((4, 128, 128), F32)], "spread",
        displacement, load_field, foundation, point_slot, plastic_flags,
        grid=(2,), ins=[halves] * 5, outs=[pl.BlockSpec((peers, 1, 4, 8, 128), lambda i: (0, i, 0, 0, 0))],
    )
    recv = lax.all_to_all(send, GROUP, 0, 0, tiled=True)
    field = (around, 8, 128)
    edge = (around // 8, 8, 128)
    message = (around + around // 8, 8, 128)
    strain, code, found, rest, to_chip, to_far, scale = call(
        lambda *refs: collect_kernel(around, *refs),
        [((3,) + field, F32), (field, jnp.int32), (field, F32), (field, F32), (message, F32), (message, F32), ((8, 128), F32)],
        [pltpu.VMEM(field, F32)], "collect", family_tan, recv,
    )
    chip, far = neighbours(to_chip, to_far)
    grouped, grouped_code, rank, origin, info = call(
        lambda *refs: arrange_kernel(around, *refs),
        [((3,) + field, F32), (field, jnp.int32), (field, jnp.int32), (field, jnp.int32), ((8, 128), jnp.int32)],
        [], "arrange", strain, code,
    )
    first = cells(grouped, grouped_code, packed, families, 8, (1, 2, 3), info=info)
    outer = cells(strain, code, packed, families, 8, (0, 7), jnp.broadcast_to(even.astype(jnp.int32), (1, 128)), chip, far)
    top, bottom = outer[2, :, 7].reshape(edge), outer[2, :, 0].reshape(edge)
    edge_chip, edge_far = neighbours(jnp.where(even, top, bottom), jnp.where(even, bottom, top))
    second = cells(grouped, grouped_code, packed, families, 8, (4, 5, 6), info=info)
    (own,) = call(
        lambda *refs: rhs_kernel(around, peers, *refs), [((2,) + field, F32)], [pltpu.VMEM(edge, F32)] * 2 + [pltpu.VMEM((4,) + field, F32)], "rhs",
        first, outer, second, rank, origin, rest, edge_chip, edge_far,
    )
    own_chip, own_far = neighbours(own, own)

    def basis(last, outputs, *vectors):
        return call(
            lambda *refs: basis_kernel(around, peers, last, *refs), outputs,
            [pltpu.VMEM((around, 24, 128), F32)] * 6 + [pltpu.VMEM((HALF + 1, around, 24, 128), F32)],
            "basis", scale, own[1], own_chip[1], own_far[1], found, chip, far, *vectors,
        )

    early, sums = basis(False, [((HALF + 1,) + field, F32), ((8, 128), F32)], own[0], own_chip[0], own_far[0])
    late, sums = basis(
        True, [((HALF,) + field, F32), ((everyone, 128), F32)], early[HALF], *neighbours(early[HALF], early[HALF]), early, sums
    )
    sums = lax.all_to_all(sums, AXES, 0, 0, tiled=True)
    send, worst = call(
        lambda *refs: last_kernel(around, *refs),
        [((peers, 2, 2, 8, 128), F32), ((8, 128), F32)], [], "last", scale, sums, early, late,
    )
    recv = lax.all_to_all(send, GROUP, 0, 0, tiled=True)
    inputs = (
        displacement, load_field, foundation, plastic_flags, point_slot, family_in, family_mid, family_out, family_tan
    )
    good, recv = lax.optimization_barrier((worst[0, 0] < MOST_LOST, recv))
    instead = lax.cond(good, lambda: (jnp.zeros_like(displacement),) * 2, lambda: plain_body(*inputs))
    shape = displacement.shape
    return call(
        lambda *refs: deliver_kernel(path, *refs), [(shape, F32), (shape, F32)], [pltpu.VMEM((2, 128, 128), F32)],
        "deliver", displacement, recv, worst, *instead, grid=(2,), outs=[halves] * 2,
        ins=[
            halves,
            pl.BlockSpec((peers, 1, 2, 8, 128), lambda i: (0, i, 0, 0, 0)),
            pl.BlockSpec((8, 128), lambda i: (0, 0)),
            halves,
            halves,
        ],
    )


def body(*inputs):
    size_x, size_y, size_z = inputs[0].shape
    along, across = lax.axis_size("blk"), lax.axis_size("micro")
    fits = (
        (size_x, size_y, size_z) == (8, 32, 128)
        and across == 4
        and size_z == 8 * along * across
        and lax.axis_size("slab") == 2
        and inputs[5].shape[0] == 4
    )
    if not fits:
        return plain_body(*inputs)
    return tuple(sliced_body(*inputs))


def solution(mesh):
    field = P("blk", "micro", "slab")
    return jax.shard_map(
        body,
        mesh=mesh,
        in_specs=(field,) * 5 + (P(),) * 4,
        out_specs=(field, field),
        check_vma=False,
    )
```

```python
import jax
import jax.numpy as jnp
from jax import lax
from jax.experimental import pallas as pl
from jax.experimental.pallas import tpu as pltpu
from jax.sharding import PartitionSpec as P

ITERS = 8
AXES = ("blk", "slab", "micro")
BF = jnp.bfloat16
F32 = jnp.float32


def split(value):
    high = lax.reduce_precision(value, 8, 7)
    return high.astype(BF), (value - high).astype(BF)


def pack_families(family_in, family_mid, family_out, family_tan):
    families, _, modes = family_in.shape
    spread = jnp.transpose(family_in, (2, 1, 0))
    spread = jnp.concatenate([spread, spread], axis=2).reshape(modes, 6 * families)
    high, low = split(spread)
    weight_in = jnp.concatenate([high, low], axis=1)
    none = jnp.zeros((families, 1, modes), BF)
    stress = jnp.concatenate([family_out, none], axis=1).reshape(4 * families, modes)
    none = jnp.zeros((families, 3, modes), BF)
    tan_high, tan_low = split(family_tan)
    tan_high = jnp.concatenate([none, tan_high[:, None]], axis=1).reshape(4 * families, modes)
    tan_low = jnp.concatenate([none, tan_low[:, None]], axis=1).reshape(4 * families, modes)
    weight_out = jnp.concatenate(
        [
            jnp.concatenate([stress, tan_high], axis=1),
            jnp.concatenate([jnp.zeros_like(stress), tan_low], axis=1),
        ],
        axis=0,
    )
    return weight_in, family_mid, weight_out


def cells_kernel(families, planes, strain_ref, code_ref, in_ref, mid_ref, out_ref, *refs, info_ref=None):
    *edges, answer_ref = refs
    modes = in_ref.shape[0]
    step = code_ref.shape[0]
    spots = [(a + i, x) for a in range(0, step, 2) for x in planes for i in range(2)]
    width = len(spots) * 128

    def evaluate(pairs):
        place = lax.broadcasted_iota(jnp.int32, (2 * families, 128), 0)
        column, family_row, flag_row = [], [], []
        for a, x in spots:
            code = code_ref[a, pl.ds(x, 1), :]
            family = lax.shift_right_logical(code, 1)
            picked = lax.rem(place, families) == jnp.broadcast_to(family, place.shape)
            pieces = []
            for j in range(3):
                value = strain_ref[j, a, pl.ds(x, 1), :]
                if edges and j == 2:
                    even, chip_ref, far_ref = edges
                    chip, far = chip_ref[0, pl.ds(a, 1), :], far_ref[0, pl.ds(a, 1), :]
                    beyond = jnp.where(even[...] == (1 if x == 7 else 0), chip, far) * 0.5
                    value = value - beyond if x == 0 else value + beyond
                value = jnp.broadcast_to(value, place.shape)
                high = value.astype(BF).astype(F32)
                piece = jnp.where(place < families, high, value - high)
                pieces.append(jnp.where(picked, piece, 0.0))
            column.append(jnp.concatenate(pieces, axis=0))
            family_row.append(family)
            flag_row.append(lax.bitwise_and(code, 1))
        spread = jnp.concatenate(column, axis=1).astype(BF)
        spread = jnp.concatenate([spread, spread], axis=0)
        family = jnp.concatenate(family_row, axis=1)
        flag = jnp.concatenate(flag_row, axis=1)
        modal = jnp.dot(in_ref[...], spread, preferred_element_type=F32)
        flagged = jnp.broadcast_to(flag, (modes, width)) > 0
        active = jnp.where(flagged, jnp.tanh(modal), modal).astype(BF)
        if pairs is None:
            wide = jnp.broadcast_to(family, (modes, width)).astype(BF)
            nothing = jnp.zeros_like(active)
            stacked = jnp.concatenate(
                [jnp.where(wide == jnp.array(f, BF), active, nothing) for f in range(families)], axis=0
            )
            mixing = jnp.concatenate([mid_ref[f] for f in range(families)], axis=1)
            hidden = jnp.dot(mixing, stacked, preferred_element_type=F32)
        else:
            nothing = jnp.zeros((modes, 256), BF)
            parts = []
            for number, (one, other) in enumerate(pairs):
                part = slice(256 * number, 256 * number + 256)
                ours = jnp.where(family[:, part] == one, 1.0, 0.0)
                ours = jnp.broadcast_to(ours, (modes, 256)).astype(BF) > jnp.array(0.5, BF)
                mine = active[:, part]
                stacked = jnp.concatenate([jnp.where(ours, mine, nothing), jnp.where(ours, nothing, mine)], axis=0)
                mixing = jnp.concatenate([mid_ref[one], mid_ref[other]], axis=1)
                parts.append(jnp.dot(mixing, stacked, preferred_element_type=F32))
            hidden = jnp.concatenate(parts, axis=1)
        bounded = jnp.tanh(hidden).astype(BF)
        both = jnp.concatenate([bounded, bounded * bounded], axis=0)
        result = jnp.dot(out_ref[...], both, preferred_element_type=F32)
        result = result[: 4 * families] + result[4 * families :]
        owner = lax.shift_right_logical(lax.broadcasted_iota(jnp.int32, (4 * families, width), 0), 2)
        result = jnp.where(owner == family, result, 0.0)
        total = result[:4]
        for f in range(1, families):
            total = total + result[4 * f : 4 * f + 4]
        for i, (a, x) in enumerate(spots):
            answer_ref[:, a, x, :] = total[:, i * 128 : (i + 1) * 128]

    if info_ref is None:
        evaluate(None)
        return
    first = pl.program_id(0) * (step // 2)
    pairs, more = [], 0
    for a in range(step // 2):
        for x in planes:
            pairs.append((info_ref[x, first + a], info_ref[x, 16 + first + a]))
            more = more + info_ref[x, 32 + first + a]

    @pl.when(more == 0)
    def _():
        evaluate(pairs)

    @pl.when(more != 0)
    def _():
        evaluate(None)


def cells(strain, code, packed, families, step, planes, *edges, info=None):
    weight_in, weight_mid, weight_out = packed
    count = code.shape[0]
    planes = tuple(planes)
    points = count * len(planes) * 128
    modes = weight_in.shape[0]

    def whole(array):
        return pl.BlockSpec(array.shape, lambda i, *_: (0,) * array.ndim)

    def kernel(*refs):
        if info is None:
            cells_kernel(families, planes, *refs)
        else:
            cells_kernel(families, planes, *refs[1:], info_ref=refs[0])

    scalars = () if info is None else (info,)
    return pl.pallas_call(
        kernel,
        grid_spec=pltpu.PrefetchScalarGridSpec(
            num_scalar_prefetch=len(scalars),
            grid=(count // step,),
            in_specs=[
                pl.BlockSpec((3, step, 8, 128), lambda i, *_: (0, i, 0, 0)),
                pl.BlockSpec((step, 8, 128), lambda i, *_: (i, 0, 0)),
                whole(weight_in),
                whole(weight_mid),
                whole(weight_out),
            ]
            + [pl.BlockSpec((1, 128), lambda i, *_: (0, 0)) for _ in edges[:1]]
            + [pl.BlockSpec((1, 8, 128), lambda i, *_: (count + i, 0, 0)) for _ in edges[1:]],
            out_specs=pl.BlockSpec((4, step, 8, 128), lambda i, *_: (0, i, 0, 0)),
        ),
        out_shape=jax.ShapeDtypeStruct((4, count, 8, 128), F32),
        compiler_params=pltpu.CompilerParams(vmem_limit_bytes=48 * 2**20),
        cost_estimate=pl.CostEstimate(
            flops=2 * points * modes * modes * (families + 1), bytes_accessed=points * 32, transcendentals=2 * points * modes
        ),
        name="cells",
    )(*scalars, strain, code, weight_in, weight_mid, weight_out, *edges)


def global_sum(value):
    count = 1
    for axis in AXES:
        count = count * lax.axis_size(axis)
    spread = jnp.broadcast_to(value.reshape(1, 1), (count, 128))
    return jnp.sum(lax.all_to_all(spread, AXES, 0, 0, tiled=True)[:, 0])


def widened(cells_, axis, dim, width, closed):
    count = lax.axis_size(axis)
    ends = count if closed else count - 1
    head = lax.slice_in_dim(cells_, 0, width, axis=dim)
    tail = lax.slice_in_dim(cells_, cells_.shape[dim] - width, cells_.shape[dim], axis=dim)
    before = lax.ppermute(tail, axis, [(i, (i + 1) % count) for i in range(ends)])
    after = lax.ppermute(head, axis, [((i + 1) % count, i) for i in range(ends)])
    return jnp.concatenate([before, cells_, after], axis=dim)


HALOS = (("blk", True), ("micro", False), ("slab", False))


def widened_all(field, width):
    return [widened(field, axis, dim, width, closed) for dim, (axis, closed) in enumerate(HALOS)]


def difference(field, dim):
    length = field.shape[dim]
    return (lax.slice_in_dim(field, 2, length, axis=dim) - lax.slice_in_dim(field, 0, length - 2, axis=dim)) * 0.5


def plain_body(
    displacement, load_field, foundation, plastic_flags, point_slot, family_in, family_mid, family_out, family_tan
):
    size_x, size_y, size_z = displacement.shape
    points = size_x * size_y * size_z
    families = family_in.shape[0]
    capacity = points // 2
    packed = pack_families(family_in, family_mid, family_out, family_tan)
    strain = [difference(w, dim) for dim, w in enumerate(widened_all(displacement, 1))]
    code = 2 * (point_slot // capacity) + plastic_flags
    tiles = points // 1024
    answers = cells(jnp.stack(strain).reshape(3, tiles, 8, 128), code.reshape(tiles, 8, 128), packed, families, 2, range(8))
    answers = answers.reshape(4, size_x, size_y, size_z)
    tangents = widened_all(0.5 + answers[3], 1)
    divergence = sum(
        difference(widened(answers[dim], axis, dim, 1, closed), dim) for dim, (axis, closed) in enumerate(HALOS)
    )
    rhs = load_field - foundation * displacement + divergence
    solution_ = jnp.zeros_like(rhs)
    residual = rhs
    direction = rhs
    current = global_sum(jnp.sum(residual * residual))
    for _ in range(ITERS):
        total = sum(
            difference(tangents[dim] * difference(w, dim), dim) for dim, w in enumerate(widened_all(direction, 2))
        )
        image = foundation * direction - total
        alpha = current / global_sum(jnp.sum(direction * image))
        solution_ = solution_ + alpha * direction
        residual = residual - alpha * image
        following = global_sum(jnp.sum(residual * residual))
        direction = residual + following / current * direction
        current = following
    return displacement + solution_, residual


VMEM = pl.BlockSpec(memory_space=pltpu.VMEM)
GROUP = ("blk", "micro")


def call(kernel, out_shapes, scratch, name, *args, grid=(), ins=None, outs=None):
    return pl.pallas_call(
        kernel,
        out_shape=[jax.ShapeDtypeStruct(shape, dtype) for shape, dtype in out_shapes],
        grid=grid,
        in_specs=ins or [VMEM] * len(args),
        out_specs=outs or [VMEM] * len(out_shapes),
        scratch_shapes=scratch,
        compiler_params=pltpu.CompilerParams(vmem_limit_bytes=40 * 2**20),
        name=name,
    )(*args)


def regroup(tiles):
    group = lax.broadcasted_iota(jnp.int32, (8, 128), 1) // 32
    result = []
    for a in range(4):
        tile = tiles[0]
        for m in range(4):
            shift = (m - a) * 32 % 128
            moved = pltpu.roll(tiles[m], shift, 1) if shift else tiles[m]
            tile = moved if m == 0 else jnp.where(group == m, moved, tile)
        result.append(tile)
    return result


def place(slab, position, peers):
    return position + slab * (peers - 1 - 2 * position)


def whereabouts(peers):
    across = lax.axis_size("micro")
    b, m, slab = lax.axis_index("blk"), lax.axis_index("micro"), lax.axis_index("slab")
    position = place(slab, b * across + jnp.where(b % 2 == 0, m, across - 1 - m), peers)
    return (slab == 0) & (position == 0), (slab == 1) & (position == peers - 1), position % 2 == 0


def spread_kernel(path, capacity, u_ref, load_ref, found_ref, slot_ref, flag_ref, send_ref, turned):
    peers = len(path)
    slab = lax.axis_index("slab")
    code = flag_ref[...]
    for family in range(1, 4):
        code = code + jnp.where(slot_ref[...] >= family * capacity, 2, 0)
    rest = load_ref[...] - found_ref[...] * u_ref[...]
    for number, value in enumerate((u_ref[...], code.astype(F32), found_ref[...], rest)):
        turned[number] = jnp.transpose(value.reshape(128, 128))
    for target in range(peers):
        start = pl.multiple_of(8 * place(slab, path[target], peers), 8)
        for number in range(4):
            send_ref[target, 0, number] = turned[number, pl.ds(start, 8), :]


def beside(tile, low, high):
    row = lax.broadcasted_iota(jnp.int32, (8, 128), 0)
    after = jnp.where(row == 7, jnp.broadcast_to(high, (8, 128)), pltpu.roll(tile, 7, 0))
    before = jnp.where(row == 0, jnp.broadcast_to(low, (8, 128)), pltpu.roll(tile, 1, 0))
    return after, before


def radial(tile):
    lane = lax.broadcasted_iota(jnp.int32, tile.shape, tile.ndim - 1)
    after = jnp.where(lane == 127, 0.0, pltpu.roll(tile, 127, tile.ndim - 1))
    before = jnp.where(lane == 0, 0.0, pltpu.roll(tile, 1, tile.ndim - 1))
    return (after - before) * 0.5


def row_of(at):
    return at % 8 // 2 * 8 + at // 8 * 2 + at % 2


def collect_kernel(around, tan_ref, recv_ref, strain_ref, code_ref, found_ref, rest_ref, chip_ref, far_ref, scale_ref, u):
    _, _, even = whereabouts(recv_ref.shape[0])
    typical = jnp.sum(jnp.sum(tan_ref[...], axis=1, keepdims=True), axis=0, keepdims=True) / tan_ref.shape[0]
    centre = jnp.broadcast_to(1.1 + 1.4 * (0.5 + 0.33 * typical), (8, 128))
    row = lax.broadcasted_iota(jnp.int32, (8, 128), 0)
    scale_ref[...] = jnp.where(row == 0, centre, jnp.where(row == 1, 1.0 / (centre - 0.4), centre - 0.4))
    for b in range(around // 8):
        for half in range(2):
            for number in range(4):
                tiles = regroup([recv_ref[4 * b + m, half, number] for m in range(4)])
                for a in range(4):
                    at = 8 * b + 4 * half + a
                    if number == 0:
                        u[at] = tiles[a]
                    elif number == 1:
                        code_ref[at] = tiles[a].astype(jnp.int32)
                    elif number == 2:
                        rows = pl.ds(row_of(at), 8, stride=around)
                        found_ref[rows, :] = tiles[a]
                    else:
                        rest_ref[at] = tiles[a]
    nothing = jnp.zeros((1, 128), F32)
    for at in range(around):
        tile = u[at]
        strain_ref[0, at] = (u[(at + 1) % around] - u[(at - 1) % around]) * 0.5
        strain_ref[1, at] = radial(tile)
        after, before = beside(tile, nothing, nothing)
        strain_ref[2, at] = (after - before) * 0.5
        chip_ref[around + at // 8, pl.ds(at % 8, 1), :] = tile[7:8]
        far_ref[around + at // 8, pl.ds(at % 8, 1), :] = tile[0:1]
    for index in range(around):
        value = found_ref[8 * index : 8 * index + 8, :]
        chip_ref[index] = value
        far_ref[index] = value
    for index in range(around, around + around // 8):
        bottom, top = far_ref[index], chip_ref[index]
        chip_ref[index] = jnp.where(even, top, bottom)
        far_ref[index] = jnp.where(even, bottom, top)


def network(count):
    pairs = []
    p = 1
    while p < count:
        k = p
        while k >= 1:
            for j in range(k % p, count - k, 2 * k):
                for i in range(j, min(j + k, count - k)):
                    if i // (2 * p) == (i + k) // (2 * p):
                        pairs.append((i, i + k))
            k //= 2
        p *= 2
    return pairs


def sort_tiles(keys, *carried):
    keys, carried = list(keys), [list(c) for c in carried]
    for i, j in network(len(keys)):
        wrong = keys[i] > keys[j]
        keys[i], keys[j] = jnp.minimum(keys[i], keys[j]), jnp.maximum(keys[i], keys[j])
        for c in carried:
            c[i], c[j] = jnp.where(wrong, c[j], c[i]), jnp.where(wrong, c[i], c[j])
    return keys, carried


def take(tile, index):
    return jnp.take_along_axis(tile, index, axis=1, mode="promise_in_bounds")


def arrange_kernel(around, strain_ref, code_ref, sorted_ref, sorted_code_ref, rank_ref, origin_ref, info_ref):
    lane = lax.broadcasted_iota(jnp.int32, (8, 128), 1)
    right = lax.shift_right_logical
    keys, strains = [], [[], [], []]
    for at in range(around):
        code = code_ref[at]
        shift = right(code, 1) * 8
        counts = lax.shift_left(jnp.ones((8, 128), jnp.int32), shift)
        for step in (1, 2, 4, 8, 16, 32, 64):
            counts = counts + jnp.where(lane >= step, pltpu.roll(counts, step, 1), 0)
        total = jnp.broadcast_to(counts[:, 127:128], (8, 128))
        first = total & 255
        second = first + (right(total, 8) & 255)
        third = second + (right(total, 16) & 255)

        def start(family):
            return jnp.where(
                family < 2, jnp.where(family < 1, 0, first), jnp.where(family < 3, second, third)
            )

        turn = (at % 8 * 16 + at // 8 * 4) % 128
        rank_ref[at] = (start(right(code, 1)) + (right(counts, shift) & 255) + (turn - 1)) & 127
        spot = (lane + (128 - turn)) & 127
        family = (
            jnp.where(spot >= first, 1, 0) + jnp.where(spot >= second, 1, 0) + jnp.where(spot >= third, 1, 0)
        )
        wanted = spot - start(family)
        shift = family * 8
        source = jnp.zeros((8, 128), jnp.int32)
        for step in (64, 32, 16, 8, 4, 2, 1):
            seen = right(take(counts, source + (step - 1)), shift) & 255
            source = jnp.where(seen <= wanted, source + step, source)
        moved = take(code, source)
        keys.append(lax.shift_left(right(moved, 1), jnp.full((8, 128), 6, jnp.int32)) + (2 * at) + (moved & 1))
        for j in range(3):
            strains[j].append(take(strain_ref[j, at], source))
    keys, strains = sort_tiles(keys, *strains)
    info = jnp.zeros((8, 128), jnp.int32)
    for at in range(around):
        family = right(keys[at], 6)
        sorted_code_ref[at] = 2 * family + (keys[at] & 1)
        origin_ref[at] = right(keys[at], 1) & 31
        for j in range(3):
            sorted_ref[j, at] = strains[j][at]
        if at % 2:
            before = right(keys[at - 1], 6)
            low = jnp.min(jnp.minimum(before, family), axis=1, keepdims=True)
            high = jnp.max(jnp.maximum(before, family), axis=1, keepdims=True)
            low, high = jnp.broadcast_to(low, (8, 128)), jnp.broadcast_to(high, (8, 128))
            odd = jnp.where((family != low) & (family != high), 1, 0) + jnp.where((before != low) & (before != high), 1, 0)
            odd = jnp.broadcast_to(jnp.max(odd, axis=1, keepdims=True), (8, 128))
            for number, value in enumerate((low, high, odd)):
                info = jnp.where(lane == 16 * number + at // 2, value, info)
    info_ref[...] = info


def rhs_kernel(around, peers, first_ref, outer_ref, second_ref, rank_ref, origin_ref, rest_ref, chip_ref, far_ref, own_ref, low_ref, high_ref, answers):
    _, _, even = whereabouts(peers)
    for index in range(around // 8):
        low_ref[index] = jnp.where(even, far_ref[index], chip_ref[index])
        high_ref[index] = jnp.where(even, chip_ref[index], far_ref[index])
    row = lax.broadcasted_iota(jnp.int32, (8, 128), 0)
    rim = (row == 0) | (row == 7)

    moved = [[jnp.where(row < 4, first_ref[j, at], second_ref[j, at]) for at in range(around)] for j in range(4)]
    _, moved = sort_tiles([origin_ref[at] for at in range(around)], *moved)
    for at in range(around):
        for j in range(4):
            answers[j, at] = jnp.where(rim, outer_ref[j, at], take(moved[j][at], rank_ref[at]))

    def answer(number, at):
        return answers[number, at]

    cycle = [answer(0, at) for at in range(around)]
    for at in range(around):
        low = low_ref[at // 8, pl.ds(at % 8, 1), :]
        high = high_ref[at // 8, pl.ds(at % 8, 1), :]
        after, before = beside(answer(2, at), low, high)
        divergence = (cycle[(at + 1) % around] - cycle[(at - 1) % around]) * 0.5
        divergence = divergence + radial(answer(1, at)) + (after - before) * 0.5
        rows = pl.ds(row_of(at), 8, stride=around)
        own_ref[0, rows, :] = rest_ref[at] + divergence
        own_ref[1, rows, :] = 0.5 + answer(3, at)


HALF = ITERS // 2
MOST_LOST = 1.0e5


def tile(plane, quarter):
    return slice(32 * plane + 8 * quarter, 32 * plane + 8 * quarter + 8)


def three(peers, own_ref, chip_ref, far_ref, put):
    _, _, even = whereabouts(peers)
    for plane in range(8):
        for quarter in range(4):
            rows = tile(plane, quarter)
            chip, far = chip_ref[rows, :], far_ref[rows, :]
            put(plane, quarter, jnp.where(even, far, chip))
            put(plane + 8, quarter, own_ref[rows, :])
            put(plane + 16, quarter, jnp.where(even, chip, far))


def within_plane(here):
    lane = lax.broadcasted_iota(jnp.int32, (8, 128), 1)
    even_row = lax.broadcasted_iota(jnp.int32, (8, 128), 0) % 2 == 0
    up = [pltpu.roll(value, 7, 0) for value in here]
    down = [pltpu.roll(value, 1, 0) for value in here]
    result = []
    for quarter in range(4):
        after = jnp.where(even_row, up[quarter], down[quarter + 1] if quarter < 3 else up[0])
        before = jnp.where(even_row, up[quarter - 1] if quarter else down[3], down[quarter])
        outer = jnp.where(lane == 127, 0.0, pltpu.roll(here[quarter], 127, 1))
        inner = jnp.where(lane == 0, 0.0, pltpu.roll(here[quarter], 1, 1))
        out = jnp.where(lane >= 126, 0.0, outer)
        result.append((after, out, pltpu.roll(out, 2, 1), (after + before) + (outer + inner)))
    return result


def own_kernel(scale_ref, tan_ref, found_ref, main_ref, after_ref, out_ref, back_ref):
    centre, inverse = scale_ref[0:1, :], scale_ref[1:2, :]
    for plane in range(8):
        parts = within_plane([tan_ref[tile(plane, quarter), :] * (0.25 * inverse) for quarter in range(4)])
        for quarter, (after, out, back, total) in enumerate(parts):
            rows = tile(plane, quarter)
            main_ref[rows, :] = (found_ref[rows, :] - centre) * inverse + total
            after_ref[rows, :] = after
            out_ref[rows, :] = out
            back_ref[rows, :] = back


def operator_kernel(
    peers, scale_ref, tan_ref, tan_chip_ref, tan_far_ref, own_main_ref, own_after_ref, own_out_ref, own_back_ref,
    found_chip_ref, found_far_ref, tan, main, after, out, back
):
    centre, inverse = scale_ref[0:1, :], scale_ref[1:2, :]
    _, _, even = whereabouts(peers)

    def put_tan(plane, quarter, value):
        tan[tile(plane, quarter), :] = value * (0.25 * inverse)

    three(peers, tan_ref, tan_chip_ref, tan_far_ref, put_tan)
    for plane in range(2, 22):
        inside = 8 <= plane < 16
        if not inside:
            parts = within_plane([tan[tile(plane, quarter), :] for quarter in range(4)])
        for quarter in range(4):
            rows = tile(plane, quarter)
            if inside:
                own = tile(plane - 8, quarter)
                total = own_main_ref[own, :]
                after[rows, :] = own_after_ref[own, :]
                out[rows, :] = own_out_ref[own, :]
                back[rows, :] = own_back_ref[own, :]
            else:
                after[rows, :], out[rows, :], back[rows, :], total = parts[quarter]
                there = tile(plane % 8, quarter)
                chip, far = found_chip_ref[there, :], found_far_ref[there, :]
                found = jnp.where(even, far, chip) if plane < 8 else jnp.where(even, chip, far)
                total = total + (found - centre) * inverse
            axial = tan[tile(plane + 1, quarter), :] + tan[tile(plane - 1, quarter), :]
            main[rows, :] = total + axial


def basis_kernel(peers, last, *refs):
    if last:
        tan, main, after, out, back, seed_ref, seed_chip_ref, seed_far_ref, earlier_ref, previous_ref, *refs = refs
        own_ref, sums_ref, vectors = refs
    else:
        operator_refs, (seed_ref, seed_chip_ref, seed_far_ref), refs = refs[:10], refs[10:13], refs[13:]
        own_ref, sums_ref, tan, main, after, out, back, vectors = refs
        operator_kernel(peers, *operator_refs, tan, main, after, out, back)
    is_first, is_last, _ = whereabouts(peers)

    def put_seed(plane, quarter, value):
        vectors[0, tile(plane, quarter), :] = value

    three(peers, seed_ref, seed_chip_ref, seed_far_ref, put_seed)

    def axial(between, plane, degree, quarter):
        term = tan[tile(between, quarter), :] * vectors[degree, tile(plane, quarter), :]
        if between == 8 or between == 15:
            term = jnp.where(is_first if between == 8 else is_last, 0.0, term)
        return term

    def apply(degree, plane, quarter):
        rows = tile(plane, quarter)
        value = vectors[degree, rows, :]
        result = main[rows, :] * value
        if quarter < 3:
            result = result - after[rows, :] * vectors[degree, tile(plane, quarter + 1), :]
        else:
            result = result - after[rows, :] * pltpu.roll(vectors[degree, tile(plane, 0), :], 6, 0)
        before = tile(plane, (quarter - 1) % 4)
        product = after[before, :] * vectors[degree, before, :]
        result = result - (product if quarter else pltpu.roll(product, 2, 0))
        result = result - out[rows, :] * pltpu.roll(value, 126, 1) - back[rows, :] * pltpu.roll(value, 2, 1)
        return result - axial(plane + 1, plane + 2, degree, quarter) - axial(plane - 1, plane - 2, degree, quarter)

    for degree in range(1, HALF + 1):
        for plane in range(2 * degree, 24 - 2 * degree):
            for quarter in range(4):
                value = apply(degree - 1, plane, quarter)
                if degree > 1:
                    value = value + value - vectors[degree - 2, tile(plane, quarter), :]
                vectors[degree, tile(plane, quarter), :] = value
    own_tiles = [(tile(plane, quarter), tile(plane + 8, quarter)) for plane in range(8) for quarter in range(4)]
    pairs = []
    if last:
        for degree in range(1, HALF + 1):
            for rows, wide_rows in own_tiles:
                value = vectors[degree, wide_rows, :]
                own_ref[degree - 1, rows, :] = value + value - earlier_ref[HALF - degree, rows, :]
            before = earlier_ref.at[HALF] if degree == 1 else own_ref.at[degree - 2]
            pairs += [(before, own_ref.at[degree - 1]), (own_ref.at[degree - 1], own_ref.at[degree - 1])]
    else:
        for degree in range(HALF + 1):
            for rows, wide_rows in own_tiles:
                own_ref[degree, rows, :] = vectors[degree, wide_rows, :]
            if degree:
                pairs.append((own_ref.at[degree - 1], own_ref.at[degree]))
            pairs.append((own_ref.at[degree], own_ref.at[degree]))
    column = lax.broadcasted_iota(jnp.int32, (1, 128), 1)
    sums = previous_ref[0:1, :] if last else jnp.zeros((1, 128), F32)
    for number, (left, right) in enumerate(pairs):
        total = tree([left[rows, :] * right[rows, :] for rows, _ in own_tiles])
        entry = jnp.sum(jnp.sum(total, axis=0, keepdims=True), axis=1, keepdims=True)
        place_of = number + (2 * HALF + 1 if last else 0)
        sums = jnp.where(column == place_of, jnp.broadcast_to(entry, (1, 128)), sums)
    sums_ref[...] = jnp.broadcast_to(sums, sums_ref.shape)


def unpack_gram(all_ref, total):
    row = jnp.sum(all_ref[...], axis=0, keepdims=True)
    moments = []
    for number in range(2 * total - 1):
        entry = jnp.broadcast_to(row[:, number : number + 1], (1, 128))
        moments.append(entry if number < 2 else entry + entry - moments[number % 2])
    gram = {}
    for i in range(total):
        for j in range(i, total):
            gram[i, j] = gram[j, i] = 0.5 * (moments[i + j] + moments[j - i])
    return gram


def tree(terms):
    while len(terms) > 1:
        terms = [a + b for a, b in zip(terms[::2], terms[1::2])] + ([terms[-1]] if len(terms) % 2 else [])
    return terms[0]


def dot(gram, left, right):
    return tree(
        [
            a * tree([gram[i, j] * b for j, b in enumerate(right) if b is not None])
            for i, a in enumerate(left)
            if a is not None
        ]
    )


def axpy(scale, left, right):
    result = []
    for a, b in zip(left, right, strict=True):
        a = None if a is None else (a if scale is None else scale * a)
        result.append(b if a is None else (a if b is None else b + a))
    return result


def times_operator(vector, centre, half_width):
    total = len(vector)
    result = [None] * total
    half = 0.5 * half_width

    def add(index, term):
        result[index] = term if result[index] is None else result[index] + term

    for j, c in enumerate(vector):
        if c is None:
            continue
        add(j, centre * c)
        add(j + 1, (half if j else half_width) * c)
        if j:
            add(j - 1, half * c)
    return result


def iterate(gram, total, centre, half_width):
    residual = [jnp.ones((1, 128), F32)] + [None] * (total - 1)
    direction = residual
    change = [None] * total
    norms = [jnp.sqrt(gram[i, i]) for i in range(total)]
    current = gram[0, 0]
    worst = jnp.zeros((1, 128), F32)
    for step in range(ITERS):
        image = times_operator(direction, centre, half_width)
        alpha = current / dot(gram, direction, image)
        change = axpy(alpha, direction, change)
        residual = axpy(-alpha, image, residual)
        following = dot(gram, residual, residual)
        bound = tree([jnp.abs(c) * n for c, n in zip(residual, norms, strict=True) if c is not None])
        worst = jnp.maximum(worst, bound * bound / following)
        worst = jnp.where(following > 0.0, worst, jnp.inf)
        if step < ITERS - 1:
            direction = axpy(following / current, direction, residual)
        current = following
    return change, residual, worst


def last_kernel(around, scale_ref, all_ref, early_ref, late_ref, send_ref, worst_ref, results):
    total = 2 * HALF + 1
    change, residual, worst = iterate(unpack_gram(all_ref, total), total, scale_ref[0:1, :], scale_ref[2:3, :])
    worst_ref[...] = jnp.broadcast_to(worst, (8, 128))
    for number, part in enumerate((change, residual)):
        part = [None if c is None else jnp.broadcast_to(c, (8, 128)) for c in part]
        for start in range(0, 8 * around, 8):
            rows = slice(start, start + 8)
            results[number, rows, :] = tree(
                [
                    c * (early_ref[index, rows, :] if index <= HALF else late_ref[index - HALF - 1, rows, :])
                    for index, c in enumerate(part)
                    if c is not None
                ]
            )
        for b in range(around // 8):
            for half in range(2):
                tiles = [
                    results[number, pl.ds(row_of(8 * b + 4 * half + a), 8, stride=around), :] for a in range(4)
                ]
                tiles = regroup(tiles)
                for m in range(4):
                    send_ref[4 * b + m, half, number] = tiles[m]


def deliver_kernel(path, u_ref, recv_ref, worst_ref, instead_updated_ref, instead_residual_ref, *refs):
    updated_ref, residual_ref, turned = refs
    slab = lax.axis_index("slab")
    for source in range(recv_ref.shape[0]):
        start = pl.multiple_of(8 * place(slab, path[source], len(path)), 8)
        for index in range(2):
            turned[index, pl.ds(start, 8), :] = recv_ref[source, 0, index]
    good = jnp.broadcast_to(worst_ref[0:1, :] < MOST_LOST, (32, 128))
    change = jnp.transpose(turned[0]).reshape(4, 32, 128)
    residual = jnp.transpose(turned[1]).reshape(4, 32, 128)
    for i in range(4):
        updated_ref[i] = jnp.where(good, u_ref[i] + change[i], instead_updated_ref[i])
        residual_ref[i] = jnp.where(good, residual[i], instead_residual_ref[i])


def sliced_body(
    displacement, load_field, foundation, plastic_flags, point_slot, family_in, family_mid, family_out, family_tan
):
    size_x, size_y, size_z = displacement.shape
    families = family_in.shape[0]
    along, across = lax.axis_size("blk"), lax.axis_size("micro")
    peers = along * across
    around = size_x * along
    everyone = peers * lax.axis_size("slab")
    path = [b * across + (m if b % 2 == 0 else across - 1 - m) for b in range(along) for m in range(across)]
    _, _, even = whereabouts(peers)
    spots = [0] * everyone
    for b in range(along):
        for s in range(2):
            for m in range(across):
                spots[place(s, path[b * across + m], peers) + peers * s] = (b * 2 + s) * across + m

    def swap(first, value):
        pairs = [(spots[i], spots[i + 1]) for i in range(first, everyone - 1, 2)]
        return lax.ppermute(value, AXES, pairs + [(b, a) for a, b in pairs])

    def neighbours(to_chip, to_far):
        far = swap(1, to_far)
        return swap(0, to_chip), far

    packed = pack_families(family_in, family_mid, family_out, family_tan)
    capacity = size_x * size_y * size_z // 2
    halves = pl.BlockSpec((4, 32, 128), lambda i: (i, 0, 0))
    (send,) = call(
        lambda *refs: spread_kernel(path, capacity, *refs),
        [((peers, 2, 4, 8, 128), F32)], [pltpu.VMEM((4, 128, 128), F32)], "spread",
        displacement, load_field, foundation, point_slot, plastic_flags,
        grid=(2,), ins=[halves] * 5, outs=[pl.BlockSpec((peers, 1, 4, 8, 128), lambda i: (0, i, 0, 0, 0))],
    )
    recv = lax.all_to_all(send, GROUP, 0, 0, tiled=True)
    field = (around, 8, 128)
    edge = (around // 8, 8, 128)
    rows = (8 * around, 128)
    message = (around + around // 8, 8, 128)
    strain, code, found, rest, to_chip, to_far, scale = call(
        lambda *refs: collect_kernel(around, *refs),
        [((3,) + field, F32), (field, jnp.int32), (rows, F32), (field, F32), (message, F32), (message, F32), ((8, 128), F32)],
        [pltpu.VMEM(field, F32)], "collect", family_tan, recv,
    )
    chip, far = neighbours(to_chip, to_far)
    grouped, grouped_code, rank, origin, info = call(
        lambda *refs: arrange_kernel(around, *refs),
        [((3,) + field, F32), (field, jnp.int32), (field, jnp.int32), (field, jnp.int32), ((8, 128), jnp.int32)],
        [], "arrange", strain, code,
    )
    first = cells(grouped, grouped_code, packed, families, 8, (1, 2, 3), info=info)
    outer = cells(strain, code, packed, families, 8, (0, 7), jnp.broadcast_to(even.astype(jnp.int32), (1, 128)), chip, far)
    top, bottom = outer[2, :, 7].reshape(edge), outer[2, :, 0].reshape(edge)
    edge_chip, edge_far = neighbours(jnp.where(even, top, bottom), jnp.where(even, bottom, top))
    grouped, outer = lax.optimization_barrier((grouped, outer))
    second = cells(grouped, grouped_code, packed, families, 8, (4, 5, 6), info=info)
    (own,) = call(
        lambda *refs: rhs_kernel(around, peers, *refs), [((2,) + rows, F32)], [pltpu.VMEM(edge, F32)] * 2 + [pltpu.VMEM((4,) + field, F32)], "rhs",
        first, outer, second, rank, origin, rest, edge_chip, edge_far,
    )
    own_chip, own_far = neighbours(own, own)

    tall = (24 * around, 128)
    vectors = [pltpu.VMEM((HALF + 1,) + tall, F32)]
    inside = call(
        own_kernel, [(rows, F32)] * 4, [], "own", scale, own[1], found,
    )
    early, sums, *operator = call(
        lambda *refs: basis_kernel(peers, False, *refs),
        [((HALF + 1,) + rows, F32), ((8, 128), F32)] + [(tall, F32)] * 5, vectors, "basis",
        scale, own[1], own_chip[1], own_far[1], *inside, chip[:around].reshape(rows), far[:around].reshape(rows),
        own[0], own_chip[0], own_far[0],
    )
    late, sums = call(
        lambda *refs: basis_kernel(peers, True, *refs), [((HALF,) + rows, F32), ((everyone, 128), F32)], vectors, "basis",
        *operator, early[HALF], *neighbours(early[HALF], early[HALF]), early, sums,
    )
    sums = lax.all_to_all(sums, AXES, 0, 0, tiled=True)
    send, worst = call(
        lambda *refs: last_kernel(around, *refs),
        [((peers, 2, 2, 8, 128), F32), ((8, 128), F32)], [pltpu.VMEM((2,) + rows, F32)], "last", scale, sums, early, late,
    )
    recv = lax.all_to_all(send, GROUP, 0, 0, tiled=True)
    inputs = (
        displacement, load_field, foundation, plastic_flags, point_slot, family_in, family_mid, family_out, family_tan
    )
    good, recv = lax.optimization_barrier((worst[0, 0] < MOST_LOST, recv))
    instead = lax.cond(good, lambda: (jnp.zeros_like(displacement),) * 2, lambda: plain_body(*inputs))
    shape = displacement.shape
    return call(
        lambda *refs: deliver_kernel(path, *refs), [(shape, F32), (shape, F32)], [pltpu.VMEM((2, 128, 128), F32)],
        "deliver", displacement, recv, worst, *instead, grid=(2,), outs=[halves] * 2,
        ins=[
            halves,
            pl.BlockSpec((peers, 1, 2, 8, 128), lambda i: (0, i, 0, 0, 0)),
            pl.BlockSpec((8, 128), lambda i: (0, 0)),
            halves,
            halves,
        ],
    )


def body(*inputs):
    size_x, size_y, size_z = inputs[0].shape
    along, across = lax.axis_size("blk"), lax.axis_size("micro")
    fits = (
        (size_x, size_y, size_z) == (8, 32, 128)
        and across == 4
        and size_z == 8 * along * across
        and lax.axis_size("slab") == 2
        and inputs[5].shape[0] == 4
    )
    if not fits:
        return plain_body(*inputs)
    return tuple(sliced_body(*inputs))


def solution(mesh):
    field = P("blk", "micro", "slab")
    return jax.shard_map(
        body,
        mesh=mesh,
        in_specs=(field,) * 5 + (P(),) * 4,
        out_specs=(field, field),
        check_vma=False,
    )
```

```python
import jax
import jax.numpy as jnp
from jax import lax
from jax.experimental import pallas as pl
from jax.experimental.pallas import tpu as pltpu
from jax.sharding import PartitionSpec as P

ITERS = 8
AXES = ("blk", "slab", "micro")
BF = jnp.bfloat16
F32 = jnp.float32


def split(value):
    high = lax.reduce_precision(value, 8, 7)
    return high.astype(BF), (value - high).astype(BF)


def pack_families(family_in, family_mid, family_out, family_tan):
    families, _, modes = family_in.shape
    spread = jnp.transpose(family_in, (2, 1, 0))
    spread = jnp.concatenate([spread, spread], axis=2).reshape(modes, 6 * families)
    high, low = split(spread)
    weight_in = jnp.concatenate([high, low], axis=1)
    none = jnp.zeros((families, 1, modes), BF)
    stress = jnp.concatenate([family_out, none], axis=1).reshape(4 * families, modes)
    weight_tan = jnp.broadcast_to(family_tan[:, :, None], (families, modes, 128))
    return weight_in, family_mid, stress, weight_tan


def cells_kernel(families, planes, strain_ref, code_ref, in_ref, mid_ref, out_ref, tan_ref, *refs, info_ref=None):
    *edges, answer_ref = refs
    modes = in_ref.shape[0]
    step = code_ref.shape[0]
    spots = [(a + i, x) for a in range(0, step, 2) for x in planes for i in range(2)]
    width = len(spots) * 128

    def evaluate(pairs):
        place = lax.broadcasted_iota(jnp.int32, (2 * families, 128), 0)
        column, family_row, flag_row = [], [], []
        for a, x in spots:
            code = code_ref[a, pl.ds(x, 1), :]
            family = lax.shift_right_logical(code, 1)
            picked = lax.rem(place, families) == jnp.broadcast_to(family, place.shape)
            pieces = []
            for j in range(3):
                value = strain_ref[j, a, pl.ds(x, 1), :]
                if edges and j == 2:
                    even, chip_ref, far_ref = edges
                    chip, far = chip_ref[0, pl.ds(a, 1), :], far_ref[0, pl.ds(a, 1), :]
                    beyond = jnp.where(even[...] == (1 if x == 7 else 0), chip, far) * 0.5
                    value = value - beyond if x == 0 else value + beyond
                value = jnp.broadcast_to(value, place.shape)
                high = value.astype(BF).astype(F32)
                piece = jnp.where(place < families, high, value - high)
                pieces.append(jnp.where(picked, piece, 0.0))
            column.append(jnp.concatenate(pieces, axis=0))
            family_row.append(family)
            flag_row.append(lax.bitwise_and(code, 1))
        spread = jnp.concatenate(column, axis=1).astype(BF)
        spread = jnp.concatenate([spread, spread], axis=0)
        family = jnp.concatenate(family_row, axis=1)
        flag = jnp.concatenate(flag_row, axis=1)
        modal = jnp.dot(in_ref[...], spread, preferred_element_type=F32)
        flagged = jnp.broadcast_to(flag, (modes, width)) > 0
        active = jnp.where(flagged, jnp.tanh(modal), modal).astype(BF)
        if pairs is None:
            wide = jnp.broadcast_to(family, (modes, width)).astype(BF)
            nothing = jnp.zeros_like(active)
            stacked = jnp.concatenate(
                [jnp.where(wide == jnp.array(f, BF), active, nothing) for f in range(families)], axis=0
            )
            mixing = jnp.concatenate([mid_ref[f] for f in range(families)], axis=1)
            hidden = jnp.dot(mixing, stacked, preferred_element_type=F32)
        else:
            nothing = jnp.zeros((modes, 256), BF)
            parts = []
            for number, (one, other) in enumerate(pairs):
                part = slice(256 * number, 256 * number + 256)
                ours = jnp.where(family[:, part] == one, 1.0, 0.0)
                ours = jnp.broadcast_to(ours, (modes, 256)).astype(BF) > jnp.array(0.5, BF)
                mine = active[:, part]
                stacked = jnp.concatenate([jnp.where(ours, mine, nothing), jnp.where(ours, nothing, mine)], axis=0)
                mixing = jnp.concatenate([mid_ref[one], mid_ref[other]], axis=1)
                parts.append(jnp.dot(mixing, stacked, preferred_element_type=F32))
            hidden = jnp.concatenate(parts, axis=1)
        bounded = jnp.tanh(hidden).astype(BF)
        result = jnp.dot(out_ref[...], bounded, preferred_element_type=F32)
        owner = lax.shift_right_logical(lax.broadcasted_iota(jnp.int32, (4 * families, width), 0), 2)
        result = jnp.where(owner == family, result, 0.0)
        total = result[:4]
        for f in range(1, families):
            total = total + result[4 * f : 4 * f + 4]
        for i, (a, x) in enumerate(spots):
            part = slice(i * 128, (i + 1) * 128)
            answer_ref[0:3, a, x, :] = total[0:3, part]
            square = bounded[:, part].astype(F32)
            square = square * square
            owner = jnp.broadcast_to(family_row[i], (modes, 128))
            if pairs is None:
                weight = tan_ref[0]
                for f in range(1, families):
                    weight = jnp.where(owner == f, tan_ref[f], weight)
            else:
                one, other = pairs[i // 2]
                weight = jnp.where(owner == one, tan_ref[one], tan_ref[other])
            answer_ref[3, a, pl.ds(x, 1), :] = jnp.sum(weight * square, axis=0, keepdims=True)

    if info_ref is None:
        evaluate(None)
        return
    first = pl.program_id(0) * (step // 2)
    pairs, more = [], 0
    for a in range(step // 2):
        for x in planes:
            pairs.append((info_ref[x, first + a], info_ref[x, 16 + first + a]))
            more = more + info_ref[x, 32 + first + a]

    @pl.when(more == 0)
    def _():
        evaluate(pairs)

    @pl.when(more != 0)
    def _():
        evaluate(None)


def cells(strain, code, packed, families, step, planes, *edges, info=None):
    weight_in, weight_mid, weight_out, weight_tan = packed
    count = code.shape[0]
    planes = tuple(planes)
    points = count * len(planes) * 128
    modes = weight_in.shape[0]

    def whole(array):
        return pl.BlockSpec(array.shape, lambda i, *_: (0,) * array.ndim)

    def kernel(*refs):
        if info is None:
            cells_kernel(families, planes, *refs)
        else:
            cells_kernel(families, planes, *refs[1:], info_ref=refs[0])

    scalars = () if info is None else (info,)
    return pl.pallas_call(
        kernel,
        grid_spec=pltpu.PrefetchScalarGridSpec(
            num_scalar_prefetch=len(scalars),
            grid=(count // step,),
            in_specs=[
                pl.BlockSpec((3, step, 8, 128), lambda i, *_: (0, i, 0, 0)),
                pl.BlockSpec((step, 8, 128), lambda i, *_: (i, 0, 0)),
                whole(weight_in),
                whole(weight_mid),
                whole(weight_out),
                whole(weight_tan),
            ]
            + [pl.BlockSpec((1, 128), lambda i, *_: (0, 0)) for _ in edges[:1]]
            + [pl.BlockSpec((1, 8, 128), lambda i, *_: (count + i, 0, 0)) for _ in edges[1:]],
            out_specs=pl.BlockSpec((4, step, 8, 128), lambda i, *_: (0, i, 0, 0)),
        ),
        out_shape=jax.ShapeDtypeStruct((4, count, 8, 128), F32),
        compiler_params=pltpu.CompilerParams(vmem_limit_bytes=48 * 2**20),
        cost_estimate=pl.CostEstimate(
            flops=2 * points * modes * modes * (families + 1), bytes_accessed=points * 32, transcendentals=2 * points * modes
        ),
        name="cells",
    )(*scalars, strain, code, weight_in, weight_mid, weight_out, weight_tan, *edges)


def global_sum(value):
    count = 1
    for axis in AXES:
        count = count * lax.axis_size(axis)
    spread = jnp.broadcast_to(value.reshape(1, 1), (count, 128))
    return jnp.sum(lax.all_to_all(spread, AXES, 0, 0, tiled=True)[:, 0])


def widened(cells_, axis, dim, width, closed):
    count = lax.axis_size(axis)
    ends = count if closed else count - 1
    head = lax.slice_in_dim(cells_, 0, width, axis=dim)
    tail = lax.slice_in_dim(cells_, cells_.shape[dim] - width, cells_.shape[dim], axis=dim)
    before = lax.ppermute(tail, axis, [(i, (i + 1) % count) for i in range(ends)])
    after = lax.ppermute(head, axis, [((i + 1) % count, i) for i in range(ends)])
    return jnp.concatenate([before, cells_, after], axis=dim)


HALOS = (("blk", True), ("micro", False), ("slab", False))


def widened_all(field, width):
    return [widened(field, axis, dim, width, closed) for dim, (axis, closed) in enumerate(HALOS)]


def difference(field, dim):
    length = field.shape[dim]
    return (lax.slice_in_dim(field, 2, length, axis=dim) - lax.slice_in_dim(field, 0, length - 2, axis=dim)) * 0.5


def plain_body(
    displacement, load_field, foundation, plastic_flags, point_slot, family_in, family_mid, family_out, family_tan
):
    size_x, size_y, size_z = displacement.shape
    points = size_x * size_y * size_z
    families = family_in.shape[0]
    capacity = points // 2
    packed = pack_families(family_in, family_mid, family_out, family_tan)
    strain = [difference(w, dim) for dim, w in enumerate(widened_all(displacement, 1))]
    code = 2 * (point_slot // capacity) + plastic_flags
    tiles = points // 1024
    answers = cells(jnp.stack(strain).reshape(3, tiles, 8, 128), code.reshape(tiles, 8, 128), packed, families, 2, range(8))
    answers = answers.reshape(4, size_x, size_y, size_z)
    tangents = widened_all(0.5 + answers[3], 1)
    divergence = sum(
        difference(widened(answers[dim], axis, dim, 1, closed), dim) for dim, (axis, closed) in enumerate(HALOS)
    )
    rhs = load_field - foundation * displacement + divergence
    solution_ = jnp.zeros_like(rhs)
    residual = rhs
    direction = rhs
    current = global_sum(jnp.sum(residual * residual))
    for _ in range(ITERS):
        total = sum(
            difference(tangents[dim] * difference(w, dim), dim) for dim, w in enumerate(widened_all(direction, 2))
        )
        image = foundation * direction - total
        alpha = current / global_sum(jnp.sum(direction * image))
        solution_ = solution_ + alpha * direction
        residual = residual - alpha * image
        following = global_sum(jnp.sum(residual * residual))
        direction = residual + following / current * direction
        current = following
    return displacement + solution_, residual


VMEM = pl.BlockSpec(memory_space=pltpu.VMEM)
GROUP = ("blk", "micro")


def call(kernel, out_shapes, scratch, name, *args, grid=(), ins=None, outs=None):
    return pl.pallas_call(
        kernel,
        out_shape=[jax.ShapeDtypeStruct(shape, dtype) for shape, dtype in out_shapes],
        grid=grid,
        in_specs=ins or [VMEM] * len(args),
        out_specs=outs or [VMEM] * len(out_shapes),
        scratch_shapes=scratch,
        compiler_params=pltpu.CompilerParams(vmem_limit_bytes=40 * 2**20),
        name=name,
    )(*args)


def regroup(tiles):
    group = lax.broadcasted_iota(jnp.int32, (8, 128), 1) // 32
    result = []
    for a in range(4):
        tile = tiles[0]
        for m in range(4):
            shift = (m - a) * 32 % 128
            moved = pltpu.roll(tiles[m], shift, 1) if shift else tiles[m]
            tile = moved if m == 0 else jnp.where(group == m, moved, tile)
        result.append(tile)
    return result


def place(slab, position, peers):
    return position + slab * (peers - 1 - 2 * position)


def whereabouts(peers):
    across = lax.axis_size("micro")
    b, m, slab = lax.axis_index("blk"), lax.axis_index("micro"), lax.axis_index("slab")
    position = place(slab, b * across + jnp.where(b % 2 == 0, m, across - 1 - m), peers)
    return (slab == 0) & (position == 0), (slab == 1) & (position == peers - 1), position % 2 == 0


def spread_kernel(path, capacity, u_ref, load_ref, found_ref, slot_ref, flag_ref, send_ref, turned):
    peers = len(path)
    slab = lax.axis_index("slab")
    code = flag_ref[...]
    for family in range(1, 4):
        code = code + jnp.where(slot_ref[...] >= family * capacity, 2, 0)
    rest = load_ref[...] - found_ref[...] * u_ref[...]
    for number, value in enumerate((u_ref[...], code.astype(F32), found_ref[...], rest)):
        turned[number] = jnp.transpose(value.reshape(128, 128))
    for target in range(peers):
        start = pl.multiple_of(8 * place(slab, path[target], peers), 8)
        for number in range(4):
            send_ref[target, 0, number] = turned[number, pl.ds(start, 8), :]


def beside(tile, low, high):
    row = lax.broadcasted_iota(jnp.int32, (8, 128), 0)
    after = jnp.where(row == 7, jnp.broadcast_to(high, (8, 128)), pltpu.roll(tile, 7, 0))
    before = jnp.where(row == 0, jnp.broadcast_to(low, (8, 128)), pltpu.roll(tile, 1, 0))
    return after, before


def radial(tile):
    lane = lax.broadcasted_iota(jnp.int32, tile.shape, tile.ndim - 1)
    after = jnp.where(lane == 127, 0.0, pltpu.roll(tile, 127, tile.ndim - 1))
    before = jnp.where(lane == 0, 0.0, pltpu.roll(tile, 1, tile.ndim - 1))
    return (after - before) * 0.5


def row_of(at):
    return at % 8 // 2 * 8 + at // 8 * 2 + at % 2


def collect_kernel(around, tan_ref, recv_ref, strain_ref, code_ref, found_ref, rest_ref, chip_ref, far_ref, scale_ref, u):
    _, _, even = whereabouts(recv_ref.shape[0])
    typical = jnp.sum(jnp.sum(tan_ref[...], axis=1, keepdims=True), axis=0, keepdims=True) / tan_ref.shape[0]
    centre = jnp.broadcast_to(1.1 + 1.4 * (0.5 + 0.33 * typical), (8, 128))
    row = lax.broadcasted_iota(jnp.int32, (8, 128), 0)
    scale_ref[...] = jnp.where(row == 0, centre, jnp.where(row == 1, 1.0 / (centre - 0.4), centre - 0.4))
    for b in range(around // 8):
        for half in range(2):
            for number in range(4):
                tiles = regroup([recv_ref[4 * b + m, half, number] for m in range(4)])
                for a in range(4):
                    at = 8 * b + 4 * half + a
                    if number == 0:
                        u[at] = tiles[a]
                    elif number == 1:
                        code_ref[at] = tiles[a].astype(jnp.int32)
                    elif number == 2:
                        rows = pl.ds(row_of(at), 8, stride=around)
                        found_ref[rows, :] = tiles[a]
                    else:
                        rest_ref[at] = tiles[a]
    nothing = jnp.zeros((1, 128), F32)
    for at in range(around):
        tile = u[at]
        strain_ref[0, at] = (u[(at + 1) % around] - u[(at - 1) % around]) * 0.5
        strain_ref[1, at] = radial(tile)
        after, before = beside(tile, nothing, nothing)
        strain_ref[2, at] = (after - before) * 0.5
        chip_ref[around + at // 8, pl.ds(at % 8, 1), :] = tile[7:8]
        far_ref[around + at // 8, pl.ds(at % 8, 1), :] = tile[0:1]
    for index in range(around):
        value = found_ref[8 * index : 8 * index + 8, :]
        chip_ref[index] = value
        far_ref[index] = value
    for index in range(around, around + around // 8):
        bottom, top = far_ref[index], chip_ref[index]
        chip_ref[index] = jnp.where(even, top, bottom)
        far_ref[index] = jnp.where(even, bottom, top)


def network(count):
    pairs = []
    p = 1
    while p < count:
        k = p
        while k >= 1:
            for j in range(k % p, count - k, 2 * k):
                for i in range(j, min(j + k, count - k)):
                    if i // (2 * p) == (i + k) // (2 * p):
                        pairs.append((i, i + k))
            k //= 2
        p *= 2
    return pairs


def sort_tiles(keys, *carried):
    keys, carried = list(keys), [list(c) for c in carried]
    for i, j in network(len(keys)):
        wrong = keys[i] > keys[j]
        keys[i], keys[j] = jnp.minimum(keys[i], keys[j]), jnp.maximum(keys[i], keys[j])
        for c in carried:
            c[i], c[j] = jnp.where(wrong, c[j], c[i]), jnp.where(wrong, c[i], c[j])
    return keys, carried


def take(tile, index):
    return jnp.take_along_axis(tile, index, axis=1, mode="promise_in_bounds")


def arrange_kernel(around, strain_ref, code_ref, sorted_ref, sorted_code_ref, rank_ref, origin_ref, info_ref):
    lane = lax.broadcasted_iota(jnp.int32, (8, 128), 1)
    right = lax.shift_right_logical
    keys, strains = [], [[], [], []]
    for at in range(around):
        code = code_ref[at]
        shift = right(code, 1) * 8
        counts = lax.shift_left(jnp.ones((8, 128), jnp.int32), shift)
        for step in (1, 2, 4, 8, 16, 32, 64):
            counts = counts + jnp.where(lane >= step, pltpu.roll(counts, step, 1), 0)
        total = jnp.broadcast_to(counts[:, 127:128], (8, 128))
        first = total & 255
        second = first + (right(total, 8) & 255)
        third = second + (right(total, 16) & 255)

        def start(family):
            return jnp.where(
                family < 2, jnp.where(family < 1, 0, first), jnp.where(family < 3, second, third)
            )

        turn = (at % 8 * 16 + at // 8 * 4) % 128
        rank_ref[at] = (start(right(code, 1)) + (right(counts, shift) & 255) + (turn - 1)) & 127
        spot = (lane + (128 - turn)) & 127
        family = (
            jnp.where(spot >= first, 1, 0) + jnp.where(spot >= second, 1, 0) + jnp.where(spot >= third, 1, 0)
        )
        wanted = spot - start(family)
        shift = family * 8
        source = jnp.zeros((8, 128), jnp.int32)
        for step in (64, 32, 16, 8, 4, 2, 1):
            seen = right(take(counts, source + (step - 1)), shift) & 255
            source = jnp.where(seen <= wanted, source + step, source)
        moved = take(code, source)
        keys.append(lax.shift_left(right(moved, 1), jnp.full((8, 128), 6, jnp.int32)) + (2 * at) + (moved & 1))
        for j in range(3):
            strains[j].append(take(strain_ref[j, at], source))
    keys, strains = sort_tiles(keys, *strains)
    info = jnp.zeros((8, 128), jnp.int32)
    for at in range(around):
        family = right(keys[at], 6)
        sorted_code_ref[at] = 2 * family + (keys[at] & 1)
        origin_ref[at] = right(keys[at], 1) & 31
        for j in range(3):
            sorted_ref[j, at] = strains[j][at]
        if at % 2:
            before = right(keys[at - 1], 6)
            low = jnp.min(jnp.minimum(before, family), axis=1, keepdims=True)
            high = jnp.max(jnp.maximum(before, family), axis=1, keepdims=True)
            low, high = jnp.broadcast_to(low, (8, 128)), jnp.broadcast_to(high, (8, 128))
            odd = jnp.where((family != low) & (family != high), 1, 0) + jnp.where((before != low) & (before != high), 1, 0)
            odd = jnp.broadcast_to(jnp.max(odd, axis=1, keepdims=True), (8, 128))
            for number, value in enumerate((low, high, odd)):
                info = jnp.where(lane == 16 * number + at // 2, value, info)
    info_ref[...] = info


def rhs_kernel(around, peers, first_ref, outer_ref, second_ref, rank_ref, origin_ref, rest_ref, chip_ref, far_ref, own_ref, low_ref, high_ref, answers):
    _, _, even = whereabouts(peers)
    for index in range(around // 8):
        low_ref[index] = jnp.where(even, far_ref[index], chip_ref[index])
        high_ref[index] = jnp.where(even, chip_ref[index], far_ref[index])
    row = lax.broadcasted_iota(jnp.int32, (8, 128), 0)
    rim = (row == 0) | (row == 7)

    moved = [[jnp.where(row < 4, first_ref[j, at], second_ref[j, at]) for at in range(around)] for j in range(4)]
    _, moved = sort_tiles([origin_ref[at] for at in range(around)], *moved)
    for at in range(around):
        for j in range(4):
            answers[j, at] = jnp.where(rim, outer_ref[j, at], take(moved[j][at], rank_ref[at]))

    def answer(number, at):
        return answers[number, at]

    cycle = [answer(0, at) for at in range(around)]
    for at in range(around):
        low = low_ref[at // 8, pl.ds(at % 8, 1), :]
        high = high_ref[at // 8, pl.ds(at % 8, 1), :]
        after, before = beside(answer(2, at), low, high)
        divergence = (cycle[(at + 1) % around] - cycle[(at - 1) % around]) * 0.5
        divergence = divergence + radial(answer(1, at)) + (after - before) * 0.5
        rows = pl.ds(row_of(at), 8, stride=around)
        own_ref[0, rows, :] = rest_ref[at] + divergence
        own_ref[1, rows, :] = 0.5 + answer(3, at)


HALF = ITERS // 2
MOST_LOST = 1.0e5


def tile(plane, quarter):
    return slice(32 * plane + 8 * quarter, 32 * plane + 8 * quarter + 8)


def three(peers, own_ref, chip_ref, far_ref, put):
    _, _, even = whereabouts(peers)
    for plane in range(8):
        for quarter in range(4):
            rows = tile(plane, quarter)
            chip, far = chip_ref[rows, :], far_ref[rows, :]
            put(plane, quarter, jnp.where(even, far, chip))
            put(plane + 8, quarter, own_ref[rows, :])
            put(plane + 16, quarter, jnp.where(even, chip, far))


def within_plane(here):
    lane = lax.broadcasted_iota(jnp.int32, (8, 128), 1)
    even_row = lax.broadcasted_iota(jnp.int32, (8, 128), 0) % 2 == 0
    up = [pltpu.roll(value, 7, 0) for value in here]
    down = [pltpu.roll(value, 1, 0) for value in here]
    result = []
    for quarter in range(4):
        after = jnp.where(even_row, up[quarter], down[quarter + 1] if quarter < 3 else up[0])
        before = jnp.where(even_row, up[quarter - 1] if quarter else down[3], down[quarter])
        outer = jnp.where(lane == 127, 0.0, pltpu.roll(here[quarter], 127, 1))
        inner = jnp.where(lane == 0, 0.0, pltpu.roll(here[quarter], 1, 1))
        out = jnp.where(lane >= 126, 0.0, outer)
        result.append((after, out, pltpu.roll(out, 2, 1), (after + before) + (outer + inner)))
    return result


def own_kernel(scale_ref, tan_ref, found_ref, main_ref, after_ref, out_ref, back_ref):
    centre, inverse = scale_ref[0:1, :], scale_ref[1:2, :]
    for plane in range(8):
        parts = within_plane([tan_ref[tile(plane, quarter), :] * (0.25 * inverse) for quarter in range(4)])
        for quarter, (after, out, back, total) in enumerate(parts):
            rows = tile(plane, quarter)
            main_ref[rows, :] = (found_ref[rows, :] - centre) * inverse + total
            after_ref[rows, :] = after
            out_ref[rows, :] = out
            back_ref[rows, :] = back


def operator_kernel(
    peers, scale_ref, tan_ref, tan_chip_ref, tan_far_ref, own_main_ref, own_after_ref, own_out_ref, own_back_ref,
    found_chip_ref, found_far_ref, tan, main, after, out, back
):
    centre, inverse = scale_ref[0:1, :], scale_ref[1:2, :]
    _, _, even = whereabouts(peers)

    def put_tan(plane, quarter, value):
        tan[tile(plane, quarter), :] = value * (0.25 * inverse)

    three(peers, tan_ref, tan_chip_ref, tan_far_ref, put_tan)
    for plane in range(2, 22):
        inside = 8 <= plane < 16
        if not inside:
            parts = within_plane([tan[tile(plane, quarter), :] for quarter in range(4)])
        for quarter in range(4):
            rows = tile(plane, quarter)
            if inside:
                own = tile(plane - 8, quarter)
                total = own_main_ref[own, :]
                after[rows, :] = own_after_ref[own, :]
                out[rows, :] = own_out_ref[own, :]
                back[rows, :] = own_back_ref[own, :]
            else:
                after[rows, :], out[rows, :], back[rows, :], total = parts[quarter]
                there = tile(plane % 8, quarter)
                chip, far = found_chip_ref[there, :], found_far_ref[there, :]
                found = jnp.where(even, far, chip) if plane < 8 else jnp.where(even, chip, far)
                total = total + (found - centre) * inverse
            axial = tan[tile(plane + 1, quarter), :] + tan[tile(plane - 1, quarter), :]
            main[rows, :] = total + axial


def basis_kernel(peers, last, *refs):
    if last:
        tan, main, after, out, back, seed_ref, seed_chip_ref, seed_far_ref, earlier_ref, previous_ref, *refs = refs
        own_ref, sums_ref, vectors = refs
    else:
        operator_refs, (seed_ref, seed_chip_ref, seed_far_ref), refs = refs[:10], refs[10:13], refs[13:]
        own_ref, tan, main, after, out, back, vectors = refs
        operator_kernel(peers, *operator_refs, tan, main, after, out, back)
    is_first, is_last, _ = whereabouts(peers)

    def put_seed(plane, quarter, value):
        vectors[0, tile(plane, quarter), :] = value

    three(peers, seed_ref, seed_chip_ref, seed_far_ref, put_seed)

    def axial(between, plane, degree, quarter):
        term = tan[tile(between, quarter), :] * vectors[degree, tile(plane, quarter), :]
        if between == 8 or between == 15:
            term = jnp.where(is_first if between == 8 else is_last, 0.0, term)
        return term

    def apply(degree, plane, quarter):
        rows = tile(plane, quarter)
        value = vectors[degree, rows, :]
        result = main[rows, :] * value
        if quarter < 3:
            result = result - after[rows, :] * vectors[degree, tile(plane, quarter + 1), :]
        else:
            result = result - after[rows, :] * pltpu.roll(vectors[degree, tile(plane, 0), :], 6, 0)
        before = tile(plane, (quarter - 1) % 4)
        product = after[before, :] * vectors[degree, before, :]
        result = result - (product if quarter else pltpu.roll(product, 2, 0))
        result = result - out[rows, :] * pltpu.roll(value, 126, 1) - back[rows, :] * pltpu.roll(value, 2, 1)
        return result - axial(plane + 1, plane + 2, degree, quarter) - axial(plane - 1, plane - 2, degree, quarter)

    for degree in range(1, HALF + 1):
        for plane in range(2 * degree, 24 - 2 * degree):
            for quarter in range(4):
                value = apply(degree - 1, plane, quarter)
                if degree > 1:
                    value = value + value - vectors[degree - 2, tile(plane, quarter), :]
                vectors[degree, tile(plane, quarter), :] = value
    own_tiles = [(tile(plane, quarter), tile(plane + 8, quarter)) for plane in range(8) for quarter in range(4)]
    if not last:
        for degree in range(HALF + 1):
            for rows, wide_rows in own_tiles:
                own_ref[degree, rows, :] = vectors[degree, wide_rows, :]
        return
    pairs = []
    for degree in range(1, HALF + 1):
        for rows, wide_rows in own_tiles:
            value = vectors[degree, wide_rows, :]
            own_ref[degree - 1, rows, :] = value + value - earlier_ref[HALF - degree, rows, :]
        before = earlier_ref.at[HALF] if degree == 1 else own_ref.at[degree - 2]
        pairs += [(before, own_ref.at[degree - 1]), (own_ref.at[degree - 1], own_ref.at[degree - 1])]
    sums = inner_products(pairs, 2 * HALF + 1, previous_ref[0:1, :])
    sums_ref[...] = jnp.broadcast_to(sums, sums_ref.shape)


def inner_products(pairs, first, sums):
    column = lax.broadcasted_iota(jnp.int32, (1, 128), 1)
    for number, (left, right) in enumerate(pairs):
        total = tree([left[start : start + 8, :] * right[start : start + 8, :] for start in range(0, left.shape[0], 8)])
        entry = jnp.sum(jnp.sum(total, axis=0, keepdims=True), axis=1, keepdims=True)
        sums = jnp.where(column == first + number, jnp.broadcast_to(entry, (1, 128)), sums)
    return sums


def products_kernel(early_ref, sums_ref):
    pairs = []
    for degree in range(HALF + 1):
        if degree:
            pairs.append((early_ref.at[degree - 1], early_ref.at[degree]))
        pairs.append((early_ref.at[degree], early_ref.at[degree]))
    sums = inner_products(pairs, 0, jnp.zeros((1, 128), F32))
    sums_ref[...] = jnp.broadcast_to(sums, sums_ref.shape)


def unpack_gram(all_ref, total):
    row = jnp.sum(all_ref[...], axis=0, keepdims=True)
    moments = []
    for number in range(2 * total - 1):
        entry = jnp.broadcast_to(row[:, number : number + 1], (1, 128))
        moments.append(entry if number < 2 else entry + entry - moments[number % 2])
    gram = {}
    for i in range(total):
        for j in range(i, total):
            gram[i, j] = gram[j, i] = 0.5 * (moments[i + j] + moments[j - i])
    return gram


def tree(terms):
    while len(terms) > 1:
        terms = [a + b for a, b in zip(terms[::2], terms[1::2])] + ([terms[-1]] if len(terms) % 2 else [])
    return terms[0]


def dot(gram, left, right):
    return tree(
        [
            a * tree([gram[i, j] * b for j, b in enumerate(right) if b is not None])
            for i, a in enumerate(left)
            if a is not None
        ]
    )


def axpy(scale, left, right):
    result = []
    for a, b in zip(left, right, strict=True):
        a = None if a is None else (a if scale is None else scale * a)
        result.append(b if a is None else (a if b is None else b + a))
    return result


def times_operator(vector, centre, half_width):
    total = len(vector)
    result = [None] * total
    half = 0.5 * half_width

    def add(index, term):
        result[index] = term if result[index] is None else result[index] + term

    for j, c in enumerate(vector):
        if c is None:
            continue
        add(j, centre * c)
        add(j + 1, (half if j else half_width) * c)
        if j:
            add(j - 1, half * c)
    return result


def iterate(gram, total, centre, half_width):
    residual = [jnp.ones((1, 128), F32)] + [None] * (total - 1)
    direction = residual
    change = [None] * total
    norms = [jnp.sqrt(gram[i, i]) for i in range(total)]
    current = gram[0, 0]
    worst = jnp.zeros((1, 128), F32)
    for step in range(ITERS):
        image = times_operator(direction, centre, half_width)
        alpha = current / dot(gram, direction, image)
        change = axpy(alpha, direction, change)
        residual = axpy(-alpha, image, residual)
        following = dot(gram, residual, residual)
        bound = tree([jnp.abs(c) * n for c, n in zip(residual, norms, strict=True) if c is not None])
        worst = jnp.maximum(worst, bound * bound / following)
        worst = jnp.where(following > 0.0, worst, jnp.inf)
        if step < ITERS - 1:
            direction = axpy(following / current, direction, residual)
        current = following
    return change, residual, worst


def last_kernel(around, scale_ref, all_ref, early_ref, late_ref, send_ref, worst_ref, results):
    total = 2 * HALF + 1
    change, residual, worst = iterate(unpack_gram(all_ref, total), total, scale_ref[0:1, :], scale_ref[2:3, :])
    worst_ref[...] = jnp.broadcast_to(worst, (8, 128))
    for number, part in enumerate((change, residual)):
        part = [None if c is None else jnp.broadcast_to(c, (8, 128)) for c in part]
        for start in range(0, 8 * around, 8):
            rows = slice(start, start + 8)
            results[number, rows, :] = tree(
                [
                    c * (early_ref[index, rows, :] if index <= HALF else late_ref[index - HALF - 1, rows, :])
                    for index, c in enumerate(part)
                    if c is not None
                ]
            )
        for b in range(around // 8):
            for half in range(2):
                tiles = [
                    results[number, pl.ds(row_of(8 * b + 4 * half + a), 8, stride=around), :] for a in range(4)
                ]
                tiles = regroup(tiles)
                for m in range(4):
                    send_ref[4 * b + m, half, number] = tiles[m]


def deliver_kernel(path, u_ref, recv_ref, worst_ref, instead_updated_ref, instead_residual_ref, *refs):
    updated_ref, residual_ref, turned = refs
    slab = lax.axis_index("slab")
    for source in range(recv_ref.shape[0]):
        start = pl.multiple_of(8 * place(slab, path[source], len(path)), 8)
        for index in range(2):
            turned[index, pl.ds(start, 8), :] = recv_ref[source, 0, index]
    good = jnp.broadcast_to(worst_ref[0:1, :] < MOST_LOST, (32, 128))
    change = jnp.transpose(turned[0]).reshape(4, 32, 128)
    residual = jnp.transpose(turned[1]).reshape(4, 32, 128)
    for i in range(4):
        updated_ref[i] = jnp.where(good, u_ref[i] + change[i], instead_updated_ref[i])
        residual_ref[i] = jnp.where(good, residual[i], instead_residual_ref[i])


def sliced_body(
    displacement, load_field, foundation, plastic_flags, point_slot, family_in, family_mid, family_out, family_tan
):
    size_x, size_y, size_z = displacement.shape
    families = family_in.shape[0]
    along, across = lax.axis_size("blk"), lax.axis_size("micro")
    peers = along * across
    around = size_x * along
    everyone = peers * lax.axis_size("slab")
    path = [b * across + (m if b % 2 == 0 else across - 1 - m) for b in range(along) for m in range(across)]
    _, _, even = whereabouts(peers)
    spots = [0] * everyone
    for b in range(along):
        for s in range(2):
            for m in range(across):
                spots[place(s, path[b * across + m], peers) + peers * s] = (b * 2 + s) * across + m

    def swap(first, value):
        pairs = [(spots[i], spots[i + 1]) for i in range(first, everyone - 1, 2)]
        return lax.ppermute(value, AXES, pairs + [(b, a) for a, b in pairs])

    def neighbours(to_chip, to_far):
        far = swap(1, to_far)
        return swap(0, to_chip), far

    packed = pack_families(family_in, family_mid, family_out, family_tan)
    capacity = size_x * size_y * size_z // 2
    halves = pl.BlockSpec((4, 32, 128), lambda i: (i, 0, 0))
    (send,) = call(
        lambda *refs: spread_kernel(path, capacity, *refs),
        [((peers, 2, 4, 8, 128), F32)], [pltpu.VMEM((4, 128, 128), F32)], "spread",
        displacement, load_field, foundation, point_slot, plastic_flags,
        grid=(2,), ins=[halves] * 5, outs=[pl.BlockSpec((peers, 1, 4, 8, 128), lambda i: (0, i, 0, 0, 0))],
    )
    recv = lax.all_to_all(send, GROUP, 0, 0, tiled=True)
    field = (around, 8, 128)
    edge = (around // 8, 8, 128)
    rows = (8 * around, 128)
    message = (around + around // 8, 8, 128)
    strain, code, found, rest, to_chip, to_far, scale = call(
        lambda *refs: collect_kernel(around, *refs),
        [((3,) + field, F32), (field, jnp.int32), (rows, F32), (field, F32), (message, F32), (message, F32), ((8, 128), F32)],
        [pltpu.VMEM(field, F32)], "collect", family_tan, recv,
    )
    chip, far = neighbours(to_chip, to_far)
    grouped, grouped_code, rank, origin, info = call(
        lambda *refs: arrange_kernel(around, *refs),
        [((3,) + field, F32), (field, jnp.int32), (field, jnp.int32), (field, jnp.int32), ((8, 128), jnp.int32)],
        [], "arrange", strain, code,
    )
    first = cells(grouped, grouped_code, packed, families, 8, (1, 2, 3), info=info)
    outer = cells(strain, code, packed, families, 8, (0, 7), jnp.broadcast_to(even.astype(jnp.int32), (1, 128)), chip, far)
    top, bottom = outer[2, :, 7].reshape(edge), outer[2, :, 0].reshape(edge)
    edge_chip, edge_far = neighbours(jnp.where(even, top, bottom), jnp.where(even, bottom, top))
    grouped, outer = lax.optimization_barrier((grouped, outer))
    second = cells(grouped, grouped_code, packed, families, 8, (4, 5, 6), info=info)
    (own,) = call(
        lambda *refs: rhs_kernel(around, peers, *refs), [((2,) + rows, F32)], [pltpu.VMEM(edge, F32)] * 2 + [pltpu.VMEM((4,) + field, F32)], "rhs",
        first, outer, second, rank, origin, rest, edge_chip, edge_far,
    )
    own_chip, own_far = neighbours(own, own)

    tall = (24 * around, 128)
    vectors = [pltpu.VMEM((HALF + 1,) + tall, F32)]
    inside = call(
        own_kernel, [(rows, F32)] * 4, [], "own", scale, own[1], found,
    )
    early, *operator = call(
        lambda *refs: basis_kernel(peers, False, *refs),
        [((HALF + 1,) + rows, F32)] + [(tall, F32)] * 5, vectors, "basis",
        scale, own[1], own_chip[1], own_far[1], *inside, chip[:around].reshape(rows), far[:around].reshape(rows),
        own[0], own_chip[0], own_far[0],
    )
    (sums,) = call(products_kernel, [((8, 128), F32)], [], "products", early)
    late, sums = call(
        lambda *refs: basis_kernel(peers, True, *refs), [((HALF,) + rows, F32), ((everyone, 128), F32)], vectors, "basis",
        *operator, early[HALF], *neighbours(early[HALF], early[HALF]), early, sums,
    )
    sums = lax.all_to_all(sums, AXES, 0, 0, tiled=True)
    send, worst = call(
        lambda *refs: last_kernel(around, *refs),
        [((peers, 2, 2, 8, 128), F32), ((8, 128), F32)], [pltpu.VMEM((2,) + rows, F32)], "last", scale, sums, early, late,
    )
    recv = lax.all_to_all(send, GROUP, 0, 0, tiled=True)
    inputs = (
        displacement, load_field, foundation, plastic_flags, point_slot, family_in, family_mid, family_out, family_tan
    )
    good, recv = lax.optimization_barrier((worst[0, 0] < MOST_LOST, recv))
    instead = lax.cond(good, lambda: (jnp.zeros_like(displacement),) * 2, lambda: plain_body(*inputs))
    shape = displacement.shape
    return call(
        lambda *refs: deliver_kernel(path, *refs), [(shape, F32), (shape, F32)], [pltpu.VMEM((2, 128, 128), F32)],
        "deliver", displacement, recv, worst, *instead, grid=(2,), outs=[halves] * 2,
        ins=[
            halves,
            pl.BlockSpec((peers, 1, 2, 8, 128), lambda i: (0, i, 0, 0, 0)),
            pl.BlockSpec((8, 128), lambda i: (0, 0)),
            halves,
            halves,
        ],
    )


def body(*inputs):
    size_x, size_y, size_z = inputs[0].shape
    along, across = lax.axis_size("blk"), lax.axis_size("micro")
    fits = (
        (size_x, size_y, size_z) == (8, 32, 128)
        and across == 4
        and size_z == 8 * along * across
        and lax.axis_size("slab") == 2
        and inputs[5].shape[0] == 4
    )
    if not fits:
        return plain_body(*inputs)
    return tuple(sliced_body(*inputs))


def solution(mesh):
    field = P("blk", "micro", "slab")
    return jax.shard_map(
        body,
        mesh=mesh,
        in_specs=(field,) * 5 + (P(),) * 4,
        out_specs=(field, field),
        check_vma=False,
    )
```

```python
import jax
import jax.numpy as jnp
from jax import lax
from jax.experimental import pallas as pl
from jax.experimental.pallas import tpu as pltpu
from jax.sharding import PartitionSpec as P

ITERS = 8
AXES = ("blk", "slab", "micro")
BF = jnp.bfloat16
F32 = jnp.float32


def split(value):
    high = lax.reduce_precision(value, 8, 7)
    return high.astype(BF), (value - high).astype(BF)


def pack_families(family_in, family_mid, family_out, family_tan):
    families, _, modes = family_in.shape
    spread = jnp.transpose(family_in, (2, 1, 0))
    spread = jnp.concatenate([spread, spread], axis=2).reshape(modes, 6 * families)
    high, low = split(spread)
    weight_in = jnp.concatenate([high, low], axis=1)
    none = jnp.zeros((families, 1, modes), BF)
    stress = jnp.concatenate([family_out, none], axis=1).reshape(4 * families, modes)
    weight_tan = jnp.broadcast_to(family_tan[:, :, None], (families, modes, 128))
    return weight_in, family_mid, stress, weight_tan


def cells_kernel(families, planes, strain_ref, code_ref, in_ref, mid_ref, out_ref, tan_ref, *refs, info_ref=None):
    *edges, answer_ref = refs
    modes = in_ref.shape[0]
    step = code_ref.shape[0]
    spots = [(a + i, x) for a in range(0, step, 2) for x in planes for i in range(2)]
    width = len(spots) * 128

    def evaluate(pairs):
        place = lax.broadcasted_iota(jnp.int32, (2 * families, 128), 0)
        column, family_row, flag_row = [], [], []
        for a, x in spots:
            code = code_ref[a, pl.ds(x, 1), :]
            family = lax.shift_right_logical(code, 1)
            picked = lax.rem(place, families) == jnp.broadcast_to(family, place.shape)
            pieces = []
            for j in range(3):
                value = strain_ref[j, a, pl.ds(x, 1), :]
                if edges and j == 2:
                    even, chip_ref, far_ref = edges
                    chip, far = chip_ref[0, pl.ds(a, 1), :], far_ref[0, pl.ds(a, 1), :]
                    beyond = jnp.where(even[...] == (1 if x == 7 else 0), chip, far) * 0.5
                    value = value - beyond if x == 0 else value + beyond
                value = jnp.broadcast_to(value, place.shape)
                high = value.astype(BF).astype(F32)
                piece = jnp.where(place < families, high, value - high)
                pieces.append(jnp.where(picked, piece, 0.0))
            column.append(jnp.concatenate(pieces, axis=0))
            family_row.append(family)
            flag_row.append(lax.bitwise_and(code, 1))
        spread = jnp.concatenate(column, axis=1).astype(BF)
        spread = jnp.concatenate([spread, spread], axis=0)
        family = jnp.concatenate(family_row, axis=1)
        flag = jnp.concatenate(flag_row, axis=1)
        modal = jnp.dot(in_ref[...], spread, preferred_element_type=F32)
        flagged = jnp.broadcast_to(flag, (modes, width)) > 0
        active = jnp.where(flagged, jnp.tanh(modal), modal).astype(BF)
        if pairs is None:
            wide = jnp.broadcast_to(family, (modes, width)).astype(BF)
            nothing = jnp.zeros_like(active)
            stacked = jnp.concatenate(
                [jnp.where(wide == jnp.array(f, BF), active, nothing) for f in range(families)], axis=0
            )
            mixing = jnp.concatenate([mid_ref[f] for f in range(families)], axis=1)
            hidden = jnp.dot(mixing, stacked, preferred_element_type=F32)
        else:
            nothing = jnp.zeros((modes, 256), BF)
            parts = []
            for number, (one, other) in enumerate(pairs):
                part = slice(256 * number, 256 * number + 256)
                ours = jnp.where(family[:, part] == one, 1.0, 0.0)
                ours = jnp.broadcast_to(ours, (modes, 256)).astype(BF) > jnp.array(0.5, BF)
                mine = active[:, part]
                stacked = jnp.concatenate([jnp.where(ours, mine, nothing), jnp.where(ours, nothing, mine)], axis=0)
                mixing = jnp.concatenate([mid_ref[one], mid_ref[other]], axis=1)
                parts.append(jnp.dot(mixing, stacked, preferred_element_type=F32))
            hidden = jnp.concatenate(parts, axis=1)
        bounded = jnp.tanh(hidden).astype(BF)
        result = jnp.dot(out_ref[...], bounded, preferred_element_type=F32)
        owner = lax.shift_right_logical(lax.broadcasted_iota(jnp.int32, (4 * families, width), 0), 2)
        result = jnp.where(owner == family, result, 0.0)
        total = result[:4]
        for f in range(1, families):
            total = total + result[4 * f : 4 * f + 4]
        for i, (a, x) in enumerate(spots):
            part = slice(i * 128, (i + 1) * 128)
            answer_ref[0:3, a, x, :] = total[0:3, part]
            square = bounded[:, part].astype(F32)
            square = square * square
            owner = jnp.broadcast_to(family_row[i], (modes, 128))
            if pairs is None:
                weight = tan_ref[0]
                for f in range(1, families):
                    weight = jnp.where(owner == f, tan_ref[f], weight)
            else:
                one, other = pairs[i // 2]
                weight = jnp.where(owner == one, tan_ref[one], tan_ref[other])
            answer_ref[3, a, pl.ds(x, 1), :] = jnp.sum(weight * square, axis=0, keepdims=True)

    if info_ref is None:
        evaluate(None)
        return
    first = pl.program_id(0) * (step // 2)
    pairs, more = [], 0
    for a in range(step // 2):
        for x in planes:
            pairs.append((info_ref[x, first + a], info_ref[x, 16 + first + a]))
            more = more + info_ref[x, 32 + first + a]

    @pl.when(more == 0)
    def _():
        evaluate(pairs)

    @pl.when(more != 0)
    def _():
        evaluate(None)


def cells(strain, code, packed, families, step, planes, *edges, info=None):
    weight_in, weight_mid, weight_out, weight_tan = packed
    count = code.shape[0]
    planes = tuple(planes)
    points = count * len(planes) * 128
    modes = weight_in.shape[0]

    def whole(array):
        return pl.BlockSpec(array.shape, lambda i, *_: (0,) * array.ndim)

    def kernel(*refs):
        if info is None:
            cells_kernel(families, planes, *refs)
        else:
            cells_kernel(families, planes, *refs[1:], info_ref=refs[0])

    scalars = () if info is None else (info,)
    return pl.pallas_call(
        kernel,
        grid_spec=pltpu.PrefetchScalarGridSpec(
            num_scalar_prefetch=len(scalars),
            grid=(count // step,),
            in_specs=[
                pl.BlockSpec((3, step, 8, 128), lambda i, *_: (0, i, 0, 0)),
                pl.BlockSpec((step, 8, 128), lambda i, *_: (i, 0, 0)),
                whole(weight_in),
                whole(weight_mid),
                whole(weight_out),
                whole(weight_tan),
            ]
            + [pl.BlockSpec((1, 128), lambda i, *_: (0, 0)) for _ in edges[:1]]
            + [pl.BlockSpec((1, 8, 128), lambda i, *_: (count + i, 0, 0)) for _ in edges[1:]],
            out_specs=pl.BlockSpec((4, step, 8, 128), lambda i, *_: (0, i, 0, 0)),
        ),
        out_shape=jax.ShapeDtypeStruct((4, count, 8, 128), F32),
        compiler_params=pltpu.CompilerParams(vmem_limit_bytes=48 * 2**20),
        cost_estimate=pl.CostEstimate(
            flops=2 * points * modes * modes * (families + 1), bytes_accessed=points * 32, transcendentals=2 * points * modes
        ),
        name="cells",
    )(*scalars, strain, code, weight_in, weight_mid, weight_out, weight_tan, *edges)


def global_sum(value):
    count = 1
    for axis in AXES:
        count = count * lax.axis_size(axis)
    spread = jnp.broadcast_to(value.reshape(1, 1), (count, 128))
    return jnp.sum(lax.all_to_all(spread, AXES, 0, 0, tiled=True)[:, 0])


def widened(cells_, axis, dim, width, closed):
    count = lax.axis_size(axis)
    ends = count if closed else count - 1
    head = lax.slice_in_dim(cells_, 0, width, axis=dim)
    tail = lax.slice_in_dim(cells_, cells_.shape[dim] - width, cells_.shape[dim], axis=dim)
    before = lax.ppermute(tail, axis, [(i, (i + 1) % count) for i in range(ends)])
    after = lax.ppermute(head, axis, [((i + 1) % count, i) for i in range(ends)])
    return jnp.concatenate([before, cells_, after], axis=dim)


HALOS = (("blk", True), ("micro", False), ("slab", False))


def widened_all(field, width):
    return [widened(field, axis, dim, width, closed) for dim, (axis, closed) in enumerate(HALOS)]


def difference(field, dim):
    length = field.shape[dim]
    return (lax.slice_in_dim(field, 2, length, axis=dim) - lax.slice_in_dim(field, 0, length - 2, axis=dim)) * 0.5


def plain_body(
    displacement, load_field, foundation, plastic_flags, point_slot, family_in, family_mid, family_out, family_tan
):
    size_x, size_y, size_z = displacement.shape
    points = size_x * size_y * size_z
    families = family_in.shape[0]
    capacity = points // 2
    packed = pack_families(family_in, family_mid, family_out, family_tan)
    strain = [difference(w, dim) for dim, w in enumerate(widened_all(displacement, 1))]
    code = 2 * (point_slot // capacity) + plastic_flags
    tiles = points // 1024
    answers = cells(jnp.stack(strain).reshape(3, tiles, 8, 128), code.reshape(tiles, 8, 128), packed, families, 2, range(8))
    answers = answers.reshape(4, size_x, size_y, size_z)
    tangents = widened_all(0.5 + answers[3], 1)
    divergence = sum(
        difference(widened(answers[dim], axis, dim, 1, closed), dim) for dim, (axis, closed) in enumerate(HALOS)
    )
    rhs = load_field - foundation * displacement + divergence
    solution_ = jnp.zeros_like(rhs)
    residual = rhs
    direction = rhs
    current = global_sum(jnp.sum(residual * residual))
    for _ in range(ITERS):
        total = sum(
            difference(tangents[dim] * difference(w, dim), dim) for dim, w in enumerate(widened_all(direction, 2))
        )
        image = foundation * direction - total
        alpha = current / global_sum(jnp.sum(direction * image))
        solution_ = solution_ + alpha * direction
        residual = residual - alpha * image
        following = global_sum(jnp.sum(residual * residual))
        direction = residual + following / current * direction
        current = following
    return displacement + solution_, residual


VMEM = pl.BlockSpec(memory_space=pltpu.VMEM)
GROUP = ("blk", "micro")


def call(kernel, out_shapes, scratch, name, *args, grid=(), ins=None, outs=None):
    return pl.pallas_call(
        kernel,
        out_shape=[jax.ShapeDtypeStruct(shape, dtype) for shape, dtype in out_shapes],
        grid=grid,
        in_specs=ins or [VMEM] * len(args),
        out_specs=outs or [VMEM] * len(out_shapes),
        scratch_shapes=scratch,
        compiler_params=pltpu.CompilerParams(vmem_limit_bytes=40 * 2**20),
        name=name,
    )(*args)


def regroup(tiles):
    group = lax.broadcasted_iota(jnp.int32, (8, 128), 1) // 32
    result = []
    for a in range(4):
        tile = tiles[0]
        for m in range(4):
            shift = (m - a) * 32 % 128
            moved = pltpu.roll(tiles[m], shift, 1) if shift else tiles[m]
            tile = moved if m == 0 else jnp.where(group == m, moved, tile)
        result.append(tile)
    return result


def place(slab, position, peers):
    return position + slab * (peers - 1 - 2 * position)


def whereabouts(peers):
    across = lax.axis_size("micro")
    b, m, slab = lax.axis_index("blk"), lax.axis_index("micro"), lax.axis_index("slab")
    position = place(slab, b * across + jnp.where(b % 2 == 0, m, across - 1 - m), peers)
    return (slab == 0) & (position == 0), (slab == 1) & (position == peers - 1), position % 2 == 0


def spread_kernel(path, capacity, u_ref, load_ref, found_ref, slot_ref, flag_ref, send_ref, turned):
    peers = len(path)
    slab = lax.axis_index("slab")
    code = flag_ref[...]
    for family in range(1, 4):
        code = code + jnp.where(slot_ref[...] >= family * capacity, 2, 0)
    rest = load_ref[...] - found_ref[...] * u_ref[...]
    for number, value in enumerate((u_ref[...], code.astype(F32), found_ref[...], rest)):
        turned[number] = jnp.transpose(value.reshape(128, 128))
    for target in range(peers):
        start = pl.multiple_of(8 * place(slab, path[target], peers), 8)
        for number in range(4):
            send_ref[target, 0, number] = turned[number, pl.ds(start, 8), :]


def beside(tile, low, high):
    row = lax.broadcasted_iota(jnp.int32, (8, 128), 0)
    after = jnp.where(row == 7, jnp.broadcast_to(high, (8, 128)), pltpu.roll(tile, 7, 0))
    before = jnp.where(row == 0, jnp.broadcast_to(low, (8, 128)), pltpu.roll(tile, 1, 0))
    return after, before


def radial(tile):
    lane = lax.broadcasted_iota(jnp.int32, tile.shape, tile.ndim - 1)
    after = jnp.where(lane == 127, 0.0, pltpu.roll(tile, 127, tile.ndim - 1))
    before = jnp.where(lane == 0, 0.0, pltpu.roll(tile, 1, tile.ndim - 1))
    return (after - before) * 0.5


def row_of(at):
    return at % 8 // 2 * 8 + at // 8 * 2 + at % 2


def collect_kernel(around, tan_ref, recv_ref, strain_ref, code_ref, found_ref, rest_ref, chip_ref, far_ref, scale_ref, u):
    _, _, even = whereabouts(recv_ref.shape[0])
    typical = jnp.sum(jnp.sum(tan_ref[...], axis=1, keepdims=True), axis=0, keepdims=True) / tan_ref.shape[0]
    centre = jnp.broadcast_to(1.1 + 1.4 * (0.5 + 0.33 * typical), (8, 128))
    row = lax.broadcasted_iota(jnp.int32, (8, 128), 0)
    scale_ref[...] = jnp.where(row == 0, centre, jnp.where(row == 1, 1.0 / (centre - 0.4), centre - 0.4))
    for b in range(around // 8):
        for half in range(2):
            for number in range(4):
                tiles = regroup([recv_ref[4 * b + m, half, number] for m in range(4)])
                for a in range(4):
                    at = 8 * b + 4 * half + a
                    if number == 0:
                        u[at] = tiles[a]
                    elif number == 1:
                        code_ref[at] = tiles[a].astype(jnp.int32)
                    elif number == 2:
                        rows = pl.ds(row_of(at), 8, stride=around)
                        found_ref[rows, :] = tiles[a]
                    else:
                        rest_ref[at] = tiles[a]
    nothing = jnp.zeros((1, 128), F32)
    for at in range(around):
        tile = u[at]
        strain_ref[0, at] = (u[(at + 1) % around] - u[(at - 1) % around]) * 0.5
        strain_ref[1, at] = radial(tile)
        after, before = beside(tile, nothing, nothing)
        strain_ref[2, at] = (after - before) * 0.5
        chip_ref[around + at // 8, pl.ds(at % 8, 1), :] = tile[7:8]
        far_ref[around + at // 8, pl.ds(at % 8, 1), :] = tile[0:1]
    for index in range(around):
        value = found_ref[8 * index : 8 * index + 8, :]
        chip_ref[index] = value
        far_ref[index] = value
    for index in range(around, around + around // 8):
        bottom, top = far_ref[index], chip_ref[index]
        chip_ref[index] = jnp.where(even, top, bottom)
        far_ref[index] = jnp.where(even, bottom, top)


def network(count):
    pairs = []
    p = 1
    while p < count:
        k = p
        while k >= 1:
            for j in range(k % p, count - k, 2 * k):
                for i in range(j, min(j + k, count - k)):
                    if i // (2 * p) == (i + k) // (2 * p):
                        pairs.append((i, i + k))
            k //= 2
        p *= 2
    return pairs


def sort_tiles(keys, *carried):
    keys, carried = list(keys), [list(c) for c in carried]
    for i, j in network(len(keys)):
        wrong = keys[i] > keys[j]
        keys[i], keys[j] = jnp.minimum(keys[i], keys[j]), jnp.maximum(keys[i], keys[j])
        for c in carried:
            c[i], c[j] = jnp.where(wrong, c[j], c[i]), jnp.where(wrong, c[i], c[j])
    return keys, carried


def take(tile, index):
    return jnp.take_along_axis(tile, index, axis=1, mode="promise_in_bounds")


def arrange_kernel(around, strain_ref, code_ref, sorted_ref, sorted_code_ref, rank_ref, origin_ref, info_ref):
    lane = lax.broadcasted_iota(jnp.int32, (8, 128), 1)
    right = lax.shift_right_logical
    keys, strains = [], [[], [], []]
    for at in range(around):
        code = code_ref[at]
        shift = right(code, 1) * 8
        counts = lax.shift_left(jnp.ones((8, 128), jnp.int32), shift)
        for step in (1, 2, 4, 8, 16, 32, 64):
            counts = counts + jnp.where(lane >= step, pltpu.roll(counts, step, 1), 0)
        total = jnp.broadcast_to(counts[:, 127:128], (8, 128))
        first = total & 255
        second = first + (right(total, 8) & 255)
        third = second + (right(total, 16) & 255)

        def start(family):
            return jnp.where(
                family < 2, jnp.where(family < 1, 0, first), jnp.where(family < 3, second, third)
            )

        turn = (at % 8 * 16 + at // 8 * 4) % 128
        rank_ref[at] = (start(right(code, 1)) + (right(counts, shift) & 255) + (turn - 1)) & 127
        spot = (lane + (128 - turn)) & 127
        family = (
            jnp.where(spot >= first, 1, 0) + jnp.where(spot >= second, 1, 0) + jnp.where(spot >= third, 1, 0)
        )
        wanted = spot - start(family)
        shift = family * 8
        source = jnp.zeros((8, 128), jnp.int32)
        for step in (64, 32, 16, 8, 4, 2, 1):
            seen = right(take(counts, source + (step - 1)), shift) & 255
            source = jnp.where(seen <= wanted, source + step, source)
        moved = take(code, source)
        keys.append(lax.shift_left(right(moved, 1), jnp.full((8, 128), 6, jnp.int32)) + (2 * at) + (moved & 1))
        for j in range(3):
            strains[j].append(take(strain_ref[j, at], source))
    keys, strains = sort_tiles(keys, *strains)
    info = jnp.zeros((8, 128), jnp.int32)
    for at in range(around):
        family = right(keys[at], 6)
        sorted_code_ref[at] = 2 * family + (keys[at] & 1)
        origin_ref[at] = right(keys[at], 1) & 31
        for j in range(3):
            sorted_ref[j, at] = strains[j][at]
        if at % 2:
            before = right(keys[at - 1], 6)
            low = jnp.min(jnp.minimum(before, family), axis=1, keepdims=True)
            high = jnp.max(jnp.maximum(before, family), axis=1, keepdims=True)
            low, high = jnp.broadcast_to(low, (8, 128)), jnp.broadcast_to(high, (8, 128))
            odd = jnp.where((family != low) & (family != high), 1, 0) + jnp.where((before != low) & (before != high), 1, 0)
            odd = jnp.broadcast_to(jnp.max(odd, axis=1, keepdims=True), (8, 128))
            for number, value in enumerate((low, high, odd)):
                info = jnp.where(lane == 16 * number + at // 2, value, info)
    info_ref[...] = info


def rhs_kernel(around, peers, first_ref, outer_ref, second_ref, rank_ref, origin_ref, rest_ref, chip_ref, far_ref, own_ref, low_ref, high_ref, answers):
    _, _, even = whereabouts(peers)
    for index in range(around // 8):
        low_ref[index] = jnp.where(even, far_ref[index], chip_ref[index])
        high_ref[index] = jnp.where(even, chip_ref[index], far_ref[index])
    row = lax.broadcasted_iota(jnp.int32, (8, 128), 0)
    rim = (row == 0) | (row == 7)

    moved = [[jnp.where(row < 4, first_ref[j, at], second_ref[j, at]) for at in range(around)] for j in range(4)]
    _, moved = sort_tiles([origin_ref[at] for at in range(around)], *moved)
    for at in range(around):
        for j in range(4):
            answers[j, at] = jnp.where(rim, outer_ref[j, at], take(moved[j][at], rank_ref[at]))

    def answer(number, at):
        return answers[number, at]

    cycle = [answer(0, at) for at in range(around)]
    for at in range(around):
        low = low_ref[at // 8, pl.ds(at % 8, 1), :]
        high = high_ref[at // 8, pl.ds(at % 8, 1), :]
        after, before = beside(answer(2, at), low, high)
        divergence = (cycle[(at + 1) % around] - cycle[(at - 1) % around]) * 0.5
        divergence = divergence + radial(answer(1, at)) + (after - before) * 0.5
        rows = pl.ds(row_of(at), 8, stride=around)
        own_ref[0, rows, :] = rest_ref[at] + divergence
        own_ref[1, rows, :] = 0.5 + answer(3, at)


HALF = ITERS // 2
MOST_LOST = 1.0e5


def tile(plane, quarter):
    return slice(32 * plane + 8 * quarter, 32 * plane + 8 * quarter + 8)


def three(peers, own_ref, chip_ref, far_ref, put):
    _, _, even = whereabouts(peers)
    for plane in range(8):
        for quarter in range(4):
            rows = tile(plane, quarter)
            chip, far = chip_ref[rows, :], far_ref[rows, :]
            put(plane, quarter, jnp.where(even, far, chip))
            put(plane + 8, quarter, own_ref[rows, :])
            put(plane + 16, quarter, jnp.where(even, chip, far))


def within_plane(here):
    lane = lax.broadcasted_iota(jnp.int32, (8, 128), 1)
    even_row = lax.broadcasted_iota(jnp.int32, (8, 128), 0) % 2 == 0
    up = [pltpu.roll(value, 7, 0) for value in here]
    down = [pltpu.roll(value, 1, 0) for value in here]
    result = []
    for quarter in range(4):
        after = jnp.where(even_row, up[quarter], down[quarter + 1] if quarter < 3 else up[0])
        before = jnp.where(even_row, up[quarter - 1] if quarter else down[3], down[quarter])
        outer = jnp.where(lane == 127, 0.0, pltpu.roll(here[quarter], 127, 1))
        inner = jnp.where(lane == 0, 0.0, pltpu.roll(here[quarter], 1, 1))
        out = jnp.where(lane >= 126, 0.0, outer)
        result.append((after, out, pltpu.roll(out, 2, 1), (after + before) + (outer + inner)))
    return result


def own_kernel(scale_ref, tan_ref, found_ref, main_ref, after_ref, out_ref, back_ref):
    centre, inverse = scale_ref[0:1, :], scale_ref[1:2, :]
    for plane in range(8):
        parts = within_plane([tan_ref[tile(plane, quarter), :] * (0.25 * inverse) for quarter in range(4)])
        for quarter, (after, out, back, total) in enumerate(parts):
            rows = tile(plane, quarter)
            main_ref[rows, :] = (found_ref[rows, :] - centre) * inverse + total
            after_ref[rows, :] = after
            out_ref[rows, :] = out
            back_ref[rows, :] = back


def operator_kernel(
    peers, scale_ref, tan_ref, tan_chip_ref, tan_far_ref, own_main_ref, own_after_ref, own_out_ref, own_back_ref,
    found_chip_ref, found_far_ref, tan, main, after, out, back
):
    centre, inverse = scale_ref[0:1, :], scale_ref[1:2, :]
    _, _, even = whereabouts(peers)

    def put_tan(plane, quarter, value):
        tan[tile(plane, quarter), :] = value * (0.25 * inverse)

    three(peers, tan_ref, tan_chip_ref, tan_far_ref, put_tan)
    for plane in range(2, 22):
        inside = 8 <= plane < 16
        if not inside:
            parts = within_plane([tan[tile(plane, quarter), :] for quarter in range(4)])
        for quarter in range(4):
            rows = tile(plane, quarter)
            if inside:
                own = tile(plane - 8, quarter)
                total = own_main_ref[own, :]
                after[rows, :] = own_after_ref[own, :]
                out[rows, :] = own_out_ref[own, :]
                back[rows, :] = own_back_ref[own, :]
            else:
                after[rows, :], out[rows, :], back[rows, :], total = parts[quarter]
                there = tile(plane % 8, quarter)
                chip, far = found_chip_ref[there, :], found_far_ref[there, :]
                found = jnp.where(even, far, chip) if plane < 8 else jnp.where(even, chip, far)
                total = total + (found - centre) * inverse
            axial = tan[tile(plane + 1, quarter), :] + tan[tile(plane - 1, quarter), :]
            main[rows, :] = total + axial


def basis_kernel(peers, last, *refs):
    if last:
        seed_far_ref, tan, main, after, out, back, earlier_ref, previous_ref, seed_ref, seed_chip_ref, *refs = refs
        own_ref, sums_ref, vectors = refs
    else:
        operator_refs, (seed_ref, seed_chip_ref, seed_far_ref), refs = refs[:10], refs[10:13], refs[13:]
        own_ref, tan, main, after, out, back, vectors = refs
        operator_kernel(peers, *operator_refs, tan, main, after, out, back)
    is_first, is_last, _ = whereabouts(peers)

    def put_seed(plane, quarter, value):
        vectors[0, tile(plane, quarter), :] = value

    three(peers, seed_ref, seed_chip_ref, seed_far_ref, put_seed)

    def axial(between, plane, degree, quarter):
        term = tan[tile(between, quarter), :] * vectors[degree, tile(plane, quarter), :]
        if between == 8 or between == 15:
            term = jnp.where(is_first if between == 8 else is_last, 0.0, term)
        return term

    def apply(degree, plane, quarter):
        rows = tile(plane, quarter)
        value = vectors[degree, rows, :]
        result = main[rows, :] * value
        if quarter < 3:
            result = result - after[rows, :] * vectors[degree, tile(plane, quarter + 1), :]
        else:
            result = result - after[rows, :] * pltpu.roll(vectors[degree, tile(plane, 0), :], 6, 0)
        before = tile(plane, (quarter - 1) % 4)
        product = after[before, :] * vectors[degree, before, :]
        result = result - (product if quarter else pltpu.roll(product, 2, 0))
        result = result - out[rows, :] * pltpu.roll(value, 126, 1) - back[rows, :] * pltpu.roll(value, 2, 1)
        return result - axial(plane + 1, plane + 2, degree, quarter) - axial(plane - 1, plane - 2, degree, quarter)

    for degree in range(1, HALF + 1):
        for plane in range(2 * degree, 24 - 2 * degree):
            for quarter in range(4):
                value = apply(degree - 1, plane, quarter)
                if degree > 1:
                    value = value + value - vectors[degree - 2, tile(plane, quarter), :]
                vectors[degree, tile(plane, quarter), :] = value
    own_tiles = [(tile(plane, quarter), tile(plane + 8, quarter)) for plane in range(8) for quarter in range(4)]
    if not last:
        for degree in range(HALF + 1):
            for rows, wide_rows in own_tiles:
                own_ref[degree, rows, :] = vectors[degree, wide_rows, :]
        return
    pairs = []
    for degree in range(1, HALF + 1):
        for rows, wide_rows in own_tiles:
            value = vectors[degree, wide_rows, :]
            own_ref[degree - 1, rows, :] = value + value - earlier_ref[HALF - degree, rows, :]
        before = earlier_ref.at[HALF] if degree == 1 else own_ref.at[degree - 2]
        pairs += [(before, own_ref.at[degree - 1]), (own_ref.at[degree - 1], own_ref.at[degree - 1])]
    sums = inner_products(pairs, 2 * HALF + 1, previous_ref[0:1, :])
    sums_ref[...] = jnp.broadcast_to(sums, sums_ref.shape)


def inner_products(pairs, first, sums):
    column = lax.broadcasted_iota(jnp.int32, (1, 128), 1)
    for number, (left, right) in enumerate(pairs):
        total = tree([left[start : start + 8, :] * right[start : start + 8, :] for start in range(0, left.shape[0], 8)])
        entry = jnp.sum(jnp.sum(total, axis=0, keepdims=True), axis=1, keepdims=True)
        sums = jnp.where(column == first + number, jnp.broadcast_to(entry, (1, 128)), sums)
    return sums


def products_kernel(early_ref, sums_ref):
    pairs = []
    for degree in range(HALF + 1):
        if degree:
            pairs.append((early_ref.at[degree - 1], early_ref.at[degree]))
        pairs.append((early_ref.at[degree], early_ref.at[degree]))
    sums = inner_products(pairs, 0, jnp.zeros((1, 128), F32))
    sums_ref[...] = jnp.broadcast_to(sums, sums_ref.shape)


def unpack_gram(all_ref, total):
    row = jnp.sum(all_ref[...], axis=0, keepdims=True)
    moments = []
    for number in range(2 * total - 1):
        entry = jnp.broadcast_to(row[:, number : number + 1], (1, 128))
        moments.append(entry if number < 2 else entry + entry - moments[number % 2])
    gram = {}
    for i in range(total):
        for j in range(i, total):
            gram[i, j] = gram[j, i] = 0.5 * (moments[i + j] + moments[j - i])
    return gram


def tree(terms):
    while len(terms) > 1:
        terms = [a + b for a, b in zip(terms[::2], terms[1::2])] + ([terms[-1]] if len(terms) % 2 else [])
    return terms[0]


def dot(gram, left, right):
    return tree(
        [
            a * tree([gram[i, j] * b for j, b in enumerate(right) if b is not None])
            for i, a in enumerate(left)
            if a is not None
        ]
    )


def axpy(scale, left, right):
    result = []
    for a, b in zip(left, right, strict=True):
        a = None if a is None else (a if scale is None else scale * a)
        result.append(b if a is None else (a if b is None else b + a))
    return result


def times_operator(vector, centre, half_width):
    total = len(vector)
    result = [None] * total
    half = 0.5 * half_width

    def add(index, term):
        result[index] = term if result[index] is None else result[index] + term

    for j, c in enumerate(vector):
        if c is None:
            continue
        add(j, centre * c)
        add(j + 1, (half if j else half_width) * c)
        if j:
            add(j - 1, half * c)
    return result


def iterate(gram, total, centre, half_width):
    residual = [jnp.ones((1, 128), F32)] + [None] * (total - 1)
    direction = residual
    change = [None] * total
    norms = [jnp.sqrt(gram[i, i]) for i in range(total)]
    current = gram[0, 0]
    worst = jnp.zeros((1, 128), F32)
    for step in range(ITERS):
        image = times_operator(direction, centre, half_width)
        alpha = current / dot(gram, direction, image)
        change = axpy(alpha, direction, change)
        residual = axpy(-alpha, image, residual)
        following = dot(gram, residual, residual)
        bound = tree([jnp.abs(c) * n for c, n in zip(residual, norms, strict=True) if c is not None])
        worst = jnp.maximum(worst, bound * bound / following)
        worst = jnp.where(following > 0.0, worst, jnp.inf)
        if step < ITERS - 1:
            direction = axpy(following / current, direction, residual)
        current = following
    return change, residual, worst


def last_kernel(around, scale_ref, all_ref, early_ref, late_ref, send_ref, worst_ref, results):
    total = 2 * HALF + 1
    change, residual, worst = iterate(unpack_gram(all_ref, total), total, scale_ref[0:1, :], scale_ref[2:3, :])
    worst_ref[...] = jnp.broadcast_to(worst, (8, 128))
    for number, part in enumerate((change, residual)):
        part = [None if c is None else jnp.broadcast_to(c, (8, 128)) for c in part]
        for start in range(0, 8 * around, 8):
            rows = slice(start, start + 8)
            results[number, rows, :] = tree(
                [
                    c * (early_ref[index, rows, :] if index <= HALF else late_ref[index - HALF - 1, rows, :])
                    for index, c in enumerate(part)
                    if c is not None
                ]
            )
        for b in range(around // 8):
            for half in range(2):
                tiles = [
                    results[number, pl.ds(row_of(8 * b + 4 * half + a), 8, stride=around), :] for a in range(4)
                ]
                tiles = regroup(tiles)
                for m in range(4):
                    send_ref[4 * b + m, half, number] = tiles[m]


def deliver_kernel(path, u_ref, recv_ref, worst_ref, instead_updated_ref, instead_residual_ref, *refs):
    updated_ref, residual_ref, turned = refs
    slab = lax.axis_index("slab")
    for source in range(recv_ref.shape[0]):
        start = pl.multiple_of(8 * place(slab, path[source], len(path)), 8)
        for index in range(2):
            turned[index, pl.ds(start, 8), :] = recv_ref[source, 0, index]
    good = jnp.broadcast_to(worst_ref[0:1, :] < MOST_LOST, (32, 128))
    change = jnp.transpose(turned[0]).reshape(4, 32, 128)
    residual = jnp.transpose(turned[1]).reshape(4, 32, 128)
    for i in range(4):
        updated_ref[i] = jnp.where(good, u_ref[i] + change[i], instead_updated_ref[i])
        residual_ref[i] = jnp.where(good, residual[i], instead_residual_ref[i])


def sliced_body(
    displacement, load_field, foundation, plastic_flags, point_slot, family_in, family_mid, family_out, family_tan
):
    size_x, size_y, size_z = displacement.shape
    families = family_in.shape[0]
    along, across = lax.axis_size("blk"), lax.axis_size("micro")
    peers = along * across
    around = size_x * along
    everyone = peers * lax.axis_size("slab")
    path = [b * across + (m if b % 2 == 0 else across - 1 - m) for b in range(along) for m in range(across)]
    _, _, even = whereabouts(peers)
    spots = [0] * everyone
    for b in range(along):
        for s in range(2):
            for m in range(across):
                spots[place(s, path[b * across + m], peers) + peers * s] = (b * 2 + s) * across + m

    def swap(first, value):
        pairs = [(spots[i], spots[i + 1]) for i in range(first, everyone - 1, 2)]
        return lax.ppermute(value, AXES, pairs + [(b, a) for a, b in pairs])

    def neighbours(to_chip, to_far):
        far = swap(1, to_far)
        return swap(0, to_chip), far

    packed = pack_families(family_in, family_mid, family_out, family_tan)
    capacity = size_x * size_y * size_z // 2
    halves = pl.BlockSpec((4, 32, 128), lambda i: (i, 0, 0))
    (send,) = call(
        lambda *refs: spread_kernel(path, capacity, *refs),
        [((peers, 2, 4, 8, 128), F32)], [pltpu.VMEM((4, 128, 128), F32)], "spread",
        displacement, load_field, foundation, point_slot, plastic_flags,
        grid=(2,), ins=[halves] * 5, outs=[pl.BlockSpec((peers, 1, 4, 8, 128), lambda i: (0, i, 0, 0, 0))],
    )
    recv = lax.all_to_all(send, GROUP, 0, 0, tiled=True)
    field = (around, 8, 128)
    edge = (around // 8, 8, 128)
    rows = (8 * around, 128)
    message = (around + around // 8, 8, 128)
    strain, code, found, rest, to_chip, to_far, scale = call(
        lambda *refs: collect_kernel(around, *refs),
        [((3,) + field, F32), (field, jnp.int32), (rows, F32), (field, F32), (message, F32), (message, F32), ((8, 128), F32)],
        [pltpu.VMEM(field, F32)], "collect", family_tan, recv,
    )
    chip, far = neighbours(to_chip, to_far)
    grouped, grouped_code, rank, origin, info = call(
        lambda *refs: arrange_kernel(around, *refs),
        [((3,) + field, F32), (field, jnp.int32), (field, jnp.int32), (field, jnp.int32), ((8, 128), jnp.int32)],
        [], "arrange", strain, code,
    )
    first = cells(grouped, grouped_code, packed, families, 8, (1, 2, 3), info=info)
    outer = cells(strain, code, packed, families, 8, (0, 7), jnp.broadcast_to(even.astype(jnp.int32), (1, 128)), chip, far)
    top, bottom = outer[2, :, 7].reshape(edge), outer[2, :, 0].reshape(edge)
    edge_chip, edge_far = neighbours(jnp.where(even, top, bottom), jnp.where(even, bottom, top))
    grouped, outer = lax.optimization_barrier((grouped, outer))
    second = cells(grouped, grouped_code, packed, families, 8, (4, 5, 6), info=info)
    (own,) = call(
        lambda *refs: rhs_kernel(around, peers, *refs), [((2,) + rows, F32)], [pltpu.VMEM(edge, F32)] * 2 + [pltpu.VMEM((4,) + field, F32)], "rhs",
        first, outer, second, rank, origin, rest, edge_chip, edge_far,
    )
    own_chip, own_far = neighbours(own, own)

    tall = (24 * around, 128)
    vectors = [pltpu.VMEM((HALF + 1,) + tall, F32)]
    inside = call(
        own_kernel, [(rows, F32)] * 4, [], "own", scale, own[1], found,
    )
    early, *operator = call(
        lambda *refs: basis_kernel(peers, False, *refs),
        [((HALF + 1,) + rows, F32)] + [(tall, F32)] * 5, vectors, "basis",
        scale, own[1], own_chip[1], own_far[1], *inside, chip[:around].reshape(rows), far[:around].reshape(rows),
        own[0], own_chip[0], own_far[0],
    )
    seed_chip, seed_far = neighbours(early[HALF], early[HALF])
    (sums,) = call(products_kernel, [((8, 128), F32)], [], "products", early)
    late, sums = call(
        lambda *refs: basis_kernel(peers, True, *refs), [((HALF,) + rows, F32), ((everyone, 128), F32)], vectors, "basis",
        seed_far, *operator, early, sums, early[HALF], seed_chip,
    )
    sums = lax.all_to_all(sums, AXES, 0, 0, tiled=True)
    send, worst = call(
        lambda *refs: last_kernel(around, *refs),
        [((peers, 2, 2, 8, 128), F32), ((8, 128), F32)], [pltpu.VMEM((2,) + rows, F32)], "last", scale, sums, early, late,
    )
    recv = lax.all_to_all(send, GROUP, 0, 0, tiled=True)
    inputs = (
        displacement, load_field, foundation, plastic_flags, point_slot, family_in, family_mid, family_out, family_tan
    )
    good, recv = lax.optimization_barrier((worst[0, 0] < MOST_LOST, recv))
    instead = lax.cond(good, lambda: (jnp.zeros_like(displacement),) * 2, lambda: plain_body(*inputs))
    shape = displacement.shape
    return call(
        lambda *refs: deliver_kernel(path, *refs), [(shape, F32), (shape, F32)], [pltpu.VMEM((2, 128, 128), F32)],
        "deliver", displacement, recv, worst, *instead, grid=(2,), outs=[halves] * 2,
        ins=[
            halves,
            pl.BlockSpec((peers, 1, 2, 8, 128), lambda i: (0, i, 0, 0, 0)),
            pl.BlockSpec((8, 128), lambda i: (0, 0)),
            halves,
            halves,
        ],
    )


def body(*inputs):
    size_x, size_y, size_z = inputs[0].shape
    along, across = lax.axis_size("blk"), lax.axis_size("micro")
    fits = (
        (size_x, size_y, size_z) == (8, 32, 128)
        and across == 4
        and size_z == 8 * along * across
        and lax.axis_size("slab") == 2
        and inputs[5].shape[0] == 4
    )
    if not fits:
        return plain_body(*inputs)
    return tuple(sliced_body(*inputs))


def solution(mesh):
    field = P("blk", "micro", "slab")
    return jax.shard_map(
        body,
        mesh=mesh,
        in_specs=(field,) * 5 + (P(),) * 4,
        out_specs=(field, field),
        check_vma=False,
    )
```

```python
import jax
import jax.numpy as jnp
from jax import lax
from jax.experimental import pallas as pl
from jax.experimental.pallas import tpu as pltpu
from jax.sharding import PartitionSpec as P

ITERS = 8
AXES = ("blk", "slab", "micro")
BF = jnp.bfloat16
F32 = jnp.float32


def split(value):
    high = lax.reduce_precision(value, 8, 7)
    return high.astype(BF), (value - high).astype(BF)


def pack_families(family_in, family_mid, family_out, family_tan):
    families, _, modes = family_in.shape
    spread = jnp.transpose(family_in, (2, 1, 0))
    spread = jnp.concatenate([spread, spread], axis=2).reshape(modes, 6 * families)
    high, low = split(spread)
    weight_in = jnp.concatenate([high, low], axis=1)
    none = jnp.zeros((families, 1, modes), BF)
    stress = jnp.concatenate([family_out, none], axis=1).reshape(4 * families, modes)
    weight_tan = jnp.broadcast_to(family_tan[:, :, None], (families, modes, 128))
    none = jnp.zeros((families, 3, modes), BF)
    tan_high, tan_low = split(family_tan)
    tan_high = jnp.concatenate([none, tan_high[:, None]], axis=1).reshape(4 * families, modes)
    tan_low = jnp.concatenate([none, tan_low[:, None]], axis=1).reshape(4 * families, modes)
    wide = jnp.concatenate(
        [
            jnp.concatenate([stress, tan_high], axis=1),
            jnp.concatenate([jnp.zeros_like(stress), tan_low], axis=1),
        ],
        axis=0,
    )
    return weight_in, family_mid, wide, stress, weight_tan


def cells_kernel(families, planes, strain_ref, code_ref, in_ref, mid_ref, out_ref, *refs, info_ref=None):
    *edges, answer_ref = refs if info_ref is None else refs[1:]
    tan_ref = None if info_ref is None else refs[0]
    modes = in_ref.shape[0]
    step = code_ref.shape[0]
    spots = [(a + i, x) for a in range(0, step, 2) for x in planes for i in range(2)]
    width = len(spots) * 128

    def evaluate(pairs):
        place = lax.broadcasted_iota(jnp.int32, (2 * families, 128), 0)
        column, family_row, flag_row = [], [], []
        for a, x in spots:
            code = code_ref[a, pl.ds(x, 1), :]
            family = lax.shift_right_logical(code, 1)
            picked = lax.rem(place, families) == jnp.broadcast_to(family, place.shape)
            pieces = []
            for j in range(3):
                value = strain_ref[j, a, pl.ds(x, 1), :]
                if edges and j == 2:
                    even, chip_ref, far_ref = edges
                    chip, far = chip_ref[0, pl.ds(a, 1), :], far_ref[0, pl.ds(a, 1), :]
                    beyond = jnp.where(even[...] == (1 if x == 7 else 0), chip, far) * 0.5
                    value = value - beyond if x == 0 else value + beyond
                value = jnp.broadcast_to(value, place.shape)
                high = value.astype(BF).astype(F32)
                piece = jnp.where(place < families, high, value - high)
                pieces.append(jnp.where(picked, piece, 0.0))
            column.append(jnp.concatenate(pieces, axis=0))
            family_row.append(family)
            flag_row.append(lax.bitwise_and(code, 1))
        spread = jnp.concatenate(column, axis=1).astype(BF)
        spread = jnp.concatenate([spread, spread], axis=0)
        family = jnp.concatenate(family_row, axis=1)
        flag = jnp.concatenate(flag_row, axis=1)
        modal = jnp.dot(in_ref[...], spread, preferred_element_type=F32)
        flagged = jnp.broadcast_to(flag, (modes, width)) > 0
        active = jnp.where(flagged, jnp.tanh(modal), modal).astype(BF)
        if pairs is None:
            wide = jnp.broadcast_to(family, (modes, width)).astype(BF)
            nothing = jnp.zeros_like(active)
            stacked = jnp.concatenate(
                [jnp.where(wide == jnp.array(f, BF), active, nothing) for f in range(families)], axis=0
            )
            mixing = jnp.concatenate([mid_ref[f] for f in range(families)], axis=1)
            hidden = jnp.dot(mixing, stacked, preferred_element_type=F32)
        else:
            nothing = jnp.zeros((modes, 256), BF)
            parts = []
            for number, (one, other) in enumerate(pairs):
                part = slice(256 * number, 256 * number + 256)
                ours = jnp.where(family[:, part] == one, 1.0, 0.0)
                ours = jnp.broadcast_to(ours, (modes, 256)).astype(BF) > jnp.array(0.5, BF)
                mine = active[:, part]
                stacked = jnp.concatenate([jnp.where(ours, mine, nothing), jnp.where(ours, nothing, mine)], axis=0)
                mixing = jnp.concatenate([mid_ref[one], mid_ref[other]], axis=1)
                parts.append(jnp.dot(mixing, stacked, preferred_element_type=F32))
            hidden = jnp.concatenate(parts, axis=1)
        bounded = jnp.tanh(hidden).astype(BF)
        if tan_ref is None:
            both = jnp.concatenate([bounded, bounded * bounded], axis=0)
            result = jnp.dot(out_ref[...], both, preferred_element_type=F32)
            result = result[: 4 * families] + result[4 * families :]
        else:
            result = jnp.dot(out_ref[...], bounded, preferred_element_type=F32)
        owner = lax.shift_right_logical(lax.broadcasted_iota(jnp.int32, (4 * families, width), 0), 2)
        result = jnp.where(owner == family, result, 0.0)
        total = result[:4]
        for f in range(1, families):
            total = total + result[4 * f : 4 * f + 4]
        for i, (a, x) in enumerate(spots):
            part = slice(i * 128, (i + 1) * 128)
            if tan_ref is None:
                answer_ref[:, a, x, :] = total[:, part]
                continue
            answer_ref[0:3, a, x, :] = total[0:3, part]
            square = bounded[:, part].astype(F32)
            square = square * square
            owner = jnp.broadcast_to(family_row[i], (modes, 128))
            if pairs is None:
                weight = tan_ref[0]
                for f in range(1, families):
                    weight = jnp.where(owner == f, tan_ref[f], weight)
            else:
                one, other = pairs[i // 2]
                weight = jnp.where(owner == one, tan_ref[one], tan_ref[other])
            answer_ref[3, a, pl.ds(x, 1), :] = jnp.sum(weight * square, axis=0, keepdims=True)

    if info_ref is None:
        evaluate(None)
        return
    first = pl.program_id(0) * (step // 2)
    pairs, more = [], 0
    for a in range(step // 2):
        for x in planes:
            pairs.append((info_ref[x, first + a], info_ref[x, 16 + first + a]))
            more = more + info_ref[x, 32 + first + a]

    @pl.when(more == 0)
    def _():
        evaluate(pairs)

    @pl.when(more != 0)
    def _():
        evaluate(None)


def cells(strain, code, packed, families, step, planes, *edges, info=None):
    weight_in, weight_mid, weight_wide, weight_out, weight_tan = packed
    weights = (weight_in, weight_mid, weight_wide) if info is None else (weight_in, weight_mid, weight_out, weight_tan)
    count = code.shape[0]
    planes = tuple(planes)
    points = count * len(planes) * 128
    modes = weight_in.shape[0]

    def whole(array):
        return pl.BlockSpec(array.shape, lambda i, *_: (0,) * array.ndim)

    def kernel(*refs):
        if info is None:
            cells_kernel(families, planes, *refs)
        else:
            cells_kernel(families, planes, *refs[1:], info_ref=refs[0])

    scalars = () if info is None else (info,)
    return pl.pallas_call(
        kernel,
        grid_spec=pltpu.PrefetchScalarGridSpec(
            num_scalar_prefetch=len(scalars),
            grid=(count // step,),
            in_specs=[
                pl.BlockSpec((3, step, 8, 128), lambda i, *_: (0, i, 0, 0)),
                pl.BlockSpec((step, 8, 128), lambda i, *_: (i, 0, 0)),
            ]
            + [whole(weight) for weight in weights]
            + [pl.BlockSpec((1, 128), lambda i, *_: (0, 0)) for _ in edges[:1]]
            + [pl.BlockSpec((1, 8, 128), lambda i, *_: (count + i, 0, 0)) for _ in edges[1:]],
            out_specs=pl.BlockSpec((4, step, 8, 128), lambda i, *_: (0, i, 0, 0)),
        ),
        out_shape=jax.ShapeDtypeStruct((4, count, 8, 128), F32),
        compiler_params=pltpu.CompilerParams(vmem_limit_bytes=48 * 2**20),
        cost_estimate=pl.CostEstimate(
            flops=2 * points * modes * modes * (families + 1), bytes_accessed=points * 32, transcendentals=2 * points * modes
        ),
        name="cells",
    )(*scalars, strain, code, *weights, *edges)


def global_sum(value):
    count = 1
    for axis in AXES:
        count = count * lax.axis_size(axis)
    spread = jnp.broadcast_to(value.reshape(1, 1), (count, 128))
    return jnp.sum(lax.all_to_all(spread, AXES, 0, 0, tiled=True)[:, 0])


def widened(cells_, axis, dim, width, closed):
    count = lax.axis_size(axis)
    ends = count if closed else count - 1
    head = lax.slice_in_dim(cells_, 0, width, axis=dim)
    tail = lax.slice_in_dim(cells_, cells_.shape[dim] - width, cells_.shape[dim], axis=dim)
    before = lax.ppermute(tail, axis, [(i, (i + 1) % count) for i in range(ends)])
    after = lax.ppermute(head, axis, [((i + 1) % count, i) for i in range(ends)])
    return jnp.concatenate([before, cells_, after], axis=dim)


HALOS = (("blk", True), ("micro", False), ("slab", False))


def widened_all(field, width):
    return [widened(field, axis, dim, width, closed) for dim, (axis, closed) in enumerate(HALOS)]


def difference(field, dim):
    length = field.shape[dim]
    return (lax.slice_in_dim(field, 2, length, axis=dim) - lax.slice_in_dim(field, 0, length - 2, axis=dim)) * 0.5


def plain_body(
    displacement, load_field, foundation, plastic_flags, point_slot, family_in, family_mid, family_out, family_tan
):
    size_x, size_y, size_z = displacement.shape
    points = size_x * size_y * size_z
    families = family_in.shape[0]
    capacity = points // 2
    packed = pack_families(family_in, family_mid, family_out, family_tan)
    strain = [difference(w, dim) for dim, w in enumerate(widened_all(displacement, 1))]
    code = 2 * (point_slot // capacity) + plastic_flags
    tiles = points // 1024
    answers = cells(jnp.stack(strain).reshape(3, tiles, 8, 128), code.reshape(tiles, 8, 128), packed, families, 2, range(8))
    answers = answers.reshape(4, size_x, size_y, size_z)
    tangents = widened_all(0.5 + answers[3], 1)
    divergence = sum(
        difference(widened(answers[dim], axis, dim, 1, closed), dim) for dim, (axis, closed) in enumerate(HALOS)
    )
    rhs = load_field - foundation * displacement + divergence
    solution_ = jnp.zeros_like(rhs)
    residual = rhs
    direction = rhs
    current = global_sum(jnp.sum(residual * residual))
    for _ in range(ITERS):
        total = sum(
            difference(tangents[dim] * difference(w, dim), dim) for dim, w in enumerate(widened_all(direction, 2))
        )
        image = foundation * direction - total
        alpha = current / global_sum(jnp.sum(direction * image))
        solution_ = solution_ + alpha * direction
        residual = residual - alpha * image
        following = global_sum(jnp.sum(residual * residual))
        direction = residual + following / current * direction
        current = following
    return displacement + solution_, residual


VMEM = pl.BlockSpec(memory_space=pltpu.VMEM)
GROUP = ("blk", "micro")


def call(kernel, out_shapes, scratch, name, *args, grid=(), ins=None, outs=None):
    return pl.pallas_call(
        kernel,
        out_shape=[jax.ShapeDtypeStruct(shape, dtype) for shape, dtype in out_shapes],
        grid=grid,
        in_specs=ins or [VMEM] * len(args),
        out_specs=outs or [VMEM] * len(out_shapes),
        scratch_shapes=scratch,
        compiler_params=pltpu.CompilerParams(vmem_limit_bytes=40 * 2**20),
        name=name,
    )(*args)


def regroup(tiles):
    group = lax.broadcasted_iota(jnp.int32, (8, 128), 1) // 32
    result = []
    for a in range(4):
        tile = tiles[0]
        for m in range(4):
            shift = (m - a) * 32 % 128
            moved = pltpu.roll(tiles[m], shift, 1) if shift else tiles[m]
            tile = moved if m == 0 else jnp.where(group == m, moved, tile)
        result.append(tile)
    return result


def place(slab, position, peers):
    return position + slab * (peers - 1 - 2 * position)


def whereabouts(peers):
    across = lax.axis_size("micro")
    b, m, slab = lax.axis_index("blk"), lax.axis_index("micro"), lax.axis_index("slab")
    position = place(slab, b * across + jnp.where(b % 2 == 0, m, across - 1 - m), peers)
    return (slab == 0) & (position == 0), (slab == 1) & (position == peers - 1), position % 2 == 0


def spread_kernel(path, capacity, u_ref, load_ref, found_ref, slot_ref, flag_ref, send_ref, turned):
    peers = len(path)
    slab = lax.axis_index("slab")
    code = flag_ref[...]
    for family in range(1, 4):
        code = code + jnp.where(slot_ref[...] >= family * capacity, 2, 0)
    rest = load_ref[...] - found_ref[...] * u_ref[...]
    for number, value in enumerate((u_ref[...], code.astype(F32), found_ref[...], rest)):
        turned[number] = jnp.transpose(value.reshape(128, 128))
    for target in range(peers):
        start = pl.multiple_of(8 * place(slab, path[target], peers), 8)
        for number in range(4):
            send_ref[target, 0, number] = turned[number, pl.ds(start, 8), :]


def beside(tile, low, high):
    row = lax.broadcasted_iota(jnp.int32, (8, 128), 0)
    after = jnp.where(row == 7, jnp.broadcast_to(high, (8, 128)), pltpu.roll(tile, 7, 0))
    before = jnp.where(row == 0, jnp.broadcast_to(low, (8, 128)), pltpu.roll(tile, 1, 0))
    return after, before


def radial(tile):
    lane = lax.broadcasted_iota(jnp.int32, tile.shape, tile.ndim - 1)
    after = jnp.where(lane == 127, 0.0, pltpu.roll(tile, 127, tile.ndim - 1))
    before = jnp.where(lane == 0, 0.0, pltpu.roll(tile, 1, tile.ndim - 1))
    return (after - before) * 0.5


def row_of(at):
    return at % 8 // 2 * 8 + at // 8 * 2 + at % 2


def collect_kernel(around, tan_ref, recv_ref, strain_ref, code_ref, found_ref, rest_ref, chip_ref, far_ref, scale_ref, u):
    _, _, even = whereabouts(recv_ref.shape[0])
    typical = jnp.sum(jnp.sum(tan_ref[...], axis=1, keepdims=True), axis=0, keepdims=True) / tan_ref.shape[0]
    centre = jnp.broadcast_to(1.1 + 1.4 * (0.5 + 0.33 * typical), (8, 128))
    row = lax.broadcasted_iota(jnp.int32, (8, 128), 0)
    scale_ref[...] = jnp.where(row == 0, centre, jnp.where(row == 1, 1.0 / (centre - 0.4), centre - 0.4))
    for b in range(around // 8):
        for half in range(2):
            for number in range(4):
                tiles = regroup([recv_ref[4 * b + m, half, number] for m in range(4)])
                for a in range(4):
                    at = 8 * b + 4 * half + a
                    if number == 0:
                        u[at] = tiles[a]
                    elif number == 1:
                        code_ref[at] = tiles[a].astype(jnp.int32)
                    elif number == 2:
                        rows = pl.ds(row_of(at), 8, stride=around)
                        found_ref[rows, :] = tiles[a]
                    else:
                        rest_ref[at] = tiles[a]
    nothing = jnp.zeros((1, 128), F32)
    for at in range(around):
        tile = u[at]
        strain_ref[0, at] = (u[(at + 1) % around] - u[(at - 1) % around]) * 0.5
        strain_ref[1, at] = radial(tile)
        after, before = beside(tile, nothing, nothing)
        strain_ref[2, at] = (after - before) * 0.5
        chip_ref[around + at // 8, pl.ds(at % 8, 1), :] = tile[7:8]
        far_ref[around + at // 8, pl.ds(at % 8, 1), :] = tile[0:1]
    for index in range(around):
        value = found_ref[8 * index : 8 * index + 8, :]
        chip_ref[index] = value
        far_ref[index] = value
    for index in range(around, around + around // 8):
        bottom, top = far_ref[index], chip_ref[index]
        chip_ref[index] = jnp.where(even, top, bottom)
        far_ref[index] = jnp.where(even, bottom, top)


def network(count):
    pairs = []
    p = 1
    while p < count:
        k = p
        while k >= 1:
            for j in range(k % p, count - k, 2 * k):
                for i in range(j, min(j + k, count - k)):
                    if i // (2 * p) == (i + k) // (2 * p):
                        pairs.append((i, i + k))
            k //= 2
        p *= 2
    return pairs


def sort_tiles(keys, *carried):
    keys, carried = list(keys), [list(c) for c in carried]
    for i, j in network(len(keys)):
        wrong = keys[i] > keys[j]
        keys[i], keys[j] = jnp.minimum(keys[i], keys[j]), jnp.maximum(keys[i], keys[j])
        for c in carried:
            c[i], c[j] = jnp.where(wrong, c[j], c[i]), jnp.where(wrong, c[i], c[j])
    return keys, carried


def take(tile, index):
    return jnp.take_along_axis(tile, index, axis=1, mode="promise_in_bounds")


def arrange_kernel(around, strain_ref, code_ref, sorted_ref, sorted_code_ref, rank_ref, origin_ref, info_ref):
    lane = lax.broadcasted_iota(jnp.int32, (8, 128), 1)
    right = lax.shift_right_logical
    keys, strains = [], [[], [], []]
    for at in range(around):
        code = code_ref[at]
        shift = right(code, 1) * 8
        counts = lax.shift_left(jnp.ones((8, 128), jnp.int32), shift)
        for step in (1, 2, 4, 8, 16, 32, 64):
            counts = counts + jnp.where(lane >= step, pltpu.roll(counts, step, 1), 0)
        total = jnp.broadcast_to(counts[:, 127:128], (8, 128))
        first = total & 255
        second = first + (right(total, 8) & 255)
        third = second + (right(total, 16) & 255)

        def start(family):
            return jnp.where(
                family < 2, jnp.where(family < 1, 0, first), jnp.where(family < 3, second, third)
            )

        turn = (at % 8 * 16 + at // 8 * 4) % 128
        rank_ref[at] = (start(right(code, 1)) + (right(counts, shift) & 255) + (turn - 1)) & 127
        spot = (lane + (128 - turn)) & 127
        family = (
            jnp.where(spot >= first, 1, 0) + jnp.where(spot >= second, 1, 0) + jnp.where(spot >= third, 1, 0)
        )
        wanted = spot - start(family)
        shift = family * 8
        source = jnp.zeros((8, 128), jnp.int32)
        for step in (64, 32, 16, 8, 4, 2, 1):
            seen = right(take(counts, source + (step - 1)), shift) & 255
            source = jnp.where(seen <= wanted, source + step, source)
        moved = take(code, source)
        keys.append(lax.shift_left(right(moved, 1), jnp.full((8, 128), 6, jnp.int32)) + (2 * at) + (moved & 1))
        for j in range(3):
            strains[j].append(take(strain_ref[j, at], source))
    keys, strains = sort_tiles(keys, *strains)
    info = jnp.zeros((8, 128), jnp.int32)
    for at in range(around):
        family = right(keys[at], 6)
        sorted_code_ref[at] = 2 * family + (keys[at] & 1)
        origin_ref[at] = right(keys[at], 1) & 31
        for j in range(3):
            sorted_ref[j, at] = strains[j][at]
        if at % 2:
            before = right(keys[at - 1], 6)
            low = jnp.min(jnp.minimum(before, family), axis=1, keepdims=True)
            high = jnp.max(jnp.maximum(before, family), axis=1, keepdims=True)
            low, high = jnp.broadcast_to(low, (8, 128)), jnp.broadcast_to(high, (8, 128))
            odd = jnp.where((family != low) & (family != high), 1, 0) + jnp.where((before != low) & (before != high), 1, 0)
            odd = jnp.broadcast_to(jnp.max(odd, axis=1, keepdims=True), (8, 128))
            for number, value in enumerate((low, high, odd)):
                info = jnp.where(lane == 16 * number + at // 2, value, info)
    info_ref[...] = info


def rhs_kernel(around, peers, first_ref, outer_ref, second_ref, rank_ref, origin_ref, rest_ref, chip_ref, far_ref, own_ref, low_ref, high_ref, answers):
    _, _, even = whereabouts(peers)
    for index in range(around // 8):
        low_ref[index] = jnp.where(even, far_ref[index], chip_ref[index])
        high_ref[index] = jnp.where(even, chip_ref[index], far_ref[index])
    row = lax.broadcasted_iota(jnp.int32, (8, 128), 0)
    rim = (row == 0) | (row == 7)

    moved = [[jnp.where(row < 4, first_ref[j, at], second_ref[j, at]) for at in range(around)] for j in range(4)]
    _, moved = sort_tiles([origin_ref[at] for at in range(around)], *moved)
    for at in range(around):
        for j in range(4):
            answers[j, at] = jnp.where(rim, outer_ref[j, at], take(moved[j][at], rank_ref[at]))

    def answer(number, at):
        return answers[number, at]

    cycle = [answer(0, at) for at in range(around)]
    for at in range(around):
        low = low_ref[at // 8, pl.ds(at % 8, 1), :]
        high = high_ref[at // 8, pl.ds(at % 8, 1), :]
        after, before = beside(answer(2, at), low, high)
        divergence = (cycle[(at + 1) % around] - cycle[(at - 1) % around]) * 0.5
        divergence = divergence + radial(answer(1, at)) + (after - before) * 0.5
        rows = pl.ds(row_of(at), 8, stride=around)
        own_ref[0, rows, :] = rest_ref[at] + divergence
        own_ref[1, rows, :] = 0.5 + answer(3, at)


HALF = ITERS // 2
MOST_LOST = 1.0e5


def tile(plane, quarter):
    return slice(32 * plane + 8 * quarter, 32 * plane + 8 * quarter + 8)


def three(peers, own_ref, chip_ref, far_ref, put):
    _, _, even = whereabouts(peers)
    for plane in range(8):
        for quarter in range(4):
            rows = tile(plane, quarter)
            chip, far = chip_ref[rows, :], far_ref[rows, :]
            put(plane, quarter, jnp.where(even, far, chip))
            put(plane + 8, quarter, own_ref[rows, :])
            put(plane + 16, quarter, jnp.where(even, chip, far))


def within_plane(here):
    lane = lax.broadcasted_iota(jnp.int32, (8, 128), 1)
    even_row = lax.broadcasted_iota(jnp.int32, (8, 128), 0) % 2 == 0
    up = [pltpu.roll(value, 7, 0) for value in here]
    down = [pltpu.roll(value, 1, 0) for value in here]
    result = []
    for quarter in range(4):
        after = jnp.where(even_row, up[quarter], down[quarter + 1] if quarter < 3 else up[0])
        before = jnp.where(even_row, up[quarter - 1] if quarter else down[3], down[quarter])
        outer = jnp.where(lane == 127, 0.0, pltpu.roll(here[quarter], 127, 1))
        inner = jnp.where(lane == 0, 0.0, pltpu.roll(here[quarter], 1, 1))
        out = jnp.where(lane >= 126, 0.0, outer)
        result.append((after, out, pltpu.roll(out, 2, 1), (after + before) + (outer + inner)))
    return result


def own_kernel(scale_ref, tan_ref, found_ref, main_ref, after_ref, out_ref, back_ref):
    centre, inverse = scale_ref[0:1, :], scale_ref[1:2, :]
    for plane in range(8):
        parts = within_plane([tan_ref[tile(plane, quarter), :] * (0.25 * inverse) for quarter in range(4)])
        for quarter, (after, out, back, total) in enumerate(parts):
            rows = tile(plane, quarter)
            main_ref[rows, :] = (found_ref[rows, :] - centre) * inverse + total
            after_ref[rows, :] = after
            out_ref[rows, :] = out
            back_ref[rows, :] = back


def operator_kernel(
    peers, scale_ref, tan_ref, tan_chip_ref, tan_far_ref, own_main_ref, own_after_ref, own_out_ref, own_back_ref,
    found_chip_ref, found_far_ref, tan, main, after, out, back
):
    centre, inverse = scale_ref[0:1, :], scale_ref[1:2, :]
    _, _, even = whereabouts(peers)

    def put_tan(plane, quarter, value):
        tan[tile(plane, quarter), :] = value * (0.25 * inverse)

    three(peers, tan_ref, tan_chip_ref, tan_far_ref, put_tan)
    for plane in range(2, 22):
        inside = 8 <= plane < 16
        if not inside:
            parts = within_plane([tan[tile(plane, quarter), :] for quarter in range(4)])
        for quarter in range(4):
            rows = tile(plane, quarter)
            if inside:
                own = tile(plane - 8, quarter)
                total = own_main_ref[own, :]
                after[rows, :] = own_after_ref[own, :]
                out[rows, :] = own_out_ref[own, :]
                back[rows, :] = own_back_ref[own, :]
            else:
                after[rows, :], out[rows, :], back[rows, :], total = parts[quarter]
                there = tile(plane % 8, quarter)
                chip, far = found_chip_ref[there, :], found_far_ref[there, :]
                found = jnp.where(even, far, chip) if plane < 8 else jnp.where(even, chip, far)
                total = total + (found - centre) * inverse
            axial = tan[tile(plane + 1, quarter), :] + tan[tile(plane - 1, quarter), :]
            main[rows, :] = total + axial


def basis_kernel(peers, last, *refs):
    if last:
        seed_far_ref, tan, main, after, out, back, earlier_ref, previous_ref, seed_ref, seed_chip_ref, *refs = refs
        own_ref, sums_ref, vectors = refs
    else:
        operator_refs, (seed_ref, seed_chip_ref, seed_far_ref), refs = refs[:10], refs[10:13], refs[13:]
        own_ref, tan, main, after, out, back, vectors = refs
        operator_kernel(peers, *operator_refs, tan, main, after, out, back)
    is_first, is_last, _ = whereabouts(peers)

    def put_seed(plane, quarter, value):
        vectors[0, tile(plane, quarter), :] = value

    three(peers, seed_ref, seed_chip_ref, seed_far_ref, put_seed)

    def axial(between, plane, degree, quarter):
        term = tan[tile(between, quarter), :] * vectors[degree, tile(plane, quarter), :]
        if between == 8 or between == 15:
            term = jnp.where(is_first if between == 8 else is_last, 0.0, term)
        return term

    def apply(degree, plane, quarter):
        rows = tile(plane, quarter)
        value = vectors[degree, rows, :]
        result = main[rows, :] * value
        if quarter < 3:
            result = result - after[rows, :] * vectors[degree, tile(plane, quarter + 1), :]
        else:
            result = result - after[rows, :] * pltpu.roll(vectors[degree, tile(plane, 0), :], 6, 0)
        before = tile(plane, (quarter - 1) % 4)
        product = after[before, :] * vectors[degree, before, :]
        result = result - (product if quarter else pltpu.roll(product, 2, 0))
        result = result - out[rows, :] * pltpu.roll(value, 126, 1) - back[rows, :] * pltpu.roll(value, 2, 1)
        return result - axial(plane + 1, plane + 2, degree, quarter) - axial(plane - 1, plane - 2, degree, quarter)

    for degree in range(1, HALF + 1):
        for plane in range(2 * degree, 24 - 2 * degree):
            for quarter in range(4):
                value = apply(degree - 1, plane, quarter)
                if degree > 1:
                    value = value + value - vectors[degree - 2, tile(plane, quarter), :]
                vectors[degree, tile(plane, quarter), :] = value
    own_tiles = [(tile(plane, quarter), tile(plane + 8, quarter)) for plane in range(8) for quarter in range(4)]
    if not last:
        for degree in range(HALF + 1):
            for rows, wide_rows in own_tiles:
                own_ref[degree, rows, :] = vectors[degree, wide_rows, :]
        return
    pairs = []
    for degree in range(1, HALF + 1):
        for rows, wide_rows in own_tiles:
            value = vectors[degree, wide_rows, :]
            own_ref[degree - 1, rows, :] = value + value - earlier_ref[HALF - degree, rows, :]
        before = earlier_ref.at[HALF] if degree == 1 else own_ref.at[degree - 2]
        pairs += [(before, own_ref.at[degree - 1]), (own_ref.at[degree - 1], own_ref.at[degree - 1])]
    sums = inner_products(pairs, 2 * HALF + 1, previous_ref[0:1, :])
    sums_ref[...] = jnp.broadcast_to(sums, sums_ref.shape)


def inner_products(pairs, first, sums):
    column = lax.broadcasted_iota(jnp.int32, (1, 128), 1)
    for number, (left, right) in enumerate(pairs):
        total = tree([left[start : start + 8, :] * right[start : start + 8, :] for start in range(0, left.shape[0], 8)])
        entry = jnp.sum(jnp.sum(total, axis=0, keepdims=True), axis=1, keepdims=True)
        sums = jnp.where(column == first + number, jnp.broadcast_to(entry, (1, 128)), sums)
    return sums


def products_kernel(early_ref, sums_ref):
    pairs = []
    for degree in range(HALF + 1):
        if degree:
            pairs.append((early_ref.at[degree - 1], early_ref.at[degree]))
        pairs.append((early_ref.at[degree], early_ref.at[degree]))
    sums = inner_products(pairs, 0, jnp.zeros((1, 128), F32))
    sums_ref[...] = jnp.broadcast_to(sums, sums_ref.shape)


def unpack_gram(all_ref, total):
    row = jnp.sum(all_ref[...], axis=0, keepdims=True)
    moments = []
    for number in range(2 * total - 1):
        entry = jnp.broadcast_to(row[:, number : number + 1], (1, 128))
        moments.append(entry if number < 2 else entry + entry - moments[number % 2])
    gram = {}
    for i in range(total):
        for j in range(i, total):
            gram[i, j] = gram[j, i] = 0.5 * (moments[i + j] + moments[j - i])
    return gram


def tree(terms):
    while len(terms) > 1:
        terms = [a + b for a, b in zip(terms[::2], terms[1::2])] + ([terms[-1]] if len(terms) % 2 else [])
    return terms[0]


def dot(gram, left, right):
    return tree(
        [
            a * tree([gram[i, j] * b for j, b in enumerate(right) if b is not None])
            for i, a in enumerate(left)
            if a is not None
        ]
    )


def axpy(scale, left, right):
    result = []
    for a, b in zip(left, right, strict=True):
        a = None if a is None else (a if scale is None else scale * a)
        result.append(b if a is None else (a if b is None else b + a))
    return result


def times_operator(vector, centre, half_width):
    total = len(vector)
    result = [None] * total
    half = 0.5 * half_width

    def add(index, term):
        result[index] = term if result[index] is None else result[index] + term

    for j, c in enumerate(vector):
        if c is None:
            continue
        add(j, centre * c)
        add(j + 1, (half if j else half_width) * c)
        if j:
            add(j - 1, half * c)
    return result


def iterate(gram, total, centre, half_width):
    residual = [jnp.ones((1, 128), F32)] + [None] * (total - 1)
    direction = residual
    change = [None] * total
    norms = [jnp.sqrt(gram[i, i]) for i in range(total)]
    current = gram[0, 0]
    worst = jnp.zeros((1, 128), F32)
    for step in range(ITERS):
        image = times_operator(direction, centre, half_width)
        alpha = current / dot(gram, direction, image)
        change = axpy(alpha, direction, change)
        residual = axpy(-alpha, image, residual)
        following = dot(gram, residual, residual)
        bound = tree([jnp.abs(c) * n for c, n in zip(residual, norms, strict=True) if c is not None])
        worst = jnp.maximum(worst, bound * bound / following)
        worst = jnp.where(following > 0.0, worst, jnp.inf)
        if step < ITERS - 1:
            direction = axpy(following / current, direction, residual)
        current = following
    return change, residual, worst


def last_kernel(around, scale_ref, all_ref, early_ref, late_ref, send_ref, worst_ref, results):
    total = 2 * HALF + 1
    change, residual, worst = iterate(unpack_gram(all_ref, total), total, scale_ref[0:1, :], scale_ref[2:3, :])
    worst_ref[...] = jnp.broadcast_to(worst, (8, 128))
    for number, part in enumerate((change, residual)):
        part = [None if c is None else jnp.broadcast_to(c, (8, 128)) for c in part]
        for start in range(0, 8 * around, 8):
            rows = slice(start, start + 8)
            results[number, rows, :] = tree(
                [
                    c * (early_ref[index, rows, :] if index <= HALF else late_ref[index - HALF - 1, rows, :])
                    for index, c in enumerate(part)
                    if c is not None
                ]
            )
        for b in range(around // 8):
            for half in range(2):
                tiles = [
                    results[number, pl.ds(row_of(8 * b + 4 * half + a), 8, stride=around), :] for a in range(4)
                ]
                tiles = regroup(tiles)
                for m in range(4):
                    send_ref[4 * b + m, half, number] = tiles[m]


def deliver_kernel(path, u_ref, recv_ref, worst_ref, instead_updated_ref, instead_residual_ref, *refs):
    updated_ref, residual_ref, turned = refs
    slab = lax.axis_index("slab")
    for source in range(recv_ref.shape[0]):
        start = pl.multiple_of(8 * place(slab, path[source], len(path)), 8)
        for index in range(2):
            turned[index, pl.ds(start, 8), :] = recv_ref[source, 0, index]
    good = jnp.broadcast_to(worst_ref[0:1, :] < MOST_LOST, (32, 128))
    change = jnp.transpose(turned[0]).reshape(4, 32, 128)
    residual = jnp.transpose(turned[1]).reshape(4, 32, 128)
    for i in range(4):
        updated_ref[i] = jnp.where(good, u_ref[i] + change[i], instead_updated_ref[i])
        residual_ref[i] = jnp.where(good, residual[i], instead_residual_ref[i])


def sliced_body(
    displacement, load_field, foundation, plastic_flags, point_slot, family_in, family_mid, family_out, family_tan
):
    size_x, size_y, size_z = displacement.shape
    families = family_in.shape[0]
    along, across = lax.axis_size("blk"), lax.axis_size("micro")
    peers = along * across
    around = size_x * along
    everyone = peers * lax.axis_size("slab")
    path = [b * across + (m if b % 2 == 0 else across - 1 - m) for b in range(along) for m in range(across)]
    _, _, even = whereabouts(peers)
    spots = [0] * everyone
    for b in range(along):
        for s in range(2):
            for m in range(across):
                spots[place(s, path[b * across + m], peers) + peers * s] = (b * 2 + s) * across + m

    def swap(first, value):
        pairs = [(spots[i], spots[i + 1]) for i in range(first, everyone - 1, 2)]
        return lax.ppermute(value, AXES, pairs + [(b, a) for a, b in pairs])

    def neighbours(to_chip, to_far):
        far = swap(1, to_far)
        return swap(0, to_chip), far

    packed = pack_families(family_in, family_mid, family_out, family_tan)
    capacity = size_x * size_y * size_z // 2
    halves = pl.BlockSpec((4, 32, 128), lambda i: (i, 0, 0))
    (send,) = call(
        lambda *refs: spread_kernel(path, capacity, *refs),
        [((peers, 2, 4, 8, 128), F32)], [pltpu.VMEM((4, 128, 128), F32)], "spread",
        displacement, load_field, foundation, point_slot, plastic_flags,
        grid=(2,), ins=[halves] * 5, outs=[pl.BlockSpec((peers, 1, 4, 8, 128), lambda i: (0, i, 0, 0, 0))],
    )
    recv = lax.all_to_all(send, GROUP, 0, 0, tiled=True)
    field = (around, 8, 128)
    edge = (around // 8, 8, 128)
    rows = (8 * around, 128)
    message = (around + around // 8, 8, 128)
    strain, code, found, rest, to_chip, to_far, scale = call(
        lambda *refs: collect_kernel(around, *refs),
        [((3,) + field, F32), (field, jnp.int32), (rows, F32), (field, F32), (message, F32), (message, F32), ((8, 128), F32)],
        [pltpu.VMEM(field, F32)], "collect", family_tan, recv,
    )
    chip, far = neighbours(to_chip, to_far)
    grouped, grouped_code, rank, origin, info = call(
        lambda *refs: arrange_kernel(around, *refs),
        [((3,) + field, F32), (field, jnp.int32), (field, jnp.int32), (field, jnp.int32), ((8, 128), jnp.int32)],
        [], "arrange", strain, code,
    )
    first = cells(grouped, grouped_code, packed, families, 8, (1, 2, 3), info=info)
    outer = cells(strain, code, packed, families, 8, (0, 7), jnp.broadcast_to(even.astype(jnp.int32), (1, 128)), chip, far)
    top, bottom = outer[2, :, 7].reshape(edge), outer[2, :, 0].reshape(edge)
    edge_chip, edge_far = neighbours(jnp.where(even, top, bottom), jnp.where(even, bottom, top))
    grouped, outer = lax.optimization_barrier((grouped, outer))
    second = cells(grouped, grouped_code, packed, families, 8, (4, 5, 6), info=info)
    (own,) = call(
        lambda *refs: rhs_kernel(around, peers, *refs), [((2,) + rows, F32)], [pltpu.VMEM(edge, F32)] * 2 + [pltpu.VMEM((4,) + field, F32)], "rhs",
        first, outer, second, rank, origin, rest, edge_chip, edge_far,
    )
    own_chip, own_far = neighbours(own, own)

    tall = (24 * around, 128)
    vectors = [pltpu.VMEM((HALF + 1,) + tall, F32)]
    inside = call(
        own_kernel, [(rows, F32)] * 4, [], "own", scale, own[1], found,
    )
    early, *operator = call(
        lambda *refs: basis_kernel(peers, False, *refs),
        [((HALF + 1,) + rows, F32)] + [(tall, F32)] * 5, vectors, "basis",
        scale, own[1], own_chip[1], own_far[1], *inside, chip[:around].reshape(rows), far[:around].reshape(rows),
        own[0], own_chip[0], own_far[0],
    )
    seed_chip, seed_far = neighbours(early[HALF], early[HALF])
    (sums,) = call(products_kernel, [((8, 128), F32)], [], "products", early)
    late, sums = call(
        lambda *refs: basis_kernel(peers, True, *refs), [((HALF,) + rows, F32), ((everyone, 128), F32)], vectors, "basis",
        seed_far, *operator, early, sums, early[HALF], seed_chip,
    )
    sums = lax.all_to_all(sums, AXES, 0, 0, tiled=True)
    send, worst = call(
        lambda *refs: last_kernel(around, *refs),
        [((peers, 2, 2, 8, 128), F32), ((8, 128), F32)], [pltpu.VMEM((2,) + rows, F32)], "last", scale, sums, early, late,
    )
    recv = lax.all_to_all(send, GROUP, 0, 0, tiled=True)
    inputs = (
        displacement, load_field, foundation, plastic_flags, point_slot, family_in, family_mid, family_out, family_tan
    )
    good, recv = lax.optimization_barrier((worst[0, 0] < MOST_LOST, recv))
    instead = lax.cond(good, lambda: (jnp.zeros_like(displacement),) * 2, lambda: plain_body(*inputs))
    shape = displacement.shape
    return call(
        lambda *refs: deliver_kernel(path, *refs), [(shape, F32), (shape, F32)], [pltpu.VMEM((2, 128, 128), F32)],
        "deliver", displacement, recv, worst, *instead, grid=(2,), outs=[halves] * 2,
        ins=[
            halves,
            pl.BlockSpec((peers, 1, 2, 8, 128), lambda i: (0, i, 0, 0, 0)),
            pl.BlockSpec((8, 128), lambda i: (0, 0)),
            halves,
            halves,
        ],
    )


def body(*inputs):
    size_x, size_y, size_z = inputs[0].shape
    along, across = lax.axis_size("blk"), lax.axis_size("micro")
    fits = (
        (size_x, size_y, size_z) == (8, 32, 128)
        and across == 4
        and size_z == 8 * along * across
        and lax.axis_size("slab") == 2
        and inputs[5].shape[0] == 4
    )
    if not fits:
        return plain_body(*inputs)
    return tuple(sliced_body(*inputs))


def solution(mesh):
    field = P("blk", "micro", "slab")
    return jax.shard_map(
        body,
        mesh=mesh,
        in_specs=(field,) * 5 + (P(),) * 4,
        out_specs=(field, field),
        check_vma=False,
    )
```

```python
import jax
import jax.numpy as jnp
from jax import lax
from jax.experimental import pallas as pl
from jax.experimental.pallas import tpu as pltpu
from jax.sharding import PartitionSpec as P

ITERS = 8
AXES = ("blk", "slab", "micro")
BF = jnp.bfloat16
F32 = jnp.float32


def split(value):
    high = lax.reduce_precision(value, 8, 7)
    return high.astype(BF), (value - high).astype(BF)


def pack_families(family_in, family_mid, family_out, family_tan):
    families, _, modes = family_in.shape
    spread = jnp.transpose(family_in, (2, 1, 0))
    spread = jnp.concatenate([spread, spread], axis=2).reshape(modes, 6 * families)
    high, low = split(spread)
    weight_in = jnp.concatenate([high, low], axis=1)
    none = jnp.zeros((families, 1, modes), BF)
    stress = jnp.concatenate([family_out, none], axis=1).reshape(4 * families, modes)
    weight_tan = jnp.broadcast_to(family_tan[:, :, None], (families, modes, 128))
    none = jnp.zeros((families, 3, modes), BF)
    tan_high, tan_low = split(family_tan)
    tan_high = jnp.concatenate([none, tan_high[:, None]], axis=1).reshape(4 * families, modes)
    tan_low = jnp.concatenate([none, tan_low[:, None]], axis=1).reshape(4 * families, modes)
    wide = jnp.concatenate(
        [
            jnp.concatenate([stress, tan_high], axis=1),
            jnp.concatenate([jnp.zeros_like(stress), tan_low], axis=1),
        ],
        axis=0,
    )
    return weight_in, family_mid, wide, stress, weight_tan


def cells_kernel(families, planes, strain_ref, code_ref, in_ref, mid_ref, out_ref, *refs, info_ref=None):
    *edges, answer_ref = refs if info_ref is None else refs[1:]
    tan_ref = None if info_ref is None else refs[0]
    modes = in_ref.shape[0]
    step = code_ref.shape[0]
    spots = [(a + i, x) for a in range(0, step, 2) for x in planes for i in range(2)]
    width = len(spots) * 128

    def evaluate(pairs):
        place = lax.broadcasted_iota(jnp.int32, (2 * families, 128), 0)
        column, family_row, flag_row = [], [], []
        for a, x in spots:
            code = code_ref[a, pl.ds(x, 1), :]
            family = lax.shift_right_logical(code, 1)
            picked = lax.rem(place, families) == jnp.broadcast_to(family, place.shape)
            pieces = []
            for j in range(3):
                value = strain_ref[j, a, pl.ds(x, 1), :]
                if edges and j == 2:
                    even, chip_ref, far_ref = edges
                    chip, far = chip_ref[a // 8, pl.ds(a % 8, 1), :], far_ref[a // 8, pl.ds(a % 8, 1), :]
                    beyond = jnp.where(even[...] == (1 if x == 7 else 0), chip, far) * 0.5
                    value = value - beyond if x == 0 else value + beyond
                value = jnp.broadcast_to(value, place.shape)
                high = value.astype(BF).astype(F32)
                piece = jnp.where(place < families, high, value - high)
                pieces.append(jnp.where(picked, piece, 0.0))
            column.append(jnp.concatenate(pieces, axis=0))
            family_row.append(family)
            flag_row.append(lax.bitwise_and(code, 1))
        spread = jnp.concatenate(column, axis=1).astype(BF)
        spread = jnp.concatenate([spread, spread], axis=0)
        family = jnp.concatenate(family_row, axis=1)
        flag = jnp.concatenate(flag_row, axis=1)
        modal = jnp.dot(in_ref[...], spread, preferred_element_type=F32)
        flagged = jnp.broadcast_to(flag, (modes, width)) > 0
        active = jnp.where(flagged, jnp.tanh(modal), modal).astype(BF)
        if pairs is None:
            wide = jnp.broadcast_to(family, (modes, width)).astype(BF)
            nothing = jnp.zeros_like(active)
            stacked = jnp.concatenate(
                [jnp.where(wide == jnp.array(f, BF), active, nothing) for f in range(families)], axis=0
            )
            mixing = jnp.concatenate([mid_ref[f] for f in range(families)], axis=1)
            hidden = jnp.dot(mixing, stacked, preferred_element_type=F32)
        else:
            nothing = jnp.zeros((modes, 256), BF)
            parts = []
            for number, (one, other) in enumerate(pairs):
                part = slice(256 * number, 256 * number + 256)
                ours = jnp.where(family[:, part] == one, 1.0, 0.0)
                ours = jnp.broadcast_to(ours, (modes, 256)).astype(BF) > jnp.array(0.5, BF)
                mine = active[:, part]
                stacked = jnp.concatenate([jnp.where(ours, mine, nothing), jnp.where(ours, nothing, mine)], axis=0)
                mixing = jnp.concatenate([mid_ref[one], mid_ref[other]], axis=1)
                parts.append(jnp.dot(mixing, stacked, preferred_element_type=F32))
            hidden = jnp.concatenate(parts, axis=1)
        bounded = jnp.tanh(hidden).astype(BF)
        if tan_ref is None:
            both = jnp.concatenate([bounded, bounded * bounded], axis=0)
            result = jnp.dot(out_ref[...], both, preferred_element_type=F32)
            result = result[: 4 * families] + result[4 * families :]
        else:
            result = jnp.dot(out_ref[...], bounded, preferred_element_type=F32)
        owner = lax.shift_right_logical(lax.broadcasted_iota(jnp.int32, (4 * families, width), 0), 2)
        result = jnp.where(owner == family, result, 0.0)
        total = result[:4]
        for f in range(1, families):
            total = total + result[4 * f : 4 * f + 4]
        for i, (a, x) in enumerate(spots):
            part = slice(i * 128, (i + 1) * 128)
            if tan_ref is None:
                answer_ref[:, a, x, :] = total[:, part]
                continue
            answer_ref[0:3, a, x, :] = total[0:3, part]
            square = bounded[:, part].astype(F32)
            square = square * square
            owner = jnp.broadcast_to(family_row[i], (modes, 128))
            if pairs is None:
                weight = tan_ref[0]
                for f in range(1, families):
                    weight = jnp.where(owner == f, tan_ref[f], weight)
            else:
                one, other = pairs[i // 2]
                weight = jnp.where(owner == one, tan_ref[one], tan_ref[other])
            answer_ref[3, a, pl.ds(x, 1), :] = jnp.sum(weight * square, axis=0, keepdims=True)

    if info_ref is None:
        evaluate(None)
        return
    first = pl.program_id(0) * (step // 2)
    pairs, more = [], 0
    for a in range(step // 2):
        for x in planes:
            pairs.append((info_ref[x, first + a], info_ref[x, 16 + first + a]))
            more = more + info_ref[x, 32 + first + a]

    @pl.when(more == 0)
    def _():
        evaluate(pairs)

    @pl.when(more != 0)
    def _():
        evaluate(None)


def cells(strain, code, packed, families, step, planes, *edges, info=None):
    weight_in, weight_mid, weight_wide, weight_out, weight_tan = packed
    weights = (weight_in, weight_mid, weight_wide) if info is None else (weight_in, weight_mid, weight_out, weight_tan)
    count = code.shape[0]
    planes = tuple(planes)
    points = count * len(planes) * 128
    modes = weight_in.shape[0]

    def whole(array):
        return pl.BlockSpec(array.shape, lambda i, *_: (0,) * array.ndim)

    def kernel(*refs):
        if info is None:
            cells_kernel(families, planes, *refs)
        else:
            cells_kernel(families, planes, *refs[1:], info_ref=refs[0])

    scalars = () if info is None else (info,)
    return pl.pallas_call(
        kernel,
        grid_spec=pltpu.PrefetchScalarGridSpec(
            num_scalar_prefetch=len(scalars),
            grid=(count // step,),
            in_specs=[
                pl.BlockSpec((3, step, 8, 128), lambda i, *_: (0, i, 0, 0)),
                pl.BlockSpec((step, 8, 128), lambda i, *_: (i, 0, 0)),
            ]
            + [whole(weight) for weight in weights]
            + [pl.BlockSpec((1, 128), lambda i, *_: (0, 0)) for _ in edges[:1]]
            + [pl.BlockSpec((step // 8, 8, 128), lambda i, *_: (count * 8 // step + i, 0, 0)) for _ in edges[1:]],
            out_specs=pl.BlockSpec((4, step, 8, 128), lambda i, *_: (0, i, 0, 0)),
        ),
        out_shape=jax.ShapeDtypeStruct((4, count, 8, 128), F32),
        compiler_params=pltpu.CompilerParams(vmem_limit_bytes=48 * 2**20),
        cost_estimate=pl.CostEstimate(
            flops=2 * points * modes * modes * (families + 1), bytes_accessed=points * 32, transcendentals=2 * points * modes
        ),
        name="cells",
    )(*scalars, strain, code, *weights, *edges)


def global_sum(value):
    count = 1
    for axis in AXES:
        count = count * lax.axis_size(axis)
    spread = jnp.broadcast_to(value.reshape(1, 1), (count, 128))
    return jnp.sum(lax.all_to_all(spread, AXES, 0, 0, tiled=True)[:, 0])


def widened(cells_, axis, dim, width, closed):
    count = lax.axis_size(axis)
    ends = count if closed else count - 1
    head = lax.slice_in_dim(cells_, 0, width, axis=dim)
    tail = lax.slice_in_dim(cells_, cells_.shape[dim] - width, cells_.shape[dim], axis=dim)
    before = lax.ppermute(tail, axis, [(i, (i + 1) % count) for i in range(ends)])
    after = lax.ppermute(head, axis, [((i + 1) % count, i) for i in range(ends)])
    return jnp.concatenate([before, cells_, after], axis=dim)


HALOS = (("blk", True), ("micro", False), ("slab", False))


def widened_all(field, width):
    return [widened(field, axis, dim, width, closed) for dim, (axis, closed) in enumerate(HALOS)]


def difference(field, dim):
    length = field.shape[dim]
    return (lax.slice_in_dim(field, 2, length, axis=dim) - lax.slice_in_dim(field, 0, length - 2, axis=dim)) * 0.5


def plain_body(
    displacement, load_field, foundation, plastic_flags, point_slot, family_in, family_mid, family_out, family_tan
):
    size_x, size_y, size_z = displacement.shape
    points = size_x * size_y * size_z
    families = family_in.shape[0]
    capacity = points // 2
    packed = pack_families(family_in, family_mid, family_out, family_tan)
    strain = [difference(w, dim) for dim, w in enumerate(widened_all(displacement, 1))]
    code = 2 * (point_slot // capacity) + plastic_flags
    tiles = points // 1024
    answers = cells(jnp.stack(strain).reshape(3, tiles, 8, 128), code.reshape(tiles, 8, 128), packed, families, 2, range(8))
    answers = answers.reshape(4, size_x, size_y, size_z)
    tangents = widened_all(0.5 + answers[3], 1)
    divergence = sum(
        difference(widened(answers[dim], axis, dim, 1, closed), dim) for dim, (axis, closed) in enumerate(HALOS)
    )
    rhs = load_field - foundation * displacement + divergence
    solution_ = jnp.zeros_like(rhs)
    residual = rhs
    direction = rhs
    current = global_sum(jnp.sum(residual * residual))
    for _ in range(ITERS):
        total = sum(
            difference(tangents[dim] * difference(w, dim), dim) for dim, w in enumerate(widened_all(direction, 2))
        )
        image = foundation * direction - total
        alpha = current / global_sum(jnp.sum(direction * image))
        solution_ = solution_ + alpha * direction
        residual = residual - alpha * image
        following = global_sum(jnp.sum(residual * residual))
        direction = residual + following / current * direction
        current = following
    return displacement + solution_, residual


VMEM = pl.BlockSpec(memory_space=pltpu.VMEM)
GROUP = ("blk", "micro")


def call(kernel, out_shapes, scratch, name, *args, grid=(), ins=None, outs=None):
    return pl.pallas_call(
        kernel,
        out_shape=[jax.ShapeDtypeStruct(shape, dtype) for shape, dtype in out_shapes],
        grid=grid,
        in_specs=ins or [VMEM] * len(args),
        out_specs=outs or [VMEM] * len(out_shapes),
        scratch_shapes=scratch,
        compiler_params=pltpu.CompilerParams(vmem_limit_bytes=40 * 2**20),
        name=name,
    )(*args)


def regroup(tiles):
    group = lax.broadcasted_iota(jnp.int32, (8, 128), 1) // 32
    result = []
    for a in range(4):
        tile = tiles[0]
        for m in range(4):
            shift = (m - a) * 32 % 128
            moved = pltpu.roll(tiles[m], shift, 1) if shift else tiles[m]
            tile = moved if m == 0 else jnp.where(group == m, moved, tile)
        result.append(tile)
    return result


def place(slab, position, peers):
    return position + slab * (peers - 1 - 2 * position)


def whereabouts(peers):
    across = lax.axis_size("micro")
    b, m, slab = lax.axis_index("blk"), lax.axis_index("micro"), lax.axis_index("slab")
    position = place(slab, b * across + jnp.where(b % 2 == 0, m, across - 1 - m), peers)
    return (slab == 0) & (position == 0), (slab == 1) & (position == peers - 1), position % 2 == 0


def spread_kernel(path, capacity, u_ref, load_ref, found_ref, slot_ref, flag_ref, send_ref, turned):
    peers = len(path)
    slab = lax.axis_index("slab")
    code = flag_ref[...]
    for family in range(1, 4):
        code = code + jnp.where(slot_ref[...] >= family * capacity, 2, 0)
    rest = load_ref[...] - found_ref[...] * u_ref[...]
    for number, value in enumerate((u_ref[...], code.astype(F32), found_ref[...], rest)):
        turned[number] = jnp.transpose(value.reshape(128, 128))
    for target in range(peers):
        start = pl.multiple_of(8 * place(slab, path[target], peers), 8)
        for number in range(4):
            send_ref[target, 0, number] = turned[number, pl.ds(start, 8), :]


def beside(tile, low, high):
    row = lax.broadcasted_iota(jnp.int32, (8, 128), 0)
    after = jnp.where(row == 7, jnp.broadcast_to(high, (8, 128)), pltpu.roll(tile, 7, 0))
    before = jnp.where(row == 0, jnp.broadcast_to(low, (8, 128)), pltpu.roll(tile, 1, 0))
    return after, before


def radial(tile):
    lane = lax.broadcasted_iota(jnp.int32, tile.shape, tile.ndim - 1)
    after = jnp.where(lane == 127, 0.0, pltpu.roll(tile, 127, tile.ndim - 1))
    before = jnp.where(lane == 0, 0.0, pltpu.roll(tile, 1, tile.ndim - 1))
    return (after - before) * 0.5


def row_of(at):
    return at % 8 // 2 * 8 + at // 8 * 2 + at % 2


def collect_kernel(around, tan_ref, recv_ref, strain_ref, code_ref, found_ref, rest_ref, chip_ref, far_ref, scale_ref, u):
    _, _, even = whereabouts(recv_ref.shape[0])
    typical = jnp.sum(jnp.sum(tan_ref[...], axis=1, keepdims=True), axis=0, keepdims=True) / tan_ref.shape[0]
    centre = jnp.broadcast_to(1.1 + 1.4 * (0.5 + 0.33 * typical), (8, 128))
    row = lax.broadcasted_iota(jnp.int32, (8, 128), 0)
    scale_ref[...] = jnp.where(row == 0, centre, jnp.where(row == 1, 1.0 / (centre - 0.4), centre - 0.4))
    for b in range(around // 8):
        for half in range(2):
            for number in range(4):
                tiles = regroup([recv_ref[4 * b + m, half, number] for m in range(4)])
                for a in range(4):
                    at = 8 * b + 4 * half + a
                    if number == 0:
                        u[at] = tiles[a]
                    elif number == 1:
                        code_ref[at] = tiles[a].astype(jnp.int32)
                    elif number == 2:
                        rows = pl.ds(row_of(at), 8, stride=around)
                        found_ref[rows, :] = tiles[a]
                    else:
                        rest_ref[at] = tiles[a]
    nothing = jnp.zeros((1, 128), F32)
    for at in range(around):
        tile = u[at]
        strain_ref[0, at] = (u[(at + 1) % around] - u[(at - 1) % around]) * 0.5
        strain_ref[1, at] = radial(tile)
        after, before = beside(tile, nothing, nothing)
        strain_ref[2, at] = (after - before) * 0.5
        chip_ref[around + at // 8, pl.ds(at % 8, 1), :] = tile[7:8]
        far_ref[around + at // 8, pl.ds(at % 8, 1), :] = tile[0:1]
    for index in range(around):
        value = found_ref[8 * index : 8 * index + 8, :]
        chip_ref[index] = value
        far_ref[index] = value
    for index in range(around, around + around // 8):
        bottom, top = far_ref[index], chip_ref[index]
        chip_ref[index] = jnp.where(even, top, bottom)
        far_ref[index] = jnp.where(even, bottom, top)


def network(count):
    pairs = []
    p = 1
    while p < count:
        k = p
        while k >= 1:
            for j in range(k % p, count - k, 2 * k):
                for i in range(j, min(j + k, count - k)):
                    if i // (2 * p) == (i + k) // (2 * p):
                        pairs.append((i, i + k))
            k //= 2
        p *= 2
    return pairs


def sort_tiles(keys, *carried):
    keys, carried = list(keys), [list(c) for c in carried]
    for i, j in network(len(keys)):
        wrong = keys[i] > keys[j]
        keys[i], keys[j] = jnp.minimum(keys[i], keys[j]), jnp.maximum(keys[i], keys[j])
        for c in carried:
            c[i], c[j] = jnp.where(wrong, c[j], c[i]), jnp.where(wrong, c[i], c[j])
    return keys, carried


def take(tile, index):
    return jnp.take_along_axis(tile, index, axis=1, mode="promise_in_bounds")


def arrange_kernel(around, strain_ref, code_ref, sorted_ref, sorted_code_ref, rank_ref, origin_ref, info_ref):
    lane = lax.broadcasted_iota(jnp.int32, (8, 128), 1)
    right = lax.shift_right_logical
    keys, strains = [], [[], [], []]
    for at in range(around):
        code = code_ref[at]
        shift = right(code, 1) * 8
        counts = lax.shift_left(jnp.ones((8, 128), jnp.int32), shift)
        for step in (1, 2, 4, 8, 16, 32, 64):
            counts = counts + jnp.where(lane >= step, pltpu.roll(counts, step, 1), 0)
        total = jnp.broadcast_to(counts[:, 127:128], (8, 128))
        first = total & 255
        second = first + (right(total, 8) & 255)
        third = second + (right(total, 16) & 255)

        def start(family):
            return jnp.where(
                family < 2, jnp.where(family < 1, 0, first), jnp.where(family < 3, second, third)
            )

        turn = (at % 8 * 16 + at // 8 * 4) % 128
        rank_ref[at] = (start(right(code, 1)) + (right(counts, shift) & 255) + (turn - 1)) & 127
        spot = (lane + (128 - turn)) & 127
        family = (
            jnp.where(spot >= first, 1, 0) + jnp.where(spot >= second, 1, 0) + jnp.where(spot >= third, 1, 0)
        )
        wanted = spot - start(family)
        shift = family * 8
        source = jnp.zeros((8, 128), jnp.int32)
        for step in (64, 32, 16, 8, 4, 2, 1):
            seen = right(take(counts, source + (step - 1)), shift) & 255
            source = jnp.where(seen <= wanted, source + step, source)
        moved = take(code, source)
        keys.append(lax.shift_left(right(moved, 1), jnp.full((8, 128), 6, jnp.int32)) + (2 * at) + (moved & 1))
        for j in range(3):
            strains[j].append(take(strain_ref[j, at], source))
    keys, strains = sort_tiles(keys, *strains)
    info = jnp.zeros((8, 128), jnp.int32)
    for at in range(around):
        family = right(keys[at], 6)
        sorted_code_ref[at] = 2 * family + (keys[at] & 1)
        origin_ref[at] = right(keys[at], 1) & 31
        for j in range(3):
            sorted_ref[j, at] = strains[j][at]
        if at % 2:
            before = right(keys[at - 1], 6)
            low = jnp.min(jnp.minimum(before, family), axis=1, keepdims=True)
            high = jnp.max(jnp.maximum(before, family), axis=1, keepdims=True)
            low, high = jnp.broadcast_to(low, (8, 128)), jnp.broadcast_to(high, (8, 128))
            odd = jnp.where((family != low) & (family != high), 1, 0) + jnp.where((before != low) & (before != high), 1, 0)
            odd = jnp.broadcast_to(jnp.max(odd, axis=1, keepdims=True), (8, 128))
            for number, value in enumerate((low, high, odd)):
                info = jnp.where(lane == 16 * number + at // 2, value, info)
    info_ref[...] = info


def rhs_kernel(around, peers, first_ref, outer_ref, second_ref, rank_ref, origin_ref, rest_ref, chip_ref, far_ref, own_ref, low_ref, high_ref, answers):
    _, _, even = whereabouts(peers)
    for index in range(around // 8):
        low_ref[index] = jnp.where(even, far_ref[index], chip_ref[index])
        high_ref[index] = jnp.where(even, chip_ref[index], far_ref[index])
    row = lax.broadcasted_iota(jnp.int32, (8, 128), 0)
    rim = (row == 0) | (row == 7)

    moved = [[jnp.where(row < 4, first_ref[j, at], second_ref[j, at]) for at in range(around)] for j in range(4)]
    _, moved = sort_tiles([origin_ref[at] for at in range(around)], *moved)
    for at in range(around):
        for j in range(4):
            answers[j, at] = jnp.where(rim, outer_ref[j, at], take(moved[j][at], rank_ref[at]))

    def answer(number, at):
        return answers[number, at]

    cycle = [answer(0, at) for at in range(around)]
    for at in range(around):
        low = low_ref[at // 8, pl.ds(at % 8, 1), :]
        high = high_ref[at // 8, pl.ds(at % 8, 1), :]
        after, before = beside(answer(2, at), low, high)
        divergence = (cycle[(at + 1) % around] - cycle[(at - 1) % around]) * 0.5
        divergence = divergence + radial(answer(1, at)) + (after - before) * 0.5
        rows = pl.ds(row_of(at), 8, stride=around)
        own_ref[0, rows, :] = rest_ref[at] + divergence
        own_ref[1, rows, :] = 0.5 + answer(3, at)


HALF = ITERS // 2
MOST_LOST = 1.0e5


def tile(plane, quarter):
    return slice(32 * plane + 8 * quarter, 32 * plane + 8 * quarter + 8)


def three(peers, own_ref, chip_ref, far_ref, put):
    _, _, even = whereabouts(peers)
    for plane in range(8):
        for quarter in range(4):
            rows = tile(plane, quarter)
            chip, far = chip_ref[rows, :], far_ref[rows, :]
            put(plane, quarter, jnp.where(even, far, chip))
            put(plane + 8, quarter, own_ref[rows, :])
            put(plane + 16, quarter, jnp.where(even, chip, far))


def within_plane(here):
    lane = lax.broadcasted_iota(jnp.int32, (8, 128), 1)
    even_row = lax.broadcasted_iota(jnp.int32, (8, 128), 0) % 2 == 0
    up = [pltpu.roll(value, 7, 0) for value in here]
    down = [pltpu.roll(value, 1, 0) for value in here]
    result = []
    for quarter in range(4):
        after = jnp.where(even_row, up[quarter], down[quarter + 1] if quarter < 3 else up[0])
        before = jnp.where(even_row, up[quarter - 1] if quarter else down[3], down[quarter])
        outer = jnp.where(lane == 127, 0.0, pltpu.roll(here[quarter], 127, 1))
        inner = jnp.where(lane == 0, 0.0, pltpu.roll(here[quarter], 1, 1))
        out = jnp.where(lane >= 126, 0.0, outer)
        result.append((after, out, pltpu.roll(out, 2, 1), (after + before) + (outer + inner)))
    return result


def own_kernel(scale_ref, tan_ref, found_ref, main_ref, after_ref, out_ref, back_ref):
    centre, inverse = scale_ref[0:1, :], scale_ref[1:2, :]
    for plane in range(8):
        parts = within_plane([tan_ref[tile(plane, quarter), :] * (0.25 * inverse) for quarter in range(4)])
        for quarter, (after, out, back, total) in enumerate(parts):
            rows = tile(plane, quarter)
            main_ref[rows, :] = (found_ref[rows, :] - centre) * inverse + total
            after_ref[rows, :] = after
            out_ref[rows, :] = out
            back_ref[rows, :] = back


def operator_kernel(
    peers, scale_ref, tan_ref, tan_chip_ref, tan_far_ref, own_main_ref, own_after_ref, own_out_ref, own_back_ref,
    found_chip_ref, found_far_ref, tan, main, after, out, back
):
    centre, inverse = scale_ref[0:1, :], scale_ref[1:2, :]
    _, _, even = whereabouts(peers)

    def put_tan(plane, quarter, value):
        tan[tile(plane, quarter), :] = value * (0.25 * inverse)

    three(peers, tan_ref, tan_chip_ref, tan_far_ref, put_tan)
    for plane in range(2, 22):
        inside = 8 <= plane < 16
        if not inside:
            parts = within_plane([tan[tile(plane, quarter), :] for quarter in range(4)])
        for quarter in range(4):
            rows = tile(plane, quarter)
            if inside:
                own = tile(plane - 8, quarter)
                total = own_main_ref[own, :]
                after[rows, :] = own_after_ref[own, :]
                out[rows, :] = own_out_ref[own, :]
                back[rows, :] = own_back_ref[own, :]
            else:
                after[rows, :], out[rows, :], back[rows, :], total = parts[quarter]
                there = tile(plane % 8, quarter)
                chip, far = found_chip_ref[there, :], found_far_ref[there, :]
                found = jnp.where(even, far, chip) if plane < 8 else jnp.where(even, chip, far)
                total = total + (found - centre) * inverse
            axial = tan[tile(plane + 1, quarter), :] + tan[tile(plane - 1, quarter), :]
            main[rows, :] = total + axial


def basis_kernel(peers, last, *refs):
    if last:
        seed_far_ref, tan, main, after, out, back, earlier_ref, previous_ref, seed_ref, seed_chip_ref, *refs = refs
        own_ref, sums_ref, vectors = refs
    else:
        operator_refs, (seed_ref, seed_chip_ref, seed_far_ref), refs = refs[:10], refs[10:13], refs[13:]
        own_ref, tan, main, after, out, back, vectors = refs
        operator_kernel(peers, *operator_refs, tan, main, after, out, back)
    is_first, is_last, _ = whereabouts(peers)

    def put_seed(plane, quarter, value):
        vectors[0, tile(plane, quarter), :] = value

    three(peers, seed_ref, seed_chip_ref, seed_far_ref, put_seed)

    def axial(between, plane, degree, quarter):
        term = tan[tile(between, quarter), :] * vectors[degree, tile(plane, quarter), :]
        if between == 8 or between == 15:
            term = jnp.where(is_first if between == 8 else is_last, 0.0, term)
        return term

    def apply(degree, plane, quarter):
        rows = tile(plane, quarter)
        value = vectors[degree, rows, :]
        result = main[rows, :] * value
        if quarter < 3:
            result = result - after[rows, :] * vectors[degree, tile(plane, quarter + 1), :]
        else:
            result = result - after[rows, :] * pltpu.roll(vectors[degree, tile(plane, 0), :], 6, 0)
        before = tile(plane, (quarter - 1) % 4)
        product = after[before, :] * vectors[degree, before, :]
        result = result - (product if quarter else pltpu.roll(product, 2, 0))
        result = result - out[rows, :] * pltpu.roll(value, 126, 1) - back[rows, :] * pltpu.roll(value, 2, 1)
        return result - axial(plane + 1, plane + 2, degree, quarter) - axial(plane - 1, plane - 2, degree, quarter)

    for degree in range(1, HALF + 1):
        for plane in range(2 * degree, 24 - 2 * degree):
            for quarter in range(4):
                value = apply(degree - 1, plane, quarter)
                if degree > 1:
                    value = value + value - vectors[degree - 2, tile(plane, quarter), :]
                vectors[degree, tile(plane, quarter), :] = value
    own_tiles = [(tile(plane, quarter), tile(plane + 8, quarter)) for plane in range(8) for quarter in range(4)]
    if not last:
        for degree in range(HALF + 1):
            for rows, wide_rows in own_tiles:
                own_ref[degree, rows, :] = vectors[degree, wide_rows, :]
        return
    pairs = []
    for degree in range(1, HALF + 1):
        for rows, wide_rows in own_tiles:
            value = vectors[degree, wide_rows, :]
            own_ref[degree - 1, rows, :] = value + value - earlier_ref[HALF - degree, rows, :]
        before = earlier_ref.at[HALF] if degree == 1 else own_ref.at[degree - 2]
        pairs += [(before, own_ref.at[degree - 1]), (own_ref.at[degree - 1], own_ref.at[degree - 1])]
    sums = inner_products(pairs, 2 * HALF + 1, previous_ref[0:1, :])
    sums_ref[...] = jnp.broadcast_to(sums, sums_ref.shape)


def inner_products(pairs, first, sums):
    column = lax.broadcasted_iota(jnp.int32, (1, 128), 1)
    for number, (left, right) in enumerate(pairs):
        total = tree([left[start : start + 8, :] * right[start : start + 8, :] for start in range(0, left.shape[0], 8)])
        entry = jnp.sum(jnp.sum(total, axis=0, keepdims=True), axis=1, keepdims=True)
        sums = jnp.where(column == first + number, jnp.broadcast_to(entry, (1, 128)), sums)
    return sums


def products_kernel(early_ref, sums_ref):
    pairs = []
    for degree in range(HALF + 1):
        if degree:
            pairs.append((early_ref.at[degree - 1], early_ref.at[degree]))
        pairs.append((early_ref.at[degree], early_ref.at[degree]))
    sums = inner_products(pairs, 0, jnp.zeros((1, 128), F32))
    sums_ref[...] = jnp.broadcast_to(sums, sums_ref.shape)


def unpack_gram(all_ref, total):
    row = jnp.sum(all_ref[...], axis=0, keepdims=True)
    moments = []
    for number in range(2 * total - 1):
        entry = jnp.broadcast_to(row[:, number : number + 1], (1, 128))
        moments.append(entry if number < 2 else entry + entry - moments[number % 2])
    gram = {}
    for i in range(total):
        for j in range(i, total):
            gram[i, j] = gram[j, i] = 0.5 * (moments[i + j] + moments[j - i])
    return gram


def tree(terms):
    while len(terms) > 1:
        terms = [a + b for a, b in zip(terms[::2], terms[1::2])] + ([terms[-1]] if len(terms) % 2 else [])
    return terms[0]


def dot(gram, left, right):
    return tree(
        [
            a * tree([gram[i, j] * b for j, b in enumerate(right) if b is not None])
            for i, a in enumerate(left)
            if a is not None
        ]
    )


def axpy(scale, left, right):
    result = []
    for a, b in zip(left, right, strict=True):
        a = None if a is None else (a if scale is None else scale * a)
        result.append(b if a is None else (a if b is None else b + a))
    return result


def times_operator(vector, centre, half_width):
    total = len(vector)
    result = [None] * total
    half = 0.5 * half_width

    def add(index, term):
        result[index] = term if result[index] is None else result[index] + term

    for j, c in enumerate(vector):
        if c is None:
            continue
        add(j, centre * c)
        add(j + 1, (half if j else half_width) * c)
        if j:
            add(j - 1, half * c)
    return result


def iterate(gram, total, centre, half_width):
    residual = [jnp.ones((1, 128), F32)] + [None] * (total - 1)
    direction = residual
    change = [None] * total
    norms = [jnp.sqrt(gram[i, i]) for i in range(total)]
    current = gram[0, 0]
    worst = jnp.zeros((1, 128), F32)
    for step in range(ITERS):
        image = times_operator(direction, centre, half_width)
        alpha = current / dot(gram, direction, image)
        change = axpy(alpha, direction, change)
        residual = axpy(-alpha, image, residual)
        following = dot(gram, residual, residual)
        bound = tree([jnp.abs(c) * n for c, n in zip(residual, norms, strict=True) if c is not None])
        worst = jnp.maximum(worst, bound * bound / following)
        worst = jnp.where(following > 0.0, worst, jnp.inf)
        if step < ITERS - 1:
            direction = axpy(following / current, direction, residual)
        current = following
    return change, residual, worst


def last_kernel(around, scale_ref, all_ref, early_ref, late_ref, send_ref, worst_ref, results):
    total = 2 * HALF + 1
    change, residual, worst = iterate(unpack_gram(all_ref, total), total, scale_ref[0:1, :], scale_ref[2:3, :])
    worst_ref[...] = jnp.broadcast_to(worst, (8, 128))
    for number, part in enumerate((change, residual)):
        part = [None if c is None else jnp.broadcast_to(c, (8, 128)) for c in part]
        for start in range(0, 8 * around, 8):
            rows = slice(start, start + 8)
            results[number, rows, :] = tree(
                [
                    c * (early_ref[index, rows, :] if index <= HALF else late_ref[index - HALF - 1, rows, :])
                    for index, c in enumerate(part)
                    if c is not None
                ]
            )
        for b in range(around // 8):
            for half in range(2):
                tiles = [
                    results[number, pl.ds(row_of(8 * b + 4 * half + a), 8, stride=around), :] for a in range(4)
                ]
                tiles = regroup(tiles)
                for m in range(4):
                    send_ref[4 * b + m, half, number] = tiles[m]


def deliver_kernel(path, u_ref, recv_ref, worst_ref, instead_updated_ref, instead_residual_ref, *refs):
    updated_ref, residual_ref, turned = refs
    slab = lax.axis_index("slab")
    for source in range(recv_ref.shape[0]):
        start = pl.multiple_of(8 * place(slab, path[source], len(path)), 8)
        for index in range(2):
            turned[index, pl.ds(start, 8), :] = recv_ref[source, 0, index]
    good = jnp.broadcast_to(worst_ref[0:1, :] < MOST_LOST, (32, 128))
    change = jnp.transpose(turned[0]).reshape(4, 32, 128)
    residual = jnp.transpose(turned[1]).reshape(4, 32, 128)
    for i in range(4):
        updated_ref[i] = jnp.where(good, u_ref[i] + change[i], instead_updated_ref[i])
        residual_ref[i] = jnp.where(good, residual[i], instead_residual_ref[i])


def sliced_body(
    displacement, load_field, foundation, plastic_flags, point_slot, family_in, family_mid, family_out, family_tan
):
    size_x, size_y, size_z = displacement.shape
    families = family_in.shape[0]
    along, across = lax.axis_size("blk"), lax.axis_size("micro")
    peers = along * across
    around = size_x * along
    everyone = peers * lax.axis_size("slab")
    path = [b * across + (m if b % 2 == 0 else across - 1 - m) for b in range(along) for m in range(across)]
    _, _, even = whereabouts(peers)
    spots = [0] * everyone
    for b in range(along):
        for s in range(2):
            for m in range(across):
                spots[place(s, path[b * across + m], peers) + peers * s] = (b * 2 + s) * across + m

    def swap(first, value):
        pairs = [(spots[i], spots[i + 1]) for i in range(first, everyone - 1, 2)]
        return lax.ppermute(value, AXES, pairs + [(b, a) for a, b in pairs])

    def neighbours(to_chip, to_far):
        far = swap(1, to_far)
        return swap(0, to_chip), far

    packed = pack_families(family_in, family_mid, family_out, family_tan)
    capacity = size_x * size_y * size_z // 2
    halves = pl.BlockSpec((4, 32, 128), lambda i: (i, 0, 0))
    (send,) = call(
        lambda *refs: spread_kernel(path, capacity, *refs),
        [((peers, 2, 4, 8, 128), F32)], [pltpu.VMEM((4, 128, 128), F32)], "spread",
        displacement, load_field, foundation, point_slot, plastic_flags,
        grid=(2,), ins=[halves] * 5, outs=[pl.BlockSpec((peers, 1, 4, 8, 128), lambda i: (0, i, 0, 0, 0))],
    )
    recv = lax.all_to_all(send, GROUP, 0, 0, tiled=True)
    field = (around, 8, 128)
    edge = (around // 8, 8, 128)
    rows = (8 * around, 128)
    message = (around + around // 8, 8, 128)
    strain, code, found, rest, to_chip, to_far, scale = call(
        lambda *refs: collect_kernel(around, *refs),
        [((3,) + field, F32), (field, jnp.int32), (rows, F32), (field, F32), (message, F32), (message, F32), ((8, 128), F32)],
        [pltpu.VMEM(field, F32)], "collect", family_tan, recv,
    )
    chip, far = neighbours(to_chip, to_far)
    grouped, grouped_code, rank, origin, info = call(
        lambda *refs: arrange_kernel(around, *refs),
        [((3,) + field, F32), (field, jnp.int32), (field, jnp.int32), (field, jnp.int32), ((8, 128), jnp.int32)],
        [], "arrange", strain, code,
    )
    first = cells(grouped, grouped_code, packed, families, 8, (1, 2, 3), info=info)
    outer = cells(strain, code, packed, families, 16, (0, 7), jnp.broadcast_to(even.astype(jnp.int32), (1, 128)), chip, far)
    top, bottom = outer[2, :, 7].reshape(edge), outer[2, :, 0].reshape(edge)
    edge_chip, edge_far = neighbours(jnp.where(even, top, bottom), jnp.where(even, bottom, top))
    grouped, outer = lax.optimization_barrier((grouped, outer))
    second = cells(grouped, grouped_code, packed, families, 8, (4, 5, 6), info=info)
    (own,) = call(
        lambda *refs: rhs_kernel(around, peers, *refs), [((2,) + rows, F32)], [pltpu.VMEM(edge, F32)] * 2 + [pltpu.VMEM((4,) + field, F32)], "rhs",
        first, outer, second, rank, origin, rest, edge_chip, edge_far,
    )
    own_chip, own_far = neighbours(own, own)

    tall = (24 * around, 128)
    vectors = [pltpu.VMEM((HALF + 1,) + tall, F32)]
    inside = call(
        own_kernel, [(rows, F32)] * 4, [], "own", scale, own[1], found,
    )
    early, *operator = call(
        lambda *refs: basis_kernel(peers, False, *refs),
        [((HALF + 1,) + rows, F32)] + [(tall, F32)] * 5, vectors, "basis",
        scale, own[1], own_chip[1], own_far[1], *inside, chip[:around].reshape(rows), far[:around].reshape(rows),
        own[0], own_chip[0], own_far[0],
    )
    seed_chip, seed_far = neighbours(early[HALF], early[HALF])
    (sums,) = call(products_kernel, [((8, 128), F32)], [], "products", early)
    late, sums = call(
        lambda *refs: basis_kernel(peers, True, *refs), [((HALF,) + rows, F32), ((everyone, 128), F32)], vectors, "basis",
        seed_far, *operator, early, sums, early[HALF], seed_chip,
    )
    sums = lax.all_to_all(sums, AXES, 0, 0, tiled=True)
    send, worst = call(
        lambda *refs: last_kernel(around, *refs),
        [((peers, 2, 2, 8, 128), F32), ((8, 128), F32)], [pltpu.VMEM((2,) + rows, F32)], "last", scale, sums, early, late,
    )
    recv = lax.all_to_all(send, GROUP, 0, 0, tiled=True)
    inputs = (
        displacement, load_field, foundation, plastic_flags, point_slot, family_in, family_mid, family_out, family_tan
    )
    good, recv = lax.optimization_barrier((worst[0, 0] < MOST_LOST, recv))
    instead = lax.cond(good, lambda: (jnp.zeros_like(displacement),) * 2, lambda: plain_body(*inputs))
    shape = displacement.shape
    return call(
        lambda *refs: deliver_kernel(path, *refs), [(shape, F32), (shape, F32)], [pltpu.VMEM((2, 128, 128), F32)],
        "deliver", displacement, recv, worst, *instead, grid=(2,), outs=[halves] * 2,
        ins=[
            halves,
            pl.BlockSpec((peers, 1, 2, 8, 128), lambda i: (0, i, 0, 0, 0)),
            pl.BlockSpec((8, 128), lambda i: (0, 0)),
            halves,
            halves,
        ],
    )


def body(*inputs):
    size_x, size_y, size_z = inputs[0].shape
    along, across = lax.axis_size("blk"), lax.axis_size("micro")
    fits = (
        (size_x, size_y, size_z) == (8, 32, 128)
        and across == 4
        and size_z == 8 * along * across
        and lax.axis_size("slab") == 2
        and inputs[5].shape[0] == 4
    )
    if not fits:
        return plain_body(*inputs)
    return tuple(sliced_body(*inputs))


def solution(mesh):
    field = P("blk", "micro", "slab")
    return jax.shard_map(
        body,
        mesh=mesh,
        in_specs=(field,) * 5 + (P(),) * 4,
        out_specs=(field, field),
        check_vma=False,
    )
```
